512 devices in a mesh: slab: 32 (over y, z_lo), tile: 8 (over x, core), tilt: 2 (over z_hi).
Axes of the slice: x: 4, y: 4, z: 16 (z_hi: 2, z_lo: 8; z = z_hi * 8 + z_lo), core: 2. Of those that a mesh axis runs over, the one named last changes fastest.
Arguments:
- source: float32 [4, 512, 64, 256], P('tilt', 'slab', 'tile'), parts along dimension 0, may hold values from -1.2 to 1.2
- labels: int32 [512, 64, 512], P('slab', 'tile', 'tilt'), parts along dimension 2, may hold values from 0 to 7
- permittivity: float32 [16], P('tilt'), parts along dimension 0, may hold values from 1 to 2
Outputs:
- sweep_field: float32 [4, 512, 64, 256], P('tilt', 'slab', 'tile'), parts along dimension 0
The draws below stay inside these ranges and needn't reach their ends.
There are 2 independent parts, one for each index of `tilt`. The reference program is written for one: setup_inputs(seed, part) draws one part's arguments, and reference() takes and returns one part's arrays. A program takes and returns all parts, laid end to end along the dimension named above; each array names one. Nothing has to cross between parts.
All inputs are finite; a program needn't handle non-finite values.
Results may differ from the reference program's by a relative error of at most 0.0003.
Values sent between devices are 32-bit elements; how exact they have to be, the bound alone decides.
No kernel may reach another device: no remote copies, remote signals or barrier semaphores. Data moves between devices by JAX's collectives and lax.ppermute only.
A program may use at most 64 MiB of HBM per device.

```python
import math
import jax
import jax.numpy as jnp
from jax import lax

NY = 256
ITERS = 3
PML = 8
NMAT = 8
NZ = 512
NX = 64


def draw_source(key, part):
    return jnp.clip(0.2 * jax.random.normal(key, (2, NZ, NX, NY), jnp.float32), -1.2, 1.2)


def set_ends(drawn, stream_key, low, largest):
    place = [jax.random.randint(jax.random.fold_in(stream_key, axis), (), 0, length) for axis, length in enumerate(drawn.shape)]
    widest = drawn.shape.index(max(drawn.shape))
    next_to = place[:widest] + [(place[widest] + 1) % drawn.shape[widest]] + place[widest + 1:]
    return drawn.at[tuple(place)].set(low).at[tuple(next_to)].set(largest)


def setup_inputs(seed: int = 0, part: int = 0) -> dict:
    streams_of = jax.random.split(jax.random.key(seed), 4)
    own_keys = jax.random.split(jax.random.fold_in(streams_of[3], part), 4)
    source = draw_source(jax.random.fold_in(jax.random.fold_in(streams_of[3], part), 71), part)
    labels = set_ends(jax.random.randint(own_keys[1], (NZ, NX, NY), 0, NMAT), jax.random.fold_in(own_keys[1], 1), 0, NMAT - 1).astype(jnp.int32)
    permittivity = jnp.clip(jnp.exp(jax.random.uniform(own_keys[2], (NMAT,), jnp.float32, math.log(1.0), math.log(2.0))), 1.0, 2.0)
    return {"source": source, "labels": labels, "permittivity": permittivity}


COUPLE = 0.02
WAVE_SHIFT = 0.15
DAMPING = 0.15
ABSORB = 0.5


def complex_multiply(former, latter):
    former_re = former[..., 0, :, :]
    former_im = former[..., 1, :, :]
    latter_re = latter[..., 0, :, :]
    latter_im = latter[..., 1, :, :]
    return jnp.stack([former_re * latter_re - former_im * latter_im,
                      former_re * latter_im + former_im * latter_re], axis=-3)


def complex_recip(number):
    number_re = number[..., 0, :, :]
    number_im = number[..., 1, :, :]
    modulus = number_re * number_re + number_im * number_im
    return jnp.stack([number_re / modulus, -number_im / modulus], axis=-3)


def line_diagonal(labels, permittivity, layer_ids, layer_count):
    relative = permittivity[labels]
    inward = jnp.maximum(jnp.maximum(PML - layer_ids, layer_ids - (layer_count - 1 - PML)), 0)
    fraction = inward.astype(jnp.float32) / PML
    absorption_profile = ABSORB * fraction * fraction
    diag_re = (2.0 + 4.0 * COUPLE) - WAVE_SHIFT * relative
    diag_im = (DAMPING * WAVE_SHIFT) * relative + absorption_profile[:, None, None]
    return jnp.stack([diag_re, diag_im], axis=1)


def neighbour_sum(estimate):
    padded = jnp.pad(estimate, ((0, 0), (0, 0), (1, 1), (1, 1)))
    return padded[:, :, 2:, 1:-1] + padded[:, :, :-2, 1:-1] + padded[:, :, 1:-1, 2:] + padded[:, :, 1:-1, :-2]


def reference(source, labels, permittivity):
    layer_ids = jnp.arange(NZ, dtype=jnp.int32)
    diagonal = line_diagonal(labels, permittivity, layer_ids, NZ)
    zero_plane = jnp.zeros((2, NX, NY), jnp.float32)

    def pivot_turn(previous, diag_layer):
        current_layer_value = complex_recip(diag_layer - previous)
        return current_layer_value, (current_layer_value, previous)

    _, (pivots, below_pivots) = lax.scan(pivot_turn, zero_plane, diagonal)

    def line_solve(rhs_field):
        def forward_turn(carried_through, input_arrays):
            rhs_layer, below_pivot = input_arrays
            current_layer_value = rhs_layer + complex_multiply(below_pivot, carried_through)
            return current_layer_value, current_layer_value

        _, eliminated = lax.scan(forward_turn, zero_plane, (rhs_field, below_pivots))

        def backward_turn(carried_through, input_arrays):
            eliminate_layer, pivot_layer_entry = input_arrays
            current_layer_value = complex_multiply(pivot_layer_entry, eliminate_layer + carried_through)
            return current_layer_value, current_layer_value

        _, solved = lax.scan(backward_turn, zero_plane, (eliminated, pivots), reverse=True)
        return solved

    rhs_field = jnp.swapaxes(source, 0, 1)
    estimate = line_solve(rhs_field)
    for sweep_index in range(ITERS - 1):
        estimate = line_solve(rhs_field + COUPLE * neighbour_sum(estimate))
    return jnp.swapaxes(estimate, 0, 1)
```

```python
import jax
import jax.numpy as jnp
from jax import lax
from jax.experimental import pallas as pl
from jax.experimental.pallas import tpu as pltpu
from jax.sharding import PartitionSpec as P

PML = 8
COUPLE = 0.02
WAVE_SHIFT = 0.15
DAMPING = 0.15
ABSORB = 0.5
NZ = 512
SLABS = 32
TILES = 8
LANES = 128
DEPTH = 8
STEPS = 6
F32 = jnp.float32
VMEM = pl.BlockSpec(memory_space=pltpu.VMEM)
SMEM = pl.BlockSpec(memory_space=pltpu.SMEM)


def chunk_of(device):
    y, z = divmod(device, 8)
    return 8 * y + (z if y % 2 == 0 else 7 - z)


CHUNK = [chunk_of(d) for d in range(SLABS)]
OWNER = [CHUNK.index(c) for c in range(SLABS)]


def roll(x, shift, axis):
    shift %= x.shape[axis]
    return x if shift == 0 else pltpu.roll(x, shift, axis)


def cmul(a, b):
    return a[0] * b[0] - a[1] * b[1], a[0] * b[1] + a[1] * b[0]


def cadd(a, b):
    return a[0] + b[0], a[1] + b[1]


def csub(a, b):
    return a[0] - b[0], a[1] - b[1]


def crecip(a):
    scale = 1.0 / (a[0] * a[0] + a[1] * a[1])
    return a[0] * scale, -a[1] * scale


def block_transpose(parts):
    lane = lax.broadcasted_iota(jnp.int32, (8, LANES), 1)
    parts = list(parts)
    for bit in (1, 2, 4, 8):
        low = (lane & (8 * bit)) == 0
        for i in range(16):
            if i & bit == 0:
                a, b = parts[i], parts[i | bit]
                parts[i] = jnp.where(low, a, roll(b, 8 * bit, 1))
                parts[i | bit] = jnp.where(low, roll(a, -8 * bit, 1), b)
    return parts


def pack_kernel(table, source, labels, out, sides):
    for side in range(2):
        lanes = pl.ds(side * LANES, LANES)
        sides[side, pl.ds(0, 2 * LANES), :] = source[:, lanes]
        lab = labels[:, lanes]
        rel = jnp.full(lab.shape, table[0], F32)
        for m in range(1, 8):
            rel = jnp.where(lab == m, table[m], rel)
        sides[side, pl.ds(2 * LANES, LANES), :] = rel
    for side in range(2):
        for quantity in range(3):
            parts = []
            for half in range(2):
                for x in range(8):
                    first = quantity * LANES + half * 64 + x
                    parts.append(sides[side, pl.ds(first, 8, stride=8), :])
            for block, part in enumerate(block_transpose(parts)):
                dest = OWNER[16 * side + block]
                out[pl.ds(dest * 24 + quantity * 8, 8), :] = part


def unpack_kernel(arrived, out, sides):
    for side in range(2):
        for c in range(2):
            parts = [arrived[pl.ds(OWNER[16 * side + b] * 16 + c * 8, 8), :] for b in range(16)]
            for i, part in enumerate(block_transpose(parts)):
                half, x = divmod(i, 8)
                sides[side, pl.ds(c * LANES + half * 64 + x, 8, stride=8), :] = part
        out[:, pl.ds(side * LANES, LANES)] = sides[side]


def lane_ids():
    lane = lax.broadcasted_iota(jnp.int32, (SLABS, LANES), 1)
    return lane >= 64, (lane // 8) % 8, lane % 8


def up(a, h):
    if h >= 2:
        return roll(a, h // 2, 0)
    upper, _, _ = lane_ids()
    turned = roll(a, 64, 1)
    return jnp.where(upper, turned, roll(turned, 1, 0))


def down(a, h):
    if h >= 2:
        return roll(a, -(h // 2), 0)
    upper, _, _ = lane_ids()
    turned = roll(a, 64, 1)
    return jnp.where(upper, roll(turned, -1, 0), turned)


def both(f, a, h):
    return f(a[0], h), f(a[1], h)


def layer(ref, quantity, r):
    return ref[pl.ds(quantity * 8 + r, SLABS, stride=24), :]


def source_layer(ref, r):
    return layer(ref, 0, r), layer(ref, 1, r)


def put(ref, i, a):
    ref[pl.ds(2 * i * SLABS, SLABS), :] = a[0]
    ref[pl.ds((2 * i + 1) * SLABS, SLABS), :] = a[1]


def get(ref, i):
    return ref[pl.ds(2 * i * SLABS, SLABS), :], ref[pl.ds((2 * i + 1) * SLABS, SLABS), :]


N_FACTORS = 7 + 2 * STEPS + 1


def factorize(arrived, factors):
    upper, _, _ = lane_ids()
    row = lax.broadcasted_iota(jnp.int32, (SLABS, LANES), 0)
    first = row * 16 + jnp.where(upper, 8, 0)
    pivots = []
    diagonal = None
    for r in range(DEPTH):
        z = first + r
        relative = layer(arrived, 2, r)
        inward = jnp.maximum(jnp.maximum(PML - z, z - (NZ - 1 - PML)), 0)
        fraction = inward.astype(F32) / PML
        diagonal = (
            (2.0 + 4.0 * COUPLE) - WAVE_SHIFT * relative,
            (DAMPING * WAVE_SHIFT) * relative + ABSORB * fraction * fraction,
        )
        if r < DEPTH - 1:
            pivots.append(crecip(diagonal if r == 0 else csub(diagonal, pivots[-1])))
            put(factors, r, pivots[-1])
    to_first = pivots[0]
    first_first = pivots[0]
    for r in range(1, DEPTH - 1):
        reached = cmul(to_first, to_first)
        to_first = cmul(to_first, pivots[r])
        first_first = cadd(first_first, cmul(reached, pivots[r]))
    corner = to_first
    last_last = pivots[-1]
    low = (row == 0) & jnp.logical_not(upper)
    left = tuple(jnp.where(low, 0.0, v) for v in corner)
    high = (row == SLABS - 1) & upper
    next_first = tuple(jnp.where(high, 0.0, v) for v in both(down, first_first, 1))
    d = csub(csub(diagonal, last_last), next_first)
    for step in range(STEPS):
        h = 1 << step
        right = both(down, left, h)
        inverse = crecip(d)
        alpha = cmul(left, both(up, inverse, h))
        gamma = cmul(right, both(down, inverse, h))
        put(factors, 7 + 2 * step, alpha)
        put(factors, 8 + 2 * step, gamma)
        d = csub(csub(d, cmul(alpha, left)), cmul(gamma, right))
        left = cmul(alpha, both(up, left, h))
    put(factors, 7 + 2 * STEPS, crecip(d))


def line_solve(rhs, factors):
    pivots = [get(factors, r) for r in range(DEPTH - 1)]
    gone = [rhs[0]]
    for r in range(1, DEPTH - 1):
        gone.append(cadd(rhs[r], cmul(pivots[r - 1], gone[-1])))
    last = cmul(pivots[-1], gone[-1])
    reach = pivots[0]
    reaches = []
    first = cmul(pivots[0], gone[0])
    for r in range(1, DEPTH - 1):
        reaches.append(reach)
        reach = cmul(reach, pivots[r])
        first = cadd(first, cmul(reach, gone[r]))
    upper, _, _ = lane_ids()
    row = lax.broadcasted_iota(jnp.int32, (SLABS, LANES), 0)
    high = (row == SLABS - 1) & upper
    low = (row == 0) & jnp.logical_not(upper)
    after = tuple(jnp.where(high, 0.0, v) for v in both(down, first, 1))
    g = cadd(cadd(rhs[DEPTH - 1], last), after)
    for step in range(STEPS):
        h = 1 << step
        from_low = cmul(get(factors, 7 + 2 * step), both(up, g, h))
        from_high = cmul(get(factors, 8 + 2 * step), both(down, g, h))
        g = cadd(g, cadd(from_low, from_high))
    separator = cmul(get(factors, 7 + 2 * STEPS), g)
    before = tuple(jnp.where(low, 0.0, v) for v in both(up, separator, 1))
    field = [None] * DEPTH
    field[DEPTH - 1] = separator
    for r in range(DEPTH - 2, -1, -1):
        lit = cadd(gone[r], before if r == 0 else cmul(reaches[r - 1], before))
        field[r] = cmul(pivots[r], cadd(lit, field[r + 1]))
    return field


def put_edges(field, edges):
    _, x, y = lane_ids()
    x_low, x_high, y_low, y_high = edges
    for c in range(2):
        sums = [None] * 4
        for r in range(DEPTH):
            f = field[r][c]
            for i, (shift, here) in enumerate(((8 * r, x), (8 * (r - 7), x), (r, y), (r - 7, y))):
                moved = roll(f, shift, 1)
                sums[i] = moved if r == 0 else jnp.where(here == r, moved, sums[i])
        for edge, value in zip(edges, sums):
            edge[pl.ds(c * SLABS, SLABS), :] = value


def transverse(field, halos):
    _, x, y = lane_ids()
    result = []
    for r in range(DEPTH):
        parts = []
        for c in range(2):
            f = field[r][c]
            edge = [h[pl.ds(c * SLABS, SLABS), :] for h in halos]
            total = jnp.where(x == 0, roll(edge[0], -8 * r, 1), roll(f, 8, 1))
            total += jnp.where(x == 7, roll(edge[1], 8 * (7 - r), 1), roll(f, -8, 1))
            total += jnp.where(y == 0, roll(edge[2], -r, 1), roll(f, 1, 1))
            total += jnp.where(y == 7, roll(edge[3], 7 - r, 1), roll(f, -1, 1))
            parts.append(total)
        result.append(tuple(parts))
    return result


def first_kernel(arrived, factors, field_out, *edges):
    factorize(arrived, factors)
    field = line_solve([source_layer(arrived, r) for r in range(DEPTH)], factors)
    for r in range(DEPTH):
        put(field_out, r, field[r])
    put_edges(field, edges)


def relaxed(arrived, factors, field_in, halos):
    spread = transverse([get(field_in, r) for r in range(DEPTH)], halos)
    rhs = []
    for r in range(DEPTH):
        s = source_layer(arrived, r)
        rhs.append((s[0] + COUPLE * spread[r][0], s[1] + COUPLE * spread[r][1]))
    return line_solve(rhs, factors)


def middle_kernel(arrived, factors, field_in, h0, h1, h2, h3, field_out, *edges):
    field = relaxed(arrived, factors, field_in, (h0, h1, h2, h3))
    for r in range(DEPTH):
        put(field_out, r, field[r])
    put_edges(field, edges)


def last_kernel(arrived, factors, field_in, h0, h1, h2, h3, out):
    field = relaxed(arrived, factors, field_in, (h0, h1, h2, h3))
    for r in range(DEPTH):
        for c in range(2):
            out[pl.ds(c * 8 + r, SLABS, stride=16), :] = field[r][c]


def call(kernel, name, outs, *args, scratch=(), smem=False):
    shapes = [jax.ShapeDtypeStruct(s, F32) for s in outs]
    specs = [VMEM] * len(args)
    if smem:
        specs[0] = SMEM
    result = pl.pallas_call(
        kernel,
        out_shape=shapes,
        in_specs=specs,
        out_specs=[VMEM] * len(outs),
        scratch_shapes=list(scratch),
        compiler_params=pltpu.CompilerParams(vmem_limit_bytes=32 << 20),
        name=name,
    )(*args)
    return result


FIELD = (DEPTH * 2 * SLABS, LANES)
FACTORS = (N_FACTORS * 2 * SLABS, LANES)
EDGE = (2 * SLABS, LANES)

TILE_UP = [(i, i + 1) for i in range(TILES - 1)]
TILE_DOWN = [(i + 1, i) for i in range(TILES - 1)]
SLAB_UP = [(OWNER[c], OWNER[c + 1]) for c in range(SLABS - 1)]
SLAB_DOWN = [(OWNER[c + 1], OWNER[c]) for c in range(SLABS - 1)]


def exchange(x_low, x_high, y_low, y_high):
    return (
        lax.ppermute(x_high, "tile", TILE_UP),
        lax.ppermute(x_low, "tile", TILE_DOWN),
        lax.ppermute(y_high, "slab", SLAB_UP),
        lax.ppermute(y_low, "slab", SLAB_DOWN),
    )


def local(source, labels, permittivity):
    rows = source.reshape(2 * 16 * 8, 256)
    marks = labels.reshape(16 * 8, 256)
    (packed,) = call(
        pack_kernel, "pack", [(SLABS * 24, LANES)], permittivity, rows, marks,
        scratch=[pltpu.VMEM((2, 3 * LANES, LANES), F32)], smem=True,
    )
    arrived = lax.all_to_all(packed.reshape(SLABS, 24, LANES), "slab", 0, 0).reshape(SLABS * 24, LANES)
    factors, field, *edges = call(first_kernel, "first", [FACTORS, FIELD] + [EDGE] * 4, arrived)
    halos = exchange(*edges)
    field, *edges = call(middle_kernel, "middle", [FIELD] + [EDGE] * 4, arrived, factors, field, *halos)
    halos = exchange(*edges)
    (packed,) = call(last_kernel, "last", [(SLABS * 16, LANES)], arrived, factors, field, *halos)
    arrived = lax.all_to_all(packed.reshape(SLABS, 16, LANES), "slab", 0, 0).reshape(SLABS * 16, LANES)
    (out,) = call(unpack_kernel, "unpack", [(2 * 16 * 8, 256)], arrived,
                  scratch=[pltpu.VMEM((2, 2 * LANES, LANES), F32)])
    return out.reshape(2, 16, 8, 256)


def solution(mesh):
    placed = (P("tilt", "slab", "tile", None), P("slab", "tile", "tilt"), P("tilt"))
    return jax.shard_map(
        local,
        mesh=mesh,
        in_specs=placed,
        out_specs=P("tilt", "slab", "tile", None),
        check_vma=False,
    )
```

```python
import jax
import jax.numpy as jnp
from jax import lax
from jax.experimental import pallas as pl
from jax.experimental.pallas import tpu as pltpu
from jax.sharding import PartitionSpec as P

PML = 8
COUPLE = 0.02
WAVE_SHIFT = 0.15
DAMPING = 0.15
ABSORB = 0.5
NZ = 512
SLABS = 32
TILES = 8
LANES = 128
DEPTH = 8
STEPS = 6
F32 = jnp.float32
VMEM = pl.BlockSpec(memory_space=pltpu.VMEM)
SMEM = pl.BlockSpec(memory_space=pltpu.SMEM)


ROWS = 32


def owner(x_half, y_chunk):
    y, z = divmod(y_chunk, 4)
    return 8 * y + 2 * z + x_half


def roll(x, shift, axis):
    shift %= x.shape[axis]
    return x if shift == 0 else pltpu.roll(x, shift, axis)


def cmul(a, b):
    return a[0] * b[0] - a[1] * b[1], a[0] * b[1] + a[1] * b[0]


def cadd(a, b):
    return a[0] + b[0], a[1] + b[1]


def csub(a, b):
    return a[0] - b[0], a[1] - b[1]


def crecip(a):
    scale = 1.0 / (a[0] * a[0] + a[1] * a[1])
    return a[0] * scale, -a[1] * scale


def lanes8():
    return lax.broadcasted_iota(jnp.int32, (8, LANES), 1)


def block_transpose(parts):
    lane = lanes8()
    parts = list(parts)
    for bit in (1, 2, 4):
        low = (lane & (16 * bit)) == 0
        for i in range(8):
            if i & bit == 0:
                a, b = parts[i], parts[i | bit]
                parts[i] = jnp.where(low, a, roll(b, 16 * bit, 1))
                parts[i | bit] = jnp.where(low, roll(a, -16 * bit, 1), b)
    return parts


def overlap_parts(arrays):
    lane = lanes8()
    slot = lane % 16
    parts = [None, None]
    for q in range(3):
        below = [roll(arrays[side][q], 4 * q + 2, 1) for side in range(2)]
        above = [roll(arrays[side][q], 4 * q - 14, 1) for side in range(2)]
        for side in range(2):
            lower = jnp.where(lane < 16, below[1 - side], below[side])
            upper = jnp.where(lane >= 112, above[1 - side], above[side])
            merged = jnp.where(slot < 4 * q + 2, lower, upper)
            parts[side] = merged if q == 0 else jnp.where(slot < 4 * q, parts[side], merged)
    return parts


def pack_kernel(table, source, labels, out, sides):
    for side in range(2):
        lanes = pl.ds(side * LANES, LANES)
        sides[side, pl.ds(0, 2 * LANES), :] = source[:, lanes]
        lab = labels[:, lanes]
        rel = jnp.full(lab.shape, table[0], F32)
        for m in range(1, 8):
            rel = jnp.where(lab == m, table[m], rel)
        sides[side, pl.ds(2 * LANES, LANES), :] = rel

    def load(side, quantity, half, x):
        return sides[side, pl.ds(quantity * LANES + half * 64 + x, 8, stride=8), :]

    for x_half in range(2):
        overlaps = [[], []]
        for half in range(2):
            for x in range(4 * x_half, 4 * x_half + 4):
                arrays = [[load(side, q, half, x) for q in range(3)] for side in range(2)]
                for side, part in enumerate(overlap_parts(arrays)):
                    overlaps[side].append(part)
        for side in range(2):
            for quantity in range(4):
                if quantity == 3:
                    parts = overlaps[side]
                else:
                    parts = [load(side, quantity, i // 4, 4 * x_half + i % 4) for i in range(8)]
                for block, part in enumerate(block_transpose(parts)):
                    dest = owner(x_half, 8 * side + block)
                    out[pl.ds(dest * ROWS + quantity * 8, 8), :] = part


def unpack_kernel(arrived, out, sides):
    for side in range(2):
        for c in range(2):
            for x_half in range(2):
                parts = [arrived[pl.ds(owner(x_half, 8 * side + b) * 16 + c * 8, 8), :] for b in range(8)]
                for i, part in enumerate(block_transpose(parts)):
                    half, x = divmod(i, 4)
                    sides[side, pl.ds(c * LANES + half * 64 + 4 * x_half + x, 8, stride=8), :] = part
        out[:, pl.ds(side * LANES, LANES)] = sides[side]


def lane_ids():
    lane = lax.broadcasted_iota(jnp.int32, (SLABS, LANES), 1)
    return lane >= 64, (lane // 16) % 4, lane % 16


def upper_half(overlap):
    lane = lax.broadcasted_iota(jnp.int32, (SLABS, LANES), 1)
    if overlap:
        lane = (lane + jnp.where(lane % 16 >= 8, 16, LANES - 16)) % LANES
    return lane >= 64


def up(a, h, upper):
    if h >= 2:
        return roll(a, h // 2, 0)
    turned = roll(a, 64, 1)
    return jnp.where(upper, turned, roll(turned, 1, 0))


def down(a, h, upper):
    if h >= 2:
        return roll(a, -(h // 2), 0)
    turned = roll(a, 64, 1)
    return jnp.where(upper, roll(turned, -1, 0), turned)


def both(f, a, h, upper):
    return f(a[0], h, upper), f(a[1], h, upper)


def layer(ref, quantity, r):
    return ref[pl.ds(quantity * 8 + r, SLABS, stride=ROWS), :]


def source_layer(ref, r):
    return layer(ref, 0, r), layer(ref, 1, r)


def overlap_layer(ref, r):
    _, _, y = lane_ids()
    packed = layer(ref, 3, r)
    quantities = []
    for q in range(3):
        quantities.append(jnp.where(y >= 8, roll(packed, -2 - 4 * q, 1), roll(packed, 14 - 4 * q, 1)))
    used = (y <= 1) | (y >= 14)
    return quantities[0], quantities[1], jnp.where(used, quantities[2], 1.0)


def inside():
    chunk = lax.axis_index("slab") // 2
    _, _, y = lane_ids()
    below = (y >= 14) & jnp.broadcast_to(chunk > 0, y.shape)
    above = (y <= 1) & jnp.broadcast_to(chunk < 15, y.shape)
    return below | above


def put(ref, i, a):
    ref[pl.ds(2 * i * SLABS, SLABS), :] = a[0]
    ref[pl.ds((2 * i + 1) * SLABS, SLABS), :] = a[1]


def get(ref, i):
    return ref[pl.ds(2 * i * SLABS, SLABS), :], ref[pl.ds((2 * i + 1) * SLABS, SLABS), :]


N_FACTORS = 7 + 2 * STEPS + 1


def factorize(relatives, factors, overlap=False):
    upper = upper_half(overlap)
    row = lax.broadcasted_iota(jnp.int32, (SLABS, LANES), 0)
    first = row * 16 + jnp.where(upper, 8, 0)
    pivots = []
    diagonal = None
    for r in range(DEPTH):
        z = first + r
        relative = relatives[r]
        inward = jnp.maximum(jnp.maximum(PML - z, z - (NZ - 1 - PML)), 0)
        fraction = inward.astype(F32) / PML
        diagonal = (
            (2.0 + 4.0 * COUPLE) - WAVE_SHIFT * relative,
            (DAMPING * WAVE_SHIFT) * relative + ABSORB * fraction * fraction,
        )
        if r < DEPTH - 1:
            pivots.append(crecip(diagonal if r == 0 else csub(diagonal, pivots[-1])))
            put(factors, r, pivots[-1])
    to_first = pivots[0]
    first_first = pivots[0]
    for r in range(1, DEPTH - 1):
        reached = cmul(to_first, to_first)
        to_first = cmul(to_first, pivots[r])
        first_first = cadd(first_first, cmul(reached, pivots[r]))
    corner = to_first
    last_last = pivots[-1]
    low = (row == 0) & jnp.logical_not(upper)
    left = tuple(jnp.where(low, 0.0, v) for v in corner)
    high = (row == SLABS - 1) & upper
    next_first = tuple(jnp.where(high, 0.0, v) for v in both(down, first_first, 1, upper))
    d = csub(csub(diagonal, last_last), next_first)
    for step in range(STEPS):
        h = 1 << step
        right = both(down, left, h, upper)
        inverse = crecip(d)
        alpha = cmul(left, both(up, inverse, h, upper))
        gamma = cmul(right, both(down, inverse, h, upper))
        put(factors, 7 + 2 * step, alpha)
        put(factors, 8 + 2 * step, gamma)
        d = csub(csub(d, cmul(alpha, left)), cmul(gamma, right))
        left = cmul(alpha, both(up, left, h, upper))
    put(factors, 7 + 2 * STEPS, crecip(d))


def line_solve(rhs, factors, overlap=False):
    pivots = [get(factors, r) for r in range(DEPTH - 1)]
    gone = [rhs[0]]
    for r in range(1, DEPTH - 1):
        gone.append(cadd(rhs[r], cmul(pivots[r - 1], gone[-1])))
    last = cmul(pivots[-1], gone[-1])
    reach = pivots[0]
    reaches = []
    first = cmul(pivots[0], gone[0])
    for r in range(1, DEPTH - 1):
        reaches.append(reach)
        reach = cmul(reach, pivots[r])
        first = cadd(first, cmul(reach, gone[r]))
    upper = upper_half(overlap)
    row = lax.broadcasted_iota(jnp.int32, (SLABS, LANES), 0)
    high = (row == SLABS - 1) & upper
    low = (row == 0) & jnp.logical_not(upper)
    after = tuple(jnp.where(high, 0.0, v) for v in both(down, first, 1, upper))
    g = cadd(cadd(rhs[DEPTH - 1], last), after)
    for step in range(STEPS):
        h = 1 << step
        from_low = cmul(get(factors, 7 + 2 * step), both(up, g, h, upper))
        from_high = cmul(get(factors, 8 + 2 * step), both(down, g, h, upper))
        g = cadd(g, cadd(from_low, from_high))
    separator = cmul(get(factors, 7 + 2 * STEPS), g)
    before = tuple(jnp.where(low, 0.0, v) for v in both(up, separator, 1, upper))
    field = [None] * DEPTH
    field[DEPTH - 1] = separator
    for r in range(DEPTH - 2, -1, -1):
        lit = cadd(gone[r], before if r == 0 else cmul(reaches[r - 1], before))
        field[r] = cmul(pivots[r], cadd(lit, field[r + 1]))
    return field


def put_edges(main, over, edges):
    _, x, y = lane_ids()
    for edge, is_high in zip(edges, (False, True)):
        for c in range(2):
            for group in range(2):
                total = None
                for i in range(4):
                    moved = roll(main[4 * group + i][c], 16 * (i - 3) if is_high else 16 * i, 1)
                    total = moved if i == 0 else jnp.where(x == i, moved, total)
                edge[pl.ds((2 * c + group) * SLABS, SLABS), :] = total
        if over is None:
            continue
        below_at, above_at = (2, 0) if is_high else (3, 1)
        total = jnp.zeros((SLABS, LANES), F32)
        for c in range(2):
            for r in range(DEPTH):
                f = over[r][c]
                below = (x == (below_at + c) % 4) & (y == 15 - r)
                above = (x == (above_at + c) % 4) & (y == r)
                total = jnp.where(below, roll(f, 16 * c - r, 1), total)
                total = jnp.where(above, roll(f, 16 * c + r, 1), total)
        edge[pl.ds(4 * SLABS, SLABS), :] = total


def transverse(main, over, halos, with_overlap):
    _, x, y = lane_ids()
    results, over_results = [], []
    for r in range(DEPTH):
        parts, over_parts = [], []
        for c in range(2):
            m, e = main[r][c], over[r][c]
            low, high = (h[pl.ds((2 * c + r // 4) * SLABS, SLABS), :] for h in halos)
            m_up, m_down = roll(m, 1, 1), roll(m, -1, 1)
            e_up, e_down = roll(e, 1, 1), roll(e, -1, 1)
            along_x = jnp.where(x == 0, roll(low, -16 * (r % 4), 1), roll(m, 16, 1)) + jnp.where(
                x == 3, roll(high, 16 * (3 - r % 4), 1), roll(m, -16, 1)
            )
            along_y = jnp.where(y == 0, e_up, m_up) + jnp.where(y == 15, e_down, m_down)
            parts.append(along_x + along_y)
            if with_overlap:
                low, high = (h[pl.ds(4 * SLABS, SLABS), :] for h in halos)
                below = y >= 8
                from_low = jnp.where(below, roll(low, -48 - 16 * c + r, 1), roll(low, -48 - 16 * c - r, 1))
                from_high = jnp.where(below, roll(high, 48 - 16 * c + r, 1), roll(high, 48 - 16 * c - r, 1))
                at_low = x == jnp.where(below, 3, 1)
                at_high = x == jnp.where(below, 2, 0)
                along_x = jnp.where(at_low, from_low, roll(e, 16, 1)) + jnp.where(at_high, from_high, roll(e, -16, 1))
                along_y = jnp.where(below, e_up + m_down, m_up + e_down)
                over_parts.append(along_x + along_y)
        results.append(parts)
        over_results.append(over_parts)
    return results, over_results


def relax(source, spread):
    return tuple(s + COUPLE * t for s, t in zip(source, spread))


def masked(field):
    keep = inside()
    return [tuple(jnp.where(keep, v, 0.0) for v in f) for f in field]


def put_all(ref, field):
    for r in range(DEPTH):
        put(ref, r, field[r])


def get_all(ref):
    return [get(ref, r) for r in range(DEPTH)]


def first_kernel(arrived, factors, over_factors, over_source, main_out, over_out, *edges):
    factorize([layer(arrived, 2, r) for r in range(DEPTH)], factors)
    main = line_solve([source_layer(arrived, r) for r in range(DEPTH)], factors)
    put_all(main_out, main)
    overlap = [overlap_layer(arrived, r) for r in range(DEPTH)]
    factorize([o[2] for o in overlap], over_factors, True)
    put_all(over_source, [o[:2] for o in overlap])
    over = masked(line_solve([o[:2] for o in overlap], over_factors, True))
    put_all(over_out, over)
    put_edges(main, over, edges)


def middle_kernel(arrived, factors, over_factors, over_source, main_in, over_in, low, high, main_out, over_out, *edges):
    spread, over_spread = transverse(get_all(main_in), get_all(over_in), (low, high), True)
    main = line_solve([relax(source_layer(arrived, r), spread[r]) for r in range(DEPTH)], factors)
    put_all(main_out, main)
    put_edges(main, None, edges)
    over = line_solve([relax(get(over_source, r), over_spread[r]) for r in range(DEPTH)], over_factors, True)
    put_all(over_out, masked(over))


def last_kernel(arrived, factors, main_in, over_in, low, high, out):
    spread, _ = transverse(get_all(main_in), get_all(over_in), (low, high), False)
    field = line_solve([relax(source_layer(arrived, r), spread[r]) for r in range(DEPTH)], factors)
    for r in range(DEPTH):
        for c in range(2):
            out[pl.ds(c * 8 + r, SLABS, stride=16), :] = field[r][c]


def call(kernel, name, outs, *args, scratch=(), smem=False):
    shapes = [jax.ShapeDtypeStruct(s, F32) for s in outs]
    specs = [VMEM] * len(args)
    if smem:
        specs[0] = SMEM
    result = pl.pallas_call(
        kernel,
        out_shape=shapes,
        in_specs=specs,
        out_specs=[VMEM] * len(outs),
        scratch_shapes=list(scratch),
        compiler_params=pltpu.CompilerParams(vmem_limit_bytes=32 << 20),
        name=name,
    )(*args)
    return result


FIELD = (DEPTH * 2 * SLABS, LANES)
FACTORS = (N_FACTORS * 2 * SLABS, LANES)
EDGE = (5 * SLABS, LANES)
SHORT_EDGE = (4 * SLABS, LANES)


def x_neighbours():
    pairs = []
    for y_chunk in range(16):
        for tile in range(TILES):
            pairs.append((owner(0, y_chunk) * TILES + tile, owner(1, y_chunk) * TILES + tile))
            if tile + 1 < TILES:
                pairs.append((owner(1, y_chunk) * TILES + tile, owner(0, y_chunk) * TILES + tile + 1))
    return pairs


X_UP = x_neighbours()
X_DOWN = [(b, a) for a, b in X_UP]


def exchange(low, high):
    axes = ("slab", "tile")
    return lax.ppermute(high, axes, X_UP), lax.ppermute(low, axes, X_DOWN)


def local(source, labels, permittivity):
    rows = source.reshape(2 * 16 * 8, 256)
    marks = labels.reshape(16 * 8, 256)
    (packed,) = call(
        pack_kernel, "pack", [(SLABS * ROWS, LANES)], permittivity, rows, marks,
        scratch=[pltpu.VMEM((2, 3 * LANES, LANES), F32)], smem=True,
    )
    arrived = lax.all_to_all(packed.reshape(SLABS, ROWS, LANES), "slab", 0, 0).reshape(SLABS * ROWS, LANES)
    factors, over_factors, over_source, main, over, *edges = call(
        first_kernel, "first", [FACTORS, FACTORS, FIELD, FIELD, FIELD, EDGE, EDGE], arrived
    )
    halos = exchange(*edges)
    main, over, *edges = call(
        middle_kernel, "middle", [FIELD, FIELD, SHORT_EDGE, SHORT_EDGE],
        arrived, factors, over_factors, over_source, main, over, *halos,
    )
    halos = exchange(*edges)
    (packed,) = call(last_kernel, "last", [(SLABS * 16, LANES)], arrived, factors, main, over, *halos)
    arrived = lax.all_to_all(packed.reshape(SLABS, 16, LANES), "slab", 0, 0).reshape(SLABS * 16, LANES)
    (out,) = call(
        unpack_kernel, "unpack", [(2 * 16 * 8, 256)], arrived, scratch=[pltpu.VMEM((2, 2 * LANES, LANES), F32)]
    )
    return out.reshape(2, 16, 8, 256)


def solution(mesh):
    placed = (P("tilt", "slab", "tile", None), P("slab", "tile", "tilt"), P("tilt"))
    return jax.shard_map(
        local,
        mesh=mesh,
        in_specs=placed,
        out_specs=P("tilt", "slab", "tile", None),
        check_vma=False,
    )
```

```python
import jax
import jax.numpy as jnp
from jax import lax
from jax.experimental import pallas as pl
from jax.experimental.pallas import tpu as pltpu
from jax.sharding import PartitionSpec as P

PML = 8
COUPLE = 0.02
WAVE_SHIFT = 0.15
DAMPING = 0.15
ABSORB = 0.5
NZ = 512
SLABS = 32
TILES = 8
LANES = 128
DEPTH = 8
STEPS = 6
F32 = jnp.float32
VMEM = pl.BlockSpec(memory_space=pltpu.VMEM)
HBM = pl.BlockSpec(memory_space=pltpu.HBM)


ROWS = 36


def roll(x, shift, axis):
    shift %= x.shape[axis]
    return x if shift == 0 else pltpu.roll(x, shift, axis)


def cmul(a, b):
    return a[0] * b[0] - a[1] * b[1], a[0] * b[1] + a[1] * b[0]


def cadd(a, b):
    return a[0] + b[0], a[1] + b[1]


def csub(a, b):
    return a[0] - b[0], a[1] - b[1]


def crecip(a):
    scale = 1.0 / (a[0] * a[0] + a[1] * a[1])
    return a[0] * scale, -a[1] * scale


def lanes8():
    return lax.broadcasted_iota(jnp.int32, (8, LANES), 1)


def lanes8():
    return lax.broadcasted_iota(jnp.int32, (8, LANES), 1)


def block_transpose(parts):
    lane = lanes8()
    parts = list(parts)
    for bit in (1, 2, 4, 8):
        low = (lane & (8 * bit)) == 0
        for i in range(16):
            if i & bit == 0:
                a, b = parts[i], parts[i | bit]
                parts[i] = jnp.where(low, a, roll(b, 8 * bit, 1))
                parts[i | bit] = jnp.where(low, roll(a, -8 * bit, 1), b)
    return parts


def overlap_parts(arrays, base):
    lane = lanes8()
    below = [roll(array, base + 2, 1) for array in arrays]
    above = [roll(array, base - 6, 1) for array in arrays]
    parts = []
    for side in range(2):
        lower = jnp.where(lane < 8, below[1 - side], below[side])
        upper = jnp.where(lane >= 120, above[1 - side], above[side])
        parts.append(jnp.where(lane % 8 < base + 2, lower, upper))
    return parts


def pack_kernel(table_hbm, source, labels, out, sides, marks, table, sems):
    copies = [pltpu.make_async_copy(table_hbm, table, sems.at[0])]
    for side in range(2):
        lanes = pl.ds(side * LANES, LANES)
        copies.append(pltpu.make_async_copy(labels.at[:, lanes], marks.at[side], sems.at[1 + side]))
        into = sides.at[side, pl.ds(0, 2 * LANES)]
        copies.append(pltpu.make_async_copy(source.at[:, lanes], into, sems.at[3 + side]))
    for copy in copies:
        copy.start()
    for copy in copies:
        copy.wait()
    for side in range(2):
        lab = marks[side]
        rel = jnp.full(lab.shape, table[0], F32)
        for m in range(1, 8):
            rel = jnp.where(lab == m, table[m], rel)
        sides[side, pl.ds(2 * LANES, LANES), :] = rel

    def load(side, quantity, half, x):
        return sides[side, pl.ds(quantity * LANES + half * 64 + x, 8, stride=8), :]

    slot = lanes8() % 8
    places = [(half, x) for half in range(2) for x in range(8)]
    pairs, singles = [[], []], [[], []]
    for quantity in range(3):
        arrays = [[load(side, quantity, half, x) for half, x in places] for side in range(2)]
        for side in range(2):
            for block, part in enumerate(block_transpose(arrays[side])):
                out[pl.ds((16 * side + block) * ROWS + quantity * 8, 8), :] = part
        for i in range(16):
            parts = overlap_parts([arrays[0][i], arrays[1][i]], 4 if quantity == 1 else 0)
            for side in range(2):
                if quantity == 0:
                    pairs[side].append(parts[side])
                elif quantity == 1:
                    pairs[side][i] = jnp.where(slot < 4, pairs[side][i], parts[side])
                else:
                    upper = roll(roll(parts[side], 4, 0), 4, 1)
                    singles[side].append(jnp.where(slot < 4, parts[side], upper))
    for side in range(2):
        for block, part in enumerate(block_transpose(pairs[side])):
            out[pl.ds((16 * side + block) * ROWS + 24, 8), :] = part
        for block, part in enumerate(block_transpose(singles[side])):
            out[pl.ds((16 * side + block) * ROWS + 32, 4), :] = part[:4]


def unpack_kernel(arrived, out, sides):
    for side in range(2):
        for c in range(2):
            parts = [arrived[pl.ds((16 * side + b) * 16 + c * 8, 8), :] for b in range(16)]
            for i, part in enumerate(block_transpose(parts)):
                half, x = divmod(i, 8)
                sides[side, pl.ds(c * LANES + half * 64 + x, 8, stride=8), :] = part
        out[:, pl.ds(side * LANES, LANES)] = sides[side]


def lane_ids():
    lane = lax.broadcasted_iota(jnp.int32, (SLABS, LANES), 1)
    return lane >= 64, (lane // 8) % 8, lane % 8


def upper_half(overlap):
    lane = lax.broadcasted_iota(jnp.int32, (SLABS, LANES), 1)
    if overlap:
        lane = (lane + jnp.where(lane % 8 >= 4, 8, LANES - 8)) % LANES
    return lane >= 64


def up(a, h, upper):
    if h >= 2:
        return roll(a, h // 2, 0)
    turned = roll(a, 64, 1)
    return jnp.where(upper, turned, roll(turned, 1, 0))


def down(a, h, upper):
    if h >= 2:
        return roll(a, -(h // 2), 0)
    turned = roll(a, 64, 1)
    return jnp.where(upper, roll(turned, -1, 0), turned)


def both(f, a, h, upper):
    return f(a[0], h, upper), f(a[1], h, upper)


def layer(ref, quantity, r):
    return ref[pl.ds(quantity * 8 + r, SLABS, stride=ROWS), :]


def source_layer(ref, r):
    return layer(ref, 0, r), layer(ref, 1, r)


def overlap_layer(ref, r):
    _, _, y = lane_ids()
    pair = ref[pl.ds(24 + r, SLABS, stride=ROWS), :]
    single = ref[pl.ds(32 + r % 4, SLABS, stride=ROWS), :]
    quantities = []
    for packed, base in ((pair, 0), (pair, 4), (single, 4 * (r // 4))):
        quantities.append(jnp.where(y >= 4, roll(packed, -2 - base, 1), roll(packed, 6 - base, 1)))
    used = (y <= 1) | (y >= 6)
    return quantities[0], quantities[1], jnp.where(used, quantities[2], 1.0)


def inside():
    chunk = lax.axis_index("slab")
    _, _, y = lane_ids()
    below = (y >= 6) & jnp.broadcast_to(chunk > 0, y.shape)
    above = (y <= 1) & jnp.broadcast_to(chunk < SLABS - 1, y.shape)
    return below | above


def put(ref, i, a):
    ref[pl.ds(2 * i * SLABS, SLABS), :] = a[0]
    ref[pl.ds((2 * i + 1) * SLABS, SLABS), :] = a[1]


def get(ref, i):
    return ref[pl.ds(2 * i * SLABS, SLABS), :], ref[pl.ds((2 * i + 1) * SLABS, SLABS), :]


N_FACTORS = 7 + 2 * STEPS + 1


def factorize(relatives, factors, overlap=False):
    upper = upper_half(overlap)
    row = lax.broadcasted_iota(jnp.int32, (SLABS, LANES), 0)
    first = row * 16 + jnp.where(upper, 8, 0)
    pivots = []
    diagonal = None
    for r in range(DEPTH):
        z = first + r
        relative = relatives[r]
        inward = jnp.maximum(jnp.maximum(PML - z, z - (NZ - 1 - PML)), 0)
        fraction = inward.astype(F32) / PML
        diagonal = (
            (2.0 + 4.0 * COUPLE) - WAVE_SHIFT * relative,
            (DAMPING * WAVE_SHIFT) * relative + ABSORB * fraction * fraction,
        )
        if r < DEPTH - 1:
            pivots.append(crecip(diagonal if r == 0 else csub(diagonal, pivots[-1])))
            put(factors, r, pivots[-1])
    to_first = pivots[0]
    first_first = pivots[0]
    for r in range(1, DEPTH - 1):
        reached = cmul(to_first, to_first)
        to_first = cmul(to_first, pivots[r])
        first_first = cadd(first_first, cmul(reached, pivots[r]))
    corner = to_first
    last_last = pivots[-1]
    low = (row == 0) & jnp.logical_not(upper)
    left = tuple(jnp.where(low, 0.0, v) for v in corner)
    high = (row == SLABS - 1) & upper
    next_first = tuple(jnp.where(high, 0.0, v) for v in both(down, first_first, 1, upper))
    d = csub(csub(diagonal, last_last), next_first)
    for step in range(STEPS):
        h = 1 << step
        right = both(down, left, h, upper)
        inverse = crecip(d)
        alpha = cmul(left, both(up, inverse, h, upper))
        gamma = cmul(right, both(down, inverse, h, upper))
        put(factors, 7 + 2 * step, alpha)
        put(factors, 8 + 2 * step, gamma)
        d = csub(csub(d, cmul(alpha, left)), cmul(gamma, right))
        left = cmul(alpha, both(up, left, h, upper))
    put(factors, 7 + 2 * STEPS, crecip(d))


def line_solve(rhs, factors, overlap=False):
    pivots = [get(factors, r) for r in range(DEPTH - 1)]
    gone = [rhs[0]]
    for r in range(1, DEPTH - 1):
        gone.append(cadd(rhs[r], cmul(pivots[r - 1], gone[-1])))
    last = cmul(pivots[-1], gone[-1])
    reach = pivots[0]
    reaches = []
    first = cmul(pivots[0], gone[0])
    for r in range(1, DEPTH - 1):
        reaches.append(reach)
        reach = cmul(reach, pivots[r])
        first = cadd(first, cmul(reach, gone[r]))
    upper = upper_half(overlap)
    row = lax.broadcasted_iota(jnp.int32, (SLABS, LANES), 0)
    high = (row == SLABS - 1) & upper
    low = (row == 0) & jnp.logical_not(upper)
    after = tuple(jnp.where(high, 0.0, v) for v in both(down, first, 1, upper))
    g = cadd(cadd(rhs[DEPTH - 1], last), after)
    for step in range(STEPS):
        h = 1 << step
        from_low = cmul(get(factors, 7 + 2 * step), both(up, g, h, upper))
        from_high = cmul(get(factors, 8 + 2 * step), both(down, g, h, upper))
        g = cadd(g, cadd(from_low, from_high))
    separator = cmul(get(factors, 7 + 2 * STEPS), g)
    before = tuple(jnp.where(low, 0.0, v) for v in both(up, separator, 1, upper))
    field = [None] * DEPTH
    field[DEPTH - 1] = separator
    for r in range(DEPTH - 2, -1, -1):
        lit = cadd(gone[r], before if r == 0 else cmul(reaches[r - 1], before))
        field[r] = cmul(pivots[r], cadd(lit, field[r + 1]))
    return field


def put_edges(main, over, edges):
    _, x, y = lane_ids()
    for edge, is_high in zip(edges, (False, True)):
        for c in range(2):
            total = None
            for r in range(DEPTH):
                moved = roll(main[r][c], 8 * (r - 7) if is_high else 8 * r, 1)
                total = moved if r == 0 else jnp.where(x == r, moved, total)
            edge[pl.ds(c * SLABS, SLABS), :] = total
        if over is None:
            continue
        below_at, above_at = (6, 0) if is_high else (7, 1)
        total = jnp.zeros((SLABS, LANES), F32)
        for c in range(2):
            for r in range(DEPTH):
                i, k = 2 * c + r // 4, r % 4
                below = (x == (below_at + i) % 8) & (y == 7 - k)
                above = (x == (above_at + i) % 8) & (y == k)
                total = jnp.where(below, roll(over[r][c], 8 * i - k, 1), total)
                total = jnp.where(above, roll(over[r][c], 8 * i + k, 1), total)
        edge[pl.ds(2 * SLABS, SLABS), :] = total


def halo(refs, place):
    tile = lax.axis_index("tile")
    rows = pl.ds(place * SLABS, SLABS)
    keep = (tile > 0, tile < TILES - 1)
    return [jnp.where(jnp.broadcast_to(k, (SLABS, LANES)), ref[rows, :], 0.0) for ref, k in zip(refs, keep)]


def transverse(main, over, halos):
    _, x, y = lane_ids()
    packed = [halo(halos, c) for c in range(2)]
    results = []
    for r in range(DEPTH):
        parts = []
        for c in range(2):
            m, e = main[r][c], over[r][c]
            low, high = packed[c]
            along_x = jnp.where(x == 0, roll(low, -8 * r, 1), roll(m, 8, 1))
            along_x += jnp.where(x == 7, roll(high, 8 * (7 - r), 1), roll(m, -8, 1))
            along_y = jnp.where(y == 0, roll(e, 1, 1), roll(m, 1, 1))
            along_y += jnp.where(y == 7, roll(e, -1, 1), roll(m, -1, 1))
            parts.append(along_x + along_y)
        results.append(parts)
    return results


def over_transverse(main, over, halos):
    _, x, y = lane_ids()
    low, high = halo(halos, 2)
    below = y >= 4
    at_low = x == jnp.where(below, 7, 1)
    at_high = x == jnp.where(below, 6, 0)
    results = []
    for r in range(DEPTH):
        parts = []
        for c in range(2):
            m, e = main[r][c], over[r][c]
            i, k = 2 * c + r // 4, r % 4
            from_low = jnp.where(below, roll(low, -56 - 8 * i + k, 1), roll(low, -56 - 8 * i - k, 1))
            from_high = jnp.where(below, roll(high, 56 - 8 * i + k, 1), roll(high, 56 - 8 * i - k, 1))
            along_x = jnp.where(at_low, from_low, roll(e, 8, 1)) + jnp.where(at_high, from_high, roll(e, -8, 1))
            along_y = jnp.where(below, roll(e, 1, 1) + roll(m, -1, 1), roll(m, 1, 1) + roll(e, -1, 1))
            parts.append(along_x + along_y)
        results.append(parts)
    return results


def relax(source, spread):
    return tuple(s + COUPLE * t for s, t in zip(source, spread))


def masked(field):
    keep = inside()
    return [tuple(jnp.where(keep, v, 0.0) for v in f) for f in field]


def put_all(ref, field):
    for r in range(DEPTH):
        put(ref, r, field[r])


def get_all(ref):
    return [get(ref, r) for r in range(DEPTH)]


def first_kernel(arrived, factors, over_factors, over_source, main_out, over_out, *edges):
    factorize([layer(arrived, 2, r) for r in range(DEPTH)], factors)
    main = line_solve([source_layer(arrived, r) for r in range(DEPTH)], factors)
    put_all(main_out, main)
    overlap = [overlap_layer(arrived, r) for r in range(DEPTH)]
    factorize([o[2] for o in overlap], over_factors, True)
    put_all(over_source, [o[:2] for o in overlap])
    over = masked(line_solve([o[:2] for o in overlap], over_factors, True))
    put_all(over_out, over)
    put_edges(main, over, edges)


def middle_kernel(arrived, factors, main_in, over_in, low, high, main_out, *edges):
    spread = transverse(get_all(main_in), get_all(over_in), (low, high))
    main = line_solve([relax(source_layer(arrived, r), spread[r]) for r in range(DEPTH)], factors)
    put_all(main_out, main)
    put_edges(main, None, edges)


def middle_over_kernel(over_factors, over_source, main_in, over_in, low, high, over_out):
    spread = over_transverse(get_all(main_in), get_all(over_in), (low, high))
    over = line_solve([relax(get(over_source, r), spread[r]) for r in range(DEPTH)], over_factors, True)
    put_all(over_out, masked(over))


def last_kernel(arrived, factors, main_in, over_in, low, high, out):
    spread = transverse(get_all(main_in), get_all(over_in), (low, high))
    field = line_solve([relax(source_layer(arrived, r), spread[r]) for r in range(DEPTH)], factors)
    for r in range(DEPTH):
        for c in range(2):
            out[pl.ds(c * 8 + r, SLABS, stride=16), :] = field[r][c]


def call(kernel, name, outs, *args, scratch=(), spec=VMEM):
    return pl.pallas_call(
        kernel,
        out_shape=[jax.ShapeDtypeStruct(s, F32) for s in outs],
        in_specs=[spec] * len(args),
        out_specs=[VMEM] * len(outs),
        scratch_shapes=list(scratch),
        compiler_params=pltpu.CompilerParams(vmem_limit_bytes=(32 if spec is VMEM else 60) << 20),
        cost_estimate=pl.CostEstimate(flops=2_000_000, bytes_accessed=1_000_000, transcendentals=0),
        name=name,
    )(*args)


FIELD = (DEPTH * 2 * SLABS, LANES)
FACTORS = (N_FACTORS * 2 * SLABS, LANES)
EDGE = (3 * SLABS, LANES)
SHORT_EDGE = (2 * SLABS, LANES)

RING_UP = [(i, (i + 1) % TILES) for i in range(TILES)]
RING_DOWN = [(b, a) for a, b in RING_UP]


def exchange(low, high):
    return lax.ppermute(high, "tile", RING_UP), lax.ppermute(low, "tile", RING_DOWN)


def local(source, labels, permittivity):
    rows = source.reshape(2 * 16 * 8, 256)
    marks = labels.reshape(16 * 8, 256)
    (packed,) = call(
        pack_kernel, "pack", [(SLABS * ROWS, LANES)], permittivity, rows, marks, spec=HBM,
        scratch=[
            pltpu.VMEM((2, 3 * LANES, LANES), F32),
            pltpu.VMEM((2, LANES, LANES), jnp.int32),
            pltpu.SMEM((8,), F32),
            pltpu.SemaphoreType.DMA((5,)),
        ],
    )
    arrived = lax.all_to_all(packed.reshape(SLABS, ROWS // 4, 4, LANES), "slab", 0, 0).reshape(SLABS * ROWS, LANES)
    factors, over_factors, over_source, main, over, *edges = call(
        first_kernel, "first", [FACTORS, FACTORS, FIELD, FIELD, FIELD, EDGE, EDGE], arrived
    )
    halos = exchange(*edges)
    next_main, *edges = call(
        middle_kernel, "middle", [FIELD, SHORT_EDGE, SHORT_EDGE], arrived, factors, main, over, *halos
    )
    next_halos = exchange(*edges)
    (over,) = call(middle_over_kernel, "middle_over", [FIELD], over_factors, over_source, main, over, *halos)
    (packed,) = call(
        last_kernel, "last", [(SLABS * 16, LANES)], arrived, factors, next_main, over, *next_halos
    )
    arrived = lax.all_to_all(packed.reshape(SLABS, 16, LANES), "slab", 0, 0).reshape(SLABS * 16, LANES)
    (out,) = call(
        unpack_kernel, "unpack", [(2 * 16 * 8, 256)], arrived, scratch=[pltpu.VMEM((2, 2 * LANES, LANES), F32)]
    )
    return out.reshape(2, 16, 8, 256)


def solution(mesh):
    placed = (P("tilt", "slab", "tile", None), P("slab", "tile", "tilt"), P("tilt"))
    return jax.shard_map(
        local,
        mesh=mesh,
        in_specs=placed,
        out_specs=P("tilt", "slab", "tile", None),
        check_vma=False,
    )
```

```python
import jax
import jax.numpy as jnp
from jax import lax
from jax.experimental import pallas as pl
from jax.experimental.pallas import tpu as pltpu
from jax.sharding import PartitionSpec as P

PML = 8
COUPLE = 0.02
WAVE_SHIFT = 0.15
DAMPING = 0.15
ABSORB = 0.5
NZ = 512
SLABS = 32
TILES = 8
LANES = 128
DEPTH = 8
STEPS = 6
F32 = jnp.float32
VMEM = pl.BlockSpec(memory_space=pltpu.VMEM)
HBM = pl.BlockSpec(memory_space=pltpu.HBM)


ROWS = 36


def roll(x, shift, axis):
    shift %= x.shape[axis]
    return x if shift == 0 else pltpu.roll(x, shift, axis)


def cmul(a, b):
    return a[0] * b[0] - a[1] * b[1], a[0] * b[1] + a[1] * b[0]


def cadd(a, b):
    return a[0] + b[0], a[1] + b[1]


def csub(a, b):
    return a[0] - b[0], a[1] - b[1]


def crecip(a):
    scale = 1.0 / (a[0] * a[0] + a[1] * a[1])
    return a[0] * scale, -a[1] * scale


def lanes8():
    return lax.broadcasted_iota(jnp.int32, (8, LANES), 1)


def lanes8():
    return lax.broadcasted_iota(jnp.int32, (8, LANES), 1)


def block_transpose(turned):
    block = lanes8() // 8
    for bit in (1, 2, 4, 8):
        odd = (block & bit) != 0
        turned = [jnp.where(odd, turned[(j + bit) % 16], turned[j]) for j in range(16)]
    return [roll(turned[-c % 16], -8 * c, 1) for c in range(16)]


def turn(arrays, shift=0):
    return [roll(array, shift + 8 * i, 1) for i, array in enumerate(arrays)]


def pack_kernel(table_hbm, source, labels, out, sides, marks, table, sems):
    copies = [pltpu.make_async_copy(table_hbm, table, sems.at[0])]
    for side in range(2):
        lanes = pl.ds(side * LANES, LANES)
        copies.append(pltpu.make_async_copy(labels.at[:, lanes], marks.at[side], sems.at[1 + side]))
        into = sides.at[side, pl.ds(0, 2 * LANES)]
        copies.append(pltpu.make_async_copy(source.at[:, lanes], into, sems.at[3 + side]))
    for copy in copies:
        copy.start()
    for copy in copies:
        copy.wait()
    for side in range(2):
        lab = marks[side]
        rel = jnp.full(lab.shape, table[0], F32)
        for m in range(1, 8):
            rel = jnp.where(lab == m, table[m], rel)
        sides[side, pl.ds(2 * LANES, LANES), :] = rel

    def load(side, quantity):
        places = [quantity * LANES + half * 64 + x for half in range(2) for x in range(8)]
        return [sides[side, pl.ds(place, 8, stride=8), :] for place in places]

    slot = lanes8() % 8
    first = slot < 4
    pairs, singles = [], []
    for side in range(2):
        arrays = [load(side, quantity) for quantity in range(3)]
        for quantity in range(3):
            for block, part in enumerate(block_transpose(turn(arrays[quantity]))):
                out[pl.ds((16 * side + block) * ROWS + quantity * 8, 8), :] = part
        pair = [jnp.where(first, v, w) for v, w in zip(turn(arrays[0], 2), turn(arrays[1], 6))]
        pairs += block_transpose(pair)
        late = [roll(v, 4, 0) for v in turn(arrays[2], 6)]
        singles += block_transpose([jnp.where(first, v, w) for v, w in zip(turn(arrays[2], 2), late)])
    from_above = (slot & 2) != 0
    for chunk in range(SLABS):
        lower = (chunk + 16) % SLABS if chunk % 16 == 0 else chunk
        upper = (chunk + 1) % SLABS
        out[pl.ds(chunk * ROWS + 24, 8), :] = jnp.where(from_above, pairs[upper], pairs[lower])
        out[pl.ds(chunk * ROWS + 32, 4), :] = jnp.where(from_above, singles[upper], singles[lower])[:4]


def unpack_kernel(arrived, out, sides):
    for side in range(2):
        for c in range(2):
            parts = [arrived[pl.ds((16 * side + b) * 16 + c * 8, 8), :] for b in range(16)]
            for i, part in enumerate(block_transpose(turn(parts))):
                half, x = divmod(i, 8)
                sides[side, pl.ds(c * LANES + half * 64 + x, 8, stride=8), :] = part
        out[:, pl.ds(side * LANES, LANES)] = sides[side]


def lane_ids():
    lane = lax.broadcasted_iota(jnp.int32, (SLABS, LANES), 1)
    return lane >= 64, (lane // 8) % 8, lane % 8


def upper_half(overlap):
    lane = lax.broadcasted_iota(jnp.int32, (SLABS, LANES), 1)
    if overlap:
        lane = (lane + jnp.where(lane % 8 >= 4, 8, LANES - 8)) % LANES
    return lane >= 64


def up(a, h, upper):
    if h >= 2:
        return roll(a, h // 2, 0)
    turned = roll(a, 64, 1)
    return jnp.where(upper, turned, roll(turned, 1, 0))


def down(a, h, upper):
    if h >= 2:
        return roll(a, -(h // 2), 0)
    turned = roll(a, 64, 1)
    return jnp.where(upper, roll(turned, -1, 0), turned)


def both(f, a, h, upper):
    return f(a[0], h, upper), f(a[1], h, upper)


def layer(ref, quantity, r):
    return ref[pl.ds(quantity * 8 + r, SLABS, stride=ROWS), :]


def source_layer(ref, r):
    return layer(ref, 0, r), layer(ref, 1, r)


def overlap_layer(ref, r):
    _, _, y = lane_ids()
    pair = ref[pl.ds(24 + r, SLABS, stride=ROWS), :]
    single = ref[pl.ds(32 + r % 4, SLABS, stride=ROWS), :]
    quantities = []
    for packed, base in ((pair, 0), (pair, 4), (single, 4 * (r // 4))):
        quantities.append(jnp.where(y >= 4, roll(packed, -2 - base, 1), roll(packed, 6 - base, 1)))
    used = (y <= 1) | (y >= 6)
    return quantities[0], quantities[1], jnp.where(used, quantities[2], 1.0)


def inside():
    chunk = lax.axis_index("slab")
    _, _, y = lane_ids()
    below = (y >= 6) & jnp.broadcast_to(chunk > 0, y.shape)
    above = (y <= 1) & jnp.broadcast_to(chunk < SLABS - 1, y.shape)
    return below | above


def put(ref, i, a):
    ref[pl.ds(2 * i * SLABS, SLABS), :] = a[0]
    ref[pl.ds((2 * i + 1) * SLABS, SLABS), :] = a[1]


def get(ref, i):
    return ref[pl.ds(2 * i * SLABS, SLABS), :], ref[pl.ds((2 * i + 1) * SLABS, SLABS), :]


N_FACTORS = 7 + 2 * STEPS + 1


def factorize(relatives, factors, overlap=False):
    upper = upper_half(overlap)
    row = lax.broadcasted_iota(jnp.int32, (SLABS, LANES), 0)
    first = row * 16 + jnp.where(upper, 8, 0)
    pivots = []
    diagonal = None
    for r in range(DEPTH):
        z = first + r
        relative = relatives[r]
        inward = jnp.maximum(jnp.maximum(PML - z, z - (NZ - 1 - PML)), 0)
        fraction = inward.astype(F32) / PML
        diagonal = (
            (2.0 + 4.0 * COUPLE) - WAVE_SHIFT * relative,
            (DAMPING * WAVE_SHIFT) * relative + ABSORB * fraction * fraction,
        )
        if r < DEPTH - 1:
            pivots.append(crecip(diagonal if r == 0 else csub(diagonal, pivots[-1])))
            put(factors, r, pivots[-1])
    to_first = pivots[0]
    first_first = pivots[0]
    for r in range(1, DEPTH - 1):
        reached = cmul(to_first, to_first)
        to_first = cmul(to_first, pivots[r])
        first_first = cadd(first_first, cmul(reached, pivots[r]))
    corner = to_first
    last_last = pivots[-1]
    low = (row == 0) & jnp.logical_not(upper)
    left = tuple(jnp.where(low, 0.0, v) for v in corner)
    high = (row == SLABS - 1) & upper
    next_first = tuple(jnp.where(high, 0.0, v) for v in both(down, first_first, 1, upper))
    d = csub(csub(diagonal, last_last), next_first)
    for step in range(STEPS):
        h = 1 << step
        right = both(down, left, h, upper)
        inverse = crecip(d)
        alpha = cmul(left, both(up, inverse, h, upper))
        gamma = cmul(right, both(down, inverse, h, upper))
        put(factors, 7 + 2 * step, alpha)
        put(factors, 8 + 2 * step, gamma)
        d = csub(csub(d, cmul(alpha, left)), cmul(gamma, right))
        left = cmul(alpha, both(up, left, h, upper))
    put(factors, 7 + 2 * STEPS, crecip(d))


def line_solve(rhs, factors, overlap=False):
    pivots = [get(factors, r) for r in range(DEPTH - 1)]
    gone = [rhs[0]]
    for r in range(1, DEPTH - 1):
        gone.append(cadd(rhs[r], cmul(pivots[r - 1], gone[-1])))
    last = cmul(pivots[-1], gone[-1])
    reach = pivots[0]
    reaches = []
    first = cmul(pivots[0], gone[0])
    for r in range(1, DEPTH - 1):
        reaches.append(reach)
        reach = cmul(reach, pivots[r])
        first = cadd(first, cmul(reach, gone[r]))
    upper = upper_half(overlap)
    row = lax.broadcasted_iota(jnp.int32, (SLABS, LANES), 0)
    high = (row == SLABS - 1) & upper
    low = (row == 0) & jnp.logical_not(upper)
    after = tuple(jnp.where(high, 0.0, v) for v in both(down, first, 1, upper))
    g = cadd(cadd(rhs[DEPTH - 1], last), after)
    for step in range(STEPS):
        h = 1 << step
        from_low = cmul(get(factors, 7 + 2 * step), both(up, g, h, upper))
        from_high = cmul(get(factors, 8 + 2 * step), both(down, g, h, upper))
        g = cadd(g, cadd(from_low, from_high))
    separator = cmul(get(factors, 7 + 2 * STEPS), g)
    before = tuple(jnp.where(low, 0.0, v) for v in both(up, separator, 1, upper))
    field = [None] * DEPTH
    field[DEPTH - 1] = separator
    for r in range(DEPTH - 2, -1, -1):
        lit = cadd(gone[r], before if r == 0 else cmul(reaches[r - 1], before))
        field[r] = cmul(pivots[r], cadd(lit, field[r + 1]))
    return field


def put_edges(main, over, edges):
    _, x, y = lane_ids()
    for edge, is_high in zip(edges, (False, True)):
        for c in range(2):
            total = None
            for r in range(DEPTH):
                moved = roll(main[r][c], 8 * (r - 7) if is_high else 8 * r, 1)
                total = moved if r == 0 else jnp.where(x == r, moved, total)
            edge[pl.ds(c * SLABS, SLABS), :] = total
        if over is None:
            continue
        below_at, above_at = (6, 0) if is_high else (7, 1)
        total = jnp.zeros((SLABS, LANES), F32)
        for c in range(2):
            for r in range(DEPTH):
                i, k = 2 * c + r // 4, r % 4
                below = (x == (below_at + i) % 8) & (y == 7 - k)
                above = (x == (above_at + i) % 8) & (y == k)
                total = jnp.where(below, roll(over[r][c], 8 * i - k, 1), total)
                total = jnp.where(above, roll(over[r][c], 8 * i + k, 1), total)
        edge[pl.ds(2 * SLABS, SLABS), :] = total


def halo(refs, place):
    tile = lax.axis_index("tile")
    rows = pl.ds(place * SLABS, SLABS)
    keep = (tile > 0, tile < TILES - 1)
    return [jnp.where(jnp.broadcast_to(k, (SLABS, LANES)), ref[rows, :], 0.0) for ref, k in zip(refs, keep)]


def transverse(main, over, halos):
    _, x, y = lane_ids()
    packed = [halo(halos, c) for c in range(2)]
    results = []
    for r in range(DEPTH):
        parts = []
        for c in range(2):
            m, e = main[r][c], over[r][c]
            low, high = packed[c]
            along_x = jnp.where(x == 0, roll(low, -8 * r, 1), roll(m, 8, 1))
            along_x += jnp.where(x == 7, roll(high, 8 * (7 - r), 1), roll(m, -8, 1))
            along_y = jnp.where(y == 0, roll(e, 1, 1), roll(m, 1, 1))
            along_y += jnp.where(y == 7, roll(e, -1, 1), roll(m, -1, 1))
            parts.append(along_x + along_y)
        results.append(parts)
    return results


def over_transverse(main, over, halos):
    _, x, y = lane_ids()
    low, high = halo(halos, 2)
    below = y >= 4
    at_low = x == jnp.where(below, 7, 1)
    at_high = x == jnp.where(below, 6, 0)
    results = []
    for r in range(DEPTH):
        parts = []
        for c in range(2):
            m, e = main[r][c], over[r][c]
            i, k = 2 * c + r // 4, r % 4
            from_low = jnp.where(below, roll(low, -56 - 8 * i + k, 1), roll(low, -56 - 8 * i - k, 1))
            from_high = jnp.where(below, roll(high, 56 - 8 * i + k, 1), roll(high, 56 - 8 * i - k, 1))
            along_x = jnp.where(at_low, from_low, roll(e, 8, 1)) + jnp.where(at_high, from_high, roll(e, -8, 1))
            along_y = jnp.where(below, roll(e, 1, 1) + roll(m, -1, 1), roll(m, 1, 1) + roll(e, -1, 1))
            parts.append(along_x + along_y)
        results.append(parts)
    return results


def relax(source, spread):
    return tuple(s + COUPLE * t for s, t in zip(source, spread))


def masked(field):
    keep = inside()
    return [tuple(jnp.where(keep, v, 0.0) for v in f) for f in field]


def put_all(ref, field):
    for r in range(DEPTH):
        put(ref, r, field[r])


def get_all(ref):
    return [get(ref, r) for r in range(DEPTH)]


def first_kernel(arrived, factors, over_factors, over_source, main_out, over_out, *edges):
    factorize([layer(arrived, 2, r) for r in range(DEPTH)], factors)
    main = line_solve([source_layer(arrived, r) for r in range(DEPTH)], factors)
    put_all(main_out, main)
    overlap = [overlap_layer(arrived, r) for r in range(DEPTH)]
    factorize([o[2] for o in overlap], over_factors, True)
    put_all(over_source, [o[:2] for o in overlap])
    over = masked(line_solve([o[:2] for o in overlap], over_factors, True))
    put_all(over_out, over)
    put_edges(main, over, edges)


def middle_kernel(arrived, factors, main_in, over_in, low, high, main_out, *edges):
    spread = transverse(get_all(main_in), get_all(over_in), (low, high))
    main = line_solve([relax(source_layer(arrived, r), spread[r]) for r in range(DEPTH)], factors)
    put_all(main_out, main)
    put_edges(main, None, edges)


def middle_over_kernel(over_factors, over_source, main_in, over_in, low, high, over_out):
    spread = over_transverse(get_all(main_in), get_all(over_in), (low, high))
    over = line_solve([relax(get(over_source, r), spread[r]) for r in range(DEPTH)], over_factors, True)
    put_all(over_out, masked(over))


def last_kernel(arrived, factors, main_in, over_in, low, high, out):
    spread = transverse(get_all(main_in), get_all(over_in), (low, high))
    field = line_solve([relax(source_layer(arrived, r), spread[r]) for r in range(DEPTH)], factors)
    for r in range(DEPTH):
        for c in range(2):
            out[pl.ds(c * 8 + r, SLABS, stride=16), :] = field[r][c]


def call(kernel, name, outs, *args, scratch=(), spec=VMEM):
    return pl.pallas_call(
        kernel,
        out_shape=[jax.ShapeDtypeStruct(s, F32) for s in outs],
        in_specs=[spec] * len(args),
        out_specs=[VMEM] * len(outs),
        scratch_shapes=list(scratch),
        compiler_params=pltpu.CompilerParams(vmem_limit_bytes=32 << 20),
        cost_estimate=pl.CostEstimate(flops=2_000_000, bytes_accessed=1_000_000, transcendentals=0),
        name=name,
    )(*args)


FIELD = (DEPTH * 2 * SLABS, LANES)
FACTORS = (N_FACTORS * 2 * SLABS, LANES)
EDGE = (3 * SLABS, LANES)
SHORT_EDGE = (2 * SLABS, LANES)

RING_UP = [(i, (i + 1) % TILES) for i in range(TILES)]
RING_DOWN = [(b, a) for a, b in RING_UP]


def exchange(low, high):
    return lax.ppermute(high, "tile", RING_UP), lax.ppermute(low, "tile", RING_DOWN)


def local(source, labels, permittivity):
    rows = source.reshape(2 * 16 * 8, 256)
    marks = labels.reshape(16 * 8, 256)
    inputs = [pltpu.with_memory_space_constraint(v, pltpu.HBM) for v in (permittivity, rows, marks)]
    (packed,) = call(
        pack_kernel, "pack", [(SLABS * ROWS, LANES)], *inputs, spec=HBM,
        scratch=[
            pltpu.VMEM((2, 3 * LANES, LANES), F32),
            pltpu.VMEM((2, LANES, LANES), jnp.int32),
            pltpu.SMEM((8,), F32),
            pltpu.SemaphoreType.DMA((5,)),
        ],
    )
    arrived = lax.all_to_all(packed.reshape(SLABS, ROWS // 4, 4, LANES), "slab", 0, 0).reshape(SLABS * ROWS, LANES)
    factors, over_factors, over_source, main, over, *edges = call(
        first_kernel, "first", [FACTORS, FACTORS, FIELD, FIELD, FIELD, EDGE, EDGE], arrived
    )
    halos = exchange(*edges)
    next_main, *edges = call(
        middle_kernel, "middle", [FIELD, SHORT_EDGE, SHORT_EDGE], arrived, factors, main, over, *halos
    )
    next_halos = exchange(*edges)
    (over,) = call(middle_over_kernel, "middle_over", [FIELD], over_factors, over_source, main, over, *halos)
    (packed,) = call(
        last_kernel, "last", [(SLABS * 16, LANES)], arrived, factors, next_main, over, *next_halos
    )
    arrived = lax.all_to_all(packed.reshape(SLABS, 16, LANES), "slab", 0, 0).reshape(SLABS * 16, LANES)
    (out,) = call(
        unpack_kernel, "unpack", [(2 * 16 * 8, 256)], arrived, scratch=[pltpu.VMEM((2, 2 * LANES, LANES), F32)]
    )
    return out.reshape(2, 16, 8, 256)


def solution(mesh):
    placed = (P("tilt", "slab", "tile", None), P("slab", "tile", "tilt"), P("tilt"))
    return jax.shard_map(
        local,
        mesh=mesh,
        in_specs=placed,
        out_specs=P("tilt", "slab", "tile", None),
        check_vma=False,
    )
```

```python
import jax
import jax.numpy as jnp
from jax import lax
from jax.experimental import pallas as pl
from jax.experimental.pallas import tpu as pltpu
from jax.sharding import PartitionSpec as P

PML = 8
COUPLE = 0.02
WAVE_SHIFT = 0.15
DAMPING = 0.15
ABSORB = 0.5
NZ = 512
SLABS = 32
TILES = 8
LANES = 128
DEPTH = 8
STEPS = 6
F32 = jnp.float32
VMEM = pl.BlockSpec(memory_space=pltpu.VMEM)
HBM = pl.BlockSpec(memory_space=pltpu.HBM)


ROWS = 36


def roll(x, shift, axis):
    shift %= x.shape[axis]
    return x if shift == 0 else pltpu.roll(x, shift, axis)


def cmul(a, b):
    return a[0] * b[0] - a[1] * b[1], a[0] * b[1] + a[1] * b[0]


def cadd(a, b):
    return a[0] + b[0], a[1] + b[1]


def csub(a, b):
    return a[0] - b[0], a[1] - b[1]


def crecip(a):
    scale = 1.0 / (a[0] * a[0] + a[1] * a[1])
    return a[0] * scale, -a[1] * scale


def lanes8():
    return lax.broadcasted_iota(jnp.int32, (8, LANES), 1)


def lanes8():
    return lax.broadcasted_iota(jnp.int32, (8, LANES), 1)


def block_transpose(turned):
    block = lanes8() // 8
    for bit in (1, 2, 4, 8):
        odd = (block & bit) != 0
        turned = [jnp.where(odd, turned[(j + bit) % 16], turned[j]) for j in range(16)]
    return [roll(turned[-c % 16], -8 * c, 1) for c in range(16)]


def turn(arrays, shift=0):
    return [roll(array, shift + 8 * i, 1) for i, array in enumerate(arrays)]


def pack_kernel(table_hbm, source, labels, out, sides, marks, table, sems):
    copies = [pltpu.make_async_copy(table_hbm, table, sems.at[0])]
    for side in range(2):
        lanes = pl.ds(side * LANES, LANES)
        copies.append(pltpu.make_async_copy(labels.at[:, lanes], marks.at[side], sems.at[1 + side]))
        into = sides.at[side, pl.ds(0, 2 * LANES)]
        copies.append(pltpu.make_async_copy(source.at[:, lanes], into, sems.at[3 + side]))
    for copy in copies:
        copy.start()
    for copy in copies:
        copy.wait()
    for side in range(2):
        lab = marks[side]
        rel = jnp.full(lab.shape, table[0], F32)
        for m in range(1, 8):
            rel = jnp.where(lab == m, table[m], rel)
        sides[side, pl.ds(2 * LANES, LANES), :] = rel

    def load(side, quantity):
        places = [quantity * LANES + half * 64 + x for half in range(2) for x in range(8)]
        return [sides[side, pl.ds(place, 8, stride=8), :] for place in places]

    slot = lanes8() % 8
    first = slot < 4
    pairs, singles = [], []
    for side in range(2):
        arrays = [load(side, quantity) for quantity in range(3)]
        for quantity in range(3):
            for block, part in enumerate(block_transpose(turn(arrays[quantity]))):
                out[pl.ds((16 * side + block) * ROWS + quantity * 8, 8), :] = part
        pair = [jnp.where(first, v, w) for v, w in zip(turn(arrays[0], 2), turn(arrays[1], 6))]
        pairs += block_transpose(pair)
        late = [roll(v, 4, 0) for v in turn(arrays[2], 6)]
        singles += block_transpose([jnp.where(first, v, w) for v, w in zip(turn(arrays[2], 2), late)])
    from_above = (slot & 2) != 0
    for chunk in range(SLABS):
        lower = (chunk + 16) % SLABS if chunk % 16 == 0 else chunk
        upper = (chunk + 1) % SLABS
        out[pl.ds(chunk * ROWS + 24, 8), :] = jnp.where(from_above, pairs[upper], pairs[lower])
        out[pl.ds(chunk * ROWS + 32, 4), :] = jnp.where(from_above, singles[upper], singles[lower])[:4]


def unpack_kernel(arrived, out, sides):
    for side in range(2):
        for c in range(2):
            parts = [arrived[pl.ds((16 * side + b) * 16 + c * 8, 8), :] for b in range(16)]
            for i, part in enumerate(block_transpose(turn(parts))):
                half, x = divmod(i, 8)
                sides[side, pl.ds(c * LANES + half * 64 + x, 8, stride=8), :] = part
        out[:, pl.ds(side * LANES, LANES)] = sides[side]


def lane_ids():
    lane = lax.broadcasted_iota(jnp.int32, (SLABS, LANES), 1)
    return lane >= 64, (lane // 8) % 8, lane % 8


def upper_half(overlap):
    lane = lax.broadcasted_iota(jnp.int32, (SLABS, LANES), 1)
    if overlap:
        lane = (lane + jnp.where(lane % 8 >= 4, 8, LANES - 8)) % LANES
    return lane >= 64


def up(a, h, upper):
    if h >= 2:
        return roll(a, h // 2, 0)
    turned = roll(a, 64, 1)
    return jnp.where(upper, turned, roll(turned, 1, 0))


def down(a, h, upper):
    if h >= 2:
        return roll(a, -(h // 2), 0)
    turned = roll(a, 64, 1)
    return jnp.where(upper, roll(turned, -1, 0), turned)


def both(f, a, h, upper):
    return f(a[0], h, upper), f(a[1], h, upper)


def layer(ref, quantity, r):
    return ref[pl.ds(quantity * 8 + r, SLABS, stride=ROWS), :]


def source_layer(ref, r):
    return layer(ref, 0, r), layer(ref, 1, r)


def overlap_layer(ref, r):
    _, _, y = lane_ids()
    pair = ref[pl.ds(24 + r, SLABS, stride=ROWS), :]
    single = ref[pl.ds(32 + r % 4, SLABS, stride=ROWS), :]
    quantities = []
    for packed, base in ((pair, 0), (pair, 4), (single, 4 * (r // 4))):
        quantities.append(jnp.where(y >= 4, roll(packed, -2 - base, 1), roll(packed, 6 - base, 1)))
    used = (y <= 1) | (y >= 6)
    return quantities[0], quantities[1], jnp.where(used, quantities[2], 1.0)


def inside():
    chunk = lax.axis_index("slab")
    _, _, y = lane_ids()
    below = (y >= 6) & jnp.broadcast_to(chunk > 0, y.shape)
    above = (y <= 1) & jnp.broadcast_to(chunk < SLABS - 1, y.shape)
    return below | above


def put(ref, i, a):
    ref[pl.ds(2 * i * SLABS, SLABS), :] = a[0]
    ref[pl.ds((2 * i + 1) * SLABS, SLABS), :] = a[1]


def get(ref, i):
    return ref[pl.ds(2 * i * SLABS, SLABS), :], ref[pl.ds((2 * i + 1) * SLABS, SLABS), :]


N_FACTORS = 7 + 2 * STEPS + 1


def factorize(relatives, factors, overlap=False):
    upper = upper_half(overlap)
    row = lax.broadcasted_iota(jnp.int32, (SLABS, LANES), 0)
    first = row * 16 + jnp.where(upper, 8, 0)
    pivots = []
    diagonal = None
    for r in range(DEPTH):
        z = first + r
        relative = relatives[r]
        inward = jnp.maximum(jnp.maximum(PML - z, z - (NZ - 1 - PML)), 0)
        fraction = inward.astype(F32) / PML
        diagonal = (
            (2.0 + 4.0 * COUPLE) - WAVE_SHIFT * relative,
            (DAMPING * WAVE_SHIFT) * relative + ABSORB * fraction * fraction,
        )
        if r < DEPTH - 1:
            pivots.append(crecip(diagonal if r == 0 else csub(diagonal, pivots[-1])))
            put(factors, r, pivots[-1])
    to_first = pivots[0]
    first_first = pivots[0]
    for r in range(1, DEPTH - 1):
        reached = cmul(to_first, to_first)
        to_first = cmul(to_first, pivots[r])
        first_first = cadd(first_first, cmul(reached, pivots[r]))
    corner = to_first
    last_last = pivots[-1]
    low = (row == 0) & jnp.logical_not(upper)
    left = tuple(jnp.where(low, 0.0, v) for v in corner)
    high = (row == SLABS - 1) & upper
    next_first = tuple(jnp.where(high, 0.0, v) for v in both(down, first_first, 1, upper))
    d = csub(csub(diagonal, last_last), next_first)
    for step in range(STEPS):
        h = 1 << step
        right = both(down, left, h, upper)
        inverse = crecip(d)
        alpha = cmul(left, both(up, inverse, h, upper))
        gamma = cmul(right, both(down, inverse, h, upper))
        put(factors, 7 + 2 * step, alpha)
        put(factors, 8 + 2 * step, gamma)
        d = csub(csub(d, cmul(alpha, left)), cmul(gamma, right))
        left = cmul(alpha, both(up, left, h, upper))
    put(factors, 7 + 2 * STEPS, crecip(d))


def line_solve(rhs, factors, overlap=False):
    pivots = [get(factors, r) for r in range(DEPTH - 1)]
    gone = [rhs[0]]
    for r in range(1, DEPTH - 1):
        gone.append(cadd(rhs[r], cmul(pivots[r - 1], gone[-1])))
    last = cmul(pivots[-1], gone[-1])
    reach = pivots[0]
    reaches = []
    first = cmul(pivots[0], gone[0])
    for r in range(1, DEPTH - 1):
        reaches.append(reach)
        reach = cmul(reach, pivots[r])
        first = cadd(first, cmul(reach, gone[r]))
    upper = upper_half(overlap)
    row = lax.broadcasted_iota(jnp.int32, (SLABS, LANES), 0)
    high = (row == SLABS - 1) & upper
    low = (row == 0) & jnp.logical_not(upper)
    after = tuple(jnp.where(high, 0.0, v) for v in both(down, first, 1, upper))
    g = cadd(cadd(rhs[DEPTH - 1], last), after)
    for step in range(STEPS):
        h = 1 << step
        from_low = cmul(get(factors, 7 + 2 * step), both(up, g, h, upper))
        from_high = cmul(get(factors, 8 + 2 * step), both(down, g, h, upper))
        g = cadd(g, cadd(from_low, from_high))
    separator = cmul(get(factors, 7 + 2 * STEPS), g)
    before = tuple(jnp.where(low, 0.0, v) for v in both(up, separator, 1, upper))
    field = [None] * DEPTH
    field[DEPTH - 1] = separator
    for r in range(DEPTH - 2, -1, -1):
        lit = cadd(gone[r], before if r == 0 else cmul(reaches[r - 1], before))
        field[r] = cmul(pivots[r], cadd(lit, field[r + 1]))
    return field


def put_edges(main, over, source, relatives, edges):
    _, x, y = lane_ids()
    for edge, is_high in zip(edges, (False, True)):
        near, far = (7, 6) if is_high else (0, 1)
        lines = [([f[c] for f in main], line) for line in (near, far) for c in range(2)]
        lines += [([f[c] for f in source], near) for c in range(2)] + [(relatives, near)]
        for place, (layers, line) in enumerate(lines):
            total = None
            for r in range(DEPTH):
                moved = roll(layers[r], 8 * (r - line), 1)
                total = moved if r == 0 else jnp.where(x == r, moved, total)
            edge[pl.ds(place * SLABS, SLABS), :] = total
        below_at, above_at = (6, 0) if is_high else (7, 1)
        total = jnp.zeros((SLABS, LANES), F32)
        for c in range(2):
            for r in range(DEPTH):
                i, k = 2 * c + r // 4, r % 4
                below = (x == (below_at + i) % 8) & (y == 7 - k)
                above = (x == (above_at + i) % 8) & (y == k)
                total = jnp.where(below, roll(over[r][c], 8 * i - k, 1), total)
                total = jnp.where(above, roll(over[r][c], 8 * i + k, 1), total)
        edge[pl.ds(7 * SLABS, SLABS), :] = total


def within():
    tile = lax.axis_index("tile")
    _, x, _ = lane_ids()
    low = (x < 4) & jnp.broadcast_to(tile > 0, x.shape)
    high = (x >= 4) & jnp.broadcast_to(tile < TILES - 1, x.shape)
    return low | high


def beside(halos, place, r):
    _, x, _ = lane_ids()
    low, high = (ref[pl.ds(place * SLABS, SLABS), :] for ref in halos)
    return jnp.where(x < 4, roll(low, -8 * r, 1), roll(high, 8 * (7 - r), 1))


def over_beside(halos, c, r):
    tile = lax.axis_index("tile")
    _, x, y = lane_ids()
    low, high = (ref[pl.ds(7 * SLABS, SLABS), :] for ref in halos)
    low = jnp.where(jnp.broadcast_to(tile > 0, x.shape), low, 0.0)
    high = jnp.where(jnp.broadcast_to(tile < TILES - 1, x.shape), high, 0.0)
    below = y >= 4
    i, k = 2 * c + r // 4, r % 4
    from_low = jnp.where(below, roll(low, -56 - 8 * i + k, 1), roll(low, -56 - 8 * i - k, 1))
    from_high = jnp.where(below, roll(high, 56 - 8 * i + k, 1), roll(high, 56 - 8 * i - k, 1))
    return jnp.where(x == jnp.where(below, 7, 1), from_low, from_high)


def sum_y(field, over):
    _, _, y = lane_ids()
    lower = jnp.where(y == 0, roll(over, 1, 1), roll(field, 1, 1))
    return lower + jnp.where(y == 7, roll(over, -1, 1), roll(field, -1, 1))


def sum_main(main, over, near):
    _, x, _ = lane_ids()
    along_x = jnp.where(x == 0, near, roll(main, 8, 1)) + jnp.where(x == 7, near, roll(main, -8, 1))
    return along_x + sum_y(main, over)


def sum_over(main, over, over_near):
    _, x, y = lane_ids()
    below = y >= 4
    along_x = jnp.where(x == jnp.where(below, 7, 1), over_near, roll(over, 8, 1))
    along_x += jnp.where(x == jnp.where(below, 6, 0), over_near, roll(over, -8, 1))
    return along_x + jnp.where(below, roll(over, 1, 1) + roll(main, -1, 1), roll(main, 1, 1) + roll(over, -1, 1))


def sum_near(main, near, far, over_near):
    return far + main + sum_y(near, over_near)


def relax(source, spread):
    return tuple(s + COUPLE * t for s, t in zip(source, spread))


def masked(field, keep):
    return [tuple(jnp.where(keep, v, 0.0) for v in f) for f in field]


def put_all(ref, field):
    for r in range(DEPTH):
        put(ref, r, field[r])


def get_all(ref):
    return [get(ref, r) for r in range(DEPTH)]


def first_kernel(arrived, factors, over_factors, over_source, main_out, over_out, *edges):
    relatives = [layer(arrived, 2, r) for r in range(DEPTH)]
    source = [source_layer(arrived, r) for r in range(DEPTH)]
    factorize(relatives, factors)
    main = line_solve(source, factors)
    put_all(main_out, main)
    overlap = [overlap_layer(arrived, r) for r in range(DEPTH)]
    factorize([o[2] for o in overlap], over_factors, True)
    put_all(over_source, [o[:2] for o in overlap])
    over = masked(line_solve([o[:2] for o in overlap], over_factors, True), inside())
    put_all(over_out, over)
    put_edges(main, over, source, relatives, edges)


def last_kernel(
    arrived, factors, over_factors, over_source, main_in, over_in, low, high, out, near_factors, main_mid, over_mid, near_mid
):
    halos = (low, high)
    keep = within()
    factorize([beside(halos, 6, r) for r in range(DEPTH)], near_factors)
    main_rhs, over_rhs, near_rhs = [], [], []
    for r in range(DEPTH):
        main_sums, over_sums, near_sums = [], [], []
        for c in range(2):
            rows = pl.ds((2 * r + c) * SLABS, SLABS)
            main, over = main_in[rows, :], over_in[rows, :]
            near = jnp.where(keep, beside(halos, c, r), 0.0)
            far = beside(halos, 2 + c, r)
            over_near = over_beside(halos, c, r)
            main_sums.append(sum_main(main, over, near))
            over_sums.append(sum_over(main, over, over_near))
            near_sums.append(sum_near(main, near, far, over_near))
        main_rhs.append(relax(source_layer(arrived, r), main_sums))
        over_rhs.append(relax(get(over_source, r), over_sums))
        near_rhs.append(relax((beside(halos, 4, r), beside(halos, 5, r)), near_sums))
    put_all(main_mid, line_solve(main_rhs, factors))
    put_all(over_mid, masked(line_solve(over_rhs, over_factors, True), inside()))
    put_all(near_mid, masked(line_solve(near_rhs, near_factors), keep))
    rhs = []
    for r in range(DEPTH):
        parts = zip(get(main_mid, r), get(over_mid, r), get(near_mid, r))
        rhs.append(relax(source_layer(arrived, r), [sum_main(*part) for part in parts]))
    field = line_solve(rhs, factors)
    for r in range(DEPTH):
        for c in range(2):
            out[pl.ds(c * 8 + r, SLABS, stride=16), :] = field[r][c]


def call(kernel, name, outs, *args, scratch=(), spec=VMEM):
    return pl.pallas_call(
        kernel,
        out_shape=[jax.ShapeDtypeStruct(s, F32) for s in outs],
        in_specs=[spec] * len(args),
        out_specs=[VMEM] * len(outs),
        scratch_shapes=list(scratch),
        compiler_params=pltpu.CompilerParams(vmem_limit_bytes=32 << 20),
        cost_estimate=pl.CostEstimate(flops=2_000_000, bytes_accessed=1_000_000, transcendentals=0),
        name=name,
    )(*args)


FIELD = (DEPTH * 2 * SLABS, LANES)
FACTORS = (N_FACTORS * 2 * SLABS, LANES)
EDGE = (8 * SLABS, LANES)

RING_UP = [(i, (i + 1) % TILES) for i in range(TILES)]
RING_DOWN = [(b, a) for a, b in RING_UP]


def exchange(low, high):
    return lax.ppermute(high, "tile", RING_UP), lax.ppermute(low, "tile", RING_DOWN)


def local(source, labels, permittivity):
    rows = source.reshape(2 * 16 * 8, 256)
    marks = labels.reshape(16 * 8, 256)
    inputs = [pltpu.with_memory_space_constraint(v, pltpu.HBM) for v in (permittivity, rows, marks)]
    (packed,) = call(
        pack_kernel, "pack", [(SLABS * ROWS, LANES)], *inputs, spec=HBM,
        scratch=[
            pltpu.VMEM((2, 3 * LANES, LANES), F32),
            pltpu.VMEM((2, LANES, LANES), jnp.int32),
            pltpu.SMEM((8,), F32),
            pltpu.SemaphoreType.DMA((5,)),
        ],
    )
    arrived = lax.all_to_all(packed.reshape(SLABS, ROWS // 4, 4, LANES), "slab", 0, 0).reshape(SLABS * ROWS, LANES)
    factors, over_factors, over_source, main, over, *edges = call(
        first_kernel, "first", [FACTORS, FACTORS, FIELD, FIELD, FIELD, EDGE, EDGE], arrived
    )
    halos = exchange(*edges)
    (packed,) = call(
        last_kernel, "last", [(SLABS * 16, LANES)], arrived, factors, over_factors, over_source, main, over, *halos,
        scratch=[pltpu.VMEM(FACTORS, F32)] + [pltpu.VMEM(FIELD, F32)] * 3,
    )
    arrived = lax.all_to_all(packed.reshape(SLABS, 16, LANES), "slab", 0, 0).reshape(SLABS * 16, LANES)
    (out,) = call(
        unpack_kernel, "unpack", [(2 * 16 * 8, 256)], arrived, scratch=[pltpu.VMEM((2, 2 * LANES, LANES), F32)]
    )
    return out.reshape(2, 16, 8, 256)


def solution(mesh):
    placed = (P("tilt", "slab", "tile", None), P("slab", "tile", "tilt"), P("tilt"))
    return jax.shard_map(
        local,
        mesh=mesh,
        in_specs=placed,
        out_specs=P("tilt", "slab", "tile", None),
        check_vma=False,
    )
```

```python
import jax
import jax.numpy as jnp
from jax import lax
from jax.experimental import pallas as pl
from jax.experimental.pallas import tpu as pltpu
from jax.sharding import PartitionSpec as P

PML = 8
COUPLE = 0.02
WAVE_SHIFT = 0.15
DAMPING = 0.15
ABSORB = 0.5
NZ = 512
SLABS = 32
TILES = 8
LANES = 128
DEPTH = 8
STEPS = 6
F32 = jnp.float32
VMEM = pl.BlockSpec(memory_space=pltpu.VMEM)
HBM = pl.BlockSpec(memory_space=pltpu.HBM)


ROWS = 36


def roll(x, shift, axis):
    shift %= x.shape[axis]
    return x if shift == 0 else pltpu.roll(x, shift, axis)


def cmul(a, b):
    return a[0] * b[0] - a[1] * b[1], a[0] * b[1] + a[1] * b[0]


def cadd(a, b):
    return a[0] + b[0], a[1] + b[1]


def csub(a, b):
    return a[0] - b[0], a[1] - b[1]


def crecip(a):
    scale = 1.0 / (a[0] * a[0] + a[1] * a[1])
    return a[0] * scale, -a[1] * scale


def lanes8():
    return lax.broadcasted_iota(jnp.int32, (8, LANES), 1)


def lanes8():
    return lax.broadcasted_iota(jnp.int32, (8, LANES), 1)


def block_transpose(turned):
    block = lanes8() // 8
    for bit in (1, 2, 4, 8):
        odd = (block & bit) != 0
        turned = [jnp.where(odd, turned[(j + bit) % 16], turned[j]) for j in range(16)]
    return [roll(turned[-c % 16], -8 * c, 1) for c in range(16)]


def turn(arrays, shift=0):
    return [roll(array, shift + 8 * i, 1) for i, array in enumerate(arrays)]


def pack_kernel(table_hbm, source, labels, out, sides, marks, table, sems):
    copies = [pltpu.make_async_copy(table_hbm, table, sems.at[0])]
    for side in range(2):
        lanes = pl.ds(side * LANES, LANES)
        copies.append(pltpu.make_async_copy(labels.at[:, lanes], marks.at[side], sems.at[1 + side]))
        into = sides.at[side, pl.ds(0, 2 * LANES)]
        copies.append(pltpu.make_async_copy(source.at[:, lanes], into, sems.at[3 + side]))
    for copy in copies:
        copy.start()
    for copy in copies:
        copy.wait()
    for side in range(2):
        lab = marks[side]
        rel = jnp.full(lab.shape, table[0], F32)
        for m in range(1, 8):
            rel = jnp.where(lab == m, table[m], rel)
        sides[side, pl.ds(2 * LANES, LANES), :] = rel

    def load(side, quantity):
        places = [quantity * LANES + half * 64 + x for half in range(2) for x in range(8)]
        return [sides[side, pl.ds(place, 8, stride=8), :] for place in places]

    slot = lanes8() % 8
    first = slot < 4
    pairs, singles = [], []
    for side in range(2):
        arrays = [load(side, quantity) for quantity in range(3)]
        for quantity in range(3):
            for block, part in enumerate(block_transpose(turn(arrays[quantity]))):
                out[pl.ds((16 * side + block) * ROWS + quantity * 8, 8), :] = part
        pair = [jnp.where(first, v, w) for v, w in zip(turn(arrays[0], 2), turn(arrays[1], 6))]
        pairs += block_transpose(pair)
        late = [roll(v, 4, 0) for v in turn(arrays[2], 6)]
        singles += block_transpose([jnp.where(first, v, w) for v, w in zip(turn(arrays[2], 2), late)])
    from_above = (slot & 2) != 0
    for chunk in range(SLABS):
        lower = (chunk + 16) % SLABS if chunk % 16 == 0 else chunk
        upper = (chunk + 1) % SLABS
        out[pl.ds(chunk * ROWS + 24, 8), :] = jnp.where(from_above, pairs[upper], pairs[lower])
        out[pl.ds(chunk * ROWS + 32, 4), :] = jnp.where(from_above, singles[upper], singles[lower])[:4]


def unpack_kernel(arrived, out, sides):
    for side in range(2):
        for c in range(2):
            parts = [arrived[pl.ds((16 * side + b) * 16 + c * 8, 8), :] for b in range(16)]
            for i, part in enumerate(block_transpose(turn(parts))):
                half, x = divmod(i, 8)
                sides[side, pl.ds(c * LANES + half * 64 + x, 8, stride=8), :] = part
        out[:, pl.ds(side * LANES, LANES)] = sides[side]


def lane_ids():
    lane = lax.broadcasted_iota(jnp.int32, (SLABS, LANES), 1)
    return lane >= 64, (lane // 8) % 8, lane % 8


def upper_half(overlap):
    lane = lax.broadcasted_iota(jnp.int32, (SLABS, LANES), 1)
    if overlap:
        lane = (lane + jnp.where(lane % 8 >= 4, 8, LANES - 8)) % LANES
    return lane >= 64


def up(a, h, upper):
    if h >= 2:
        return roll(a, h // 2, 0)
    turned = roll(a, 64, 1)
    return jnp.where(upper, turned, roll(turned, 1, 0))


def down(a, h, upper):
    if h >= 2:
        return roll(a, -(h // 2), 0)
    turned = roll(a, 64, 1)
    return jnp.where(upper, roll(turned, -1, 0), turned)


def both(f, a, h, upper):
    return f(a[0], h, upper), f(a[1], h, upper)


def layer(ref, quantity, r):
    return ref[pl.ds(quantity * 8 + r, SLABS, stride=ROWS), :]


def source_layer(ref, r):
    return layer(ref, 0, r), layer(ref, 1, r)


def overlap_layer(ref, r):
    _, _, y = lane_ids()
    pair = ref[pl.ds(24 + r, SLABS, stride=ROWS), :]
    single = ref[pl.ds(32 + r % 4, SLABS, stride=ROWS), :]
    quantities = []
    for packed, base in ((pair, 0), (pair, 4), (single, 4 * (r // 4))):
        quantities.append(jnp.where(y >= 4, roll(packed, -2 - base, 1), roll(packed, 6 - base, 1)))
    used = (y <= 1) | (y >= 6)
    return quantities[0], quantities[1], jnp.where(used, quantities[2], 1.0)


def inside():
    chunk = lax.axis_index("slab")
    _, _, y = lane_ids()
    below = (y >= 6) & jnp.broadcast_to(chunk > 0, y.shape)
    above = (y <= 1) & jnp.broadcast_to(chunk < SLABS - 1, y.shape)
    return below | above


def put(ref, i, a):
    ref[pl.ds(2 * i * SLABS, SLABS), :] = a[0]
    ref[pl.ds((2 * i + 1) * SLABS, SLABS), :] = a[1]


def get(ref, i):
    return ref[pl.ds(2 * i * SLABS, SLABS), :], ref[pl.ds((2 * i + 1) * SLABS, SLABS), :]


N_FACTORS = 7 + 2 * STEPS + 1


def factorize(relatives, factors, overlap=False):
    upper = upper_half(overlap)
    row = lax.broadcasted_iota(jnp.int32, (SLABS, LANES), 0)
    first = row * 16 + jnp.where(upper, 8, 0)
    pivots = []
    diagonal = None
    for r in range(DEPTH):
        z = first + r
        relative = relatives[r]
        inward = jnp.maximum(jnp.maximum(PML - z, z - (NZ - 1 - PML)), 0)
        fraction = inward.astype(F32) / PML
        diagonal = (
            (2.0 + 4.0 * COUPLE) - WAVE_SHIFT * relative,
            (DAMPING * WAVE_SHIFT) * relative + ABSORB * fraction * fraction,
        )
        if r < DEPTH - 1:
            pivots.append(crecip(diagonal if r == 0 else csub(diagonal, pivots[-1])))
            put(factors, r, pivots[-1])
    to_first = pivots[0]
    first_first = pivots[0]
    for r in range(1, DEPTH - 1):
        reached = cmul(to_first, to_first)
        to_first = cmul(to_first, pivots[r])
        first_first = cadd(first_first, cmul(reached, pivots[r]))
    corner = to_first
    last_last = pivots[-1]
    low = (row == 0) & jnp.logical_not(upper)
    left = tuple(jnp.where(low, 0.0, v) for v in corner)
    high = (row == SLABS - 1) & upper
    next_first = tuple(jnp.where(high, 0.0, v) for v in both(down, first_first, 1, upper))
    d = csub(csub(diagonal, last_last), next_first)
    for step in range(STEPS):
        h = 1 << step
        right = both(down, left, h, upper)
        inverse = crecip(d)
        alpha = cmul(left, both(up, inverse, h, upper))
        gamma = cmul(right, both(down, inverse, h, upper))
        put(factors, 7 + 2 * step, alpha)
        put(factors, 8 + 2 * step, gamma)
        d = csub(csub(d, cmul(alpha, left)), cmul(gamma, right))
        left = cmul(alpha, both(up, left, h, upper))
    put(factors, 7 + 2 * STEPS, crecip(d))


def line_solve(rhs, factors, overlap=False):
    pivots = [get(factors, r) for r in range(DEPTH - 1)]
    gone = [rhs[0]]
    for r in range(1, DEPTH - 1):
        gone.append(cadd(rhs[r], cmul(pivots[r - 1], gone[-1])))
    last = cmul(pivots[-1], gone[-1])
    reach = pivots[0]
    reaches = []
    first = cmul(pivots[0], gone[0])
    for r in range(1, DEPTH - 1):
        reaches.append(reach)
        reach = cmul(reach, pivots[r])
        first = cadd(first, cmul(reach, gone[r]))
    upper = upper_half(overlap)
    row = lax.broadcasted_iota(jnp.int32, (SLABS, LANES), 0)
    high = (row == SLABS - 1) & upper
    low = (row == 0) & jnp.logical_not(upper)
    after = tuple(jnp.where(high, 0.0, v) for v in both(down, first, 1, upper))
    g = cadd(cadd(rhs[DEPTH - 1], last), after)
    for step in range(STEPS):
        h = 1 << step
        from_low = cmul(get(factors, 7 + 2 * step), both(up, g, h, upper))
        from_high = cmul(get(factors, 8 + 2 * step), both(down, g, h, upper))
        g = cadd(g, cadd(from_low, from_high))
    separator = cmul(get(factors, 7 + 2 * STEPS), g)
    before = tuple(jnp.where(low, 0.0, v) for v in both(up, separator, 1, upper))
    field = [None] * DEPTH
    field[DEPTH - 1] = separator
    for r in range(DEPTH - 2, -1, -1):
        lit = cadd(gone[r], before if r == 0 else cmul(reaches[r - 1], before))
        field[r] = cmul(pivots[r], cadd(lit, field[r + 1]))
    return field


def put_edges(main, source, relatives, edges):
    _, x, _ = lane_ids()
    for edge, is_high in zip(edges, (False, True)):
        place_to = 0 if is_high else 7
        near, far = (7, 6) if is_high else (0, 1)
        lines = [([f[c] for f in main], line) for line in (near, far) for c in range(2)]
        lines += [([f[c] for f in source], near) for c in range(2)] + [(relatives, near)]
        for place, (layers, line) in enumerate(lines):
            total = None
            for r in range(DEPTH):
                moved = roll(layers[r], 8 * (place_to - line + r), 1)
                total = moved if r == 0 else jnp.where(x == (place_to + r) % 8, moved, total)
            edge[pl.ds(place * SLABS, SLABS), :] = total


def over_place(c, r):
    n = 8 * c + r
    return n if n < 9 else n + 9


def over_lanes(base, c, r):
    lane = lax.broadcasted_iota(jnp.int32, (SLABS, LANES), 1) % 64
    first = base + over_place(c, r)
    return (lane == (first - 1) % 64) | (lane == (first + 8) % 64)


def put_over_edges(over, edges):
    for edge, is_high in zip(edges, (False, True)):
        turned, base = (-56, 0) if is_high else (56, 56)
        total = jnp.zeros((SLABS, LANES), F32)
        for c in range(2):
            for r in range(DEPTH):
                moved = roll(over[r][c], turned + over_place(c, r), 1)
                total = jnp.where(over_lanes(base, c, r), moved, total)
        edge[...] = total


def within():
    tile = lax.axis_index("tile")
    _, x, _ = lane_ids()
    low = (x < 4) & jnp.broadcast_to(tile > 0, x.shape)
    high = (x >= 4) & jnp.broadcast_to(tile < TILES - 1, x.shape)
    return low | high


def beside(halos, place, r):
    _, x, _ = lane_ids()
    low, high = (ref[pl.ds(place * SLABS, SLABS), :] for ref in halos)
    return roll(jnp.where(x == r, low, high), -8 * r, 1)


def over_beside(low, high, c, r):
    return roll(jnp.where(over_lanes(0, c, r), low, high), -over_place(c, r), 1)


def sum_y(field, over):
    _, _, y = lane_ids()
    return roll(jnp.where(y == 7, over, field), 1, 1) + roll(jnp.where(y == 0, over, field), -1, 1)


def sum_main(main, over, near):
    _, x, _ = lane_ids()
    along_x = jnp.where(x == 0, near, roll(main, 8, 1)) + jnp.where(x == 7, near, roll(main, -8, 1))
    return along_x + sum_y(main, over)


def over_edge():
    _, x, y = lane_ids()
    below = y >= 4
    return x == jnp.where(below, 7, 1), x == jnp.where(below, 6, 0)


def sum_over(main, over):
    at_low, at_high = over_edge()
    along_x = jnp.where(at_low, 0.0, roll(over, 8, 1)) + jnp.where(at_high, 0.0, roll(over, -8, 1))
    return along_x + sum_y(over, main)


def relax(source, spread):
    return tuple(s + COUPLE * t for s, t in zip(source, spread))


def masked(field, keep):
    return [tuple(jnp.where(keep, v, 0.0) for v in f) for f in field]


def put_all(ref, field):
    for r in range(DEPTH):
        put(ref, r, field[r])


def get_all(ref):
    return [get(ref, r) for r in range(DEPTH)]


def first_kernel(arrived, factors, main_out, *edges):
    relatives = [layer(arrived, 2, r) for r in range(DEPTH)]
    source = [source_layer(arrived, r) for r in range(DEPTH)]
    factorize(relatives, factors)
    main = line_solve(source, factors)
    put_all(main_out, main)
    put_edges(main, source, relatives, edges)


def over_kernel(arrived, main_in, over_factors, main_part, over_part, *edges):
    overlap = [overlap_layer(arrived, r) for r in range(DEPTH)]
    factorize([o[2] for o in overlap], over_factors, True)
    over = masked(line_solve([o[:2] for o in overlap], over_factors, True), inside())
    put_over_edges(over, edges)
    for r in range(DEPTH):
        main = get(main_in, r)
        put(main_part, r, relax(source_layer(arrived, r), [sum_main(m, e, 0.0) for m, e in zip(main, over[r])]))
        put(over_part, r, relax(overlap[r][:2], [sum_over(m, e) for m, e in zip(main, over[r])]))


def last_kernel(
    arrived, factors, over_factors, main_in, main_part, over_part, low, high, over_low, over_high,
    out, near_factors, main_mid, over_mid, near_mid,
):
    halos = (low, high)
    keep = within()
    _, x, _ = lane_ids()
    outermost = (x == 0) | (x == 7)
    at_low, at_high = over_edge()
    over_outermost = at_low | at_high
    tile = lax.axis_index("tile")
    cells_low = jnp.where(jnp.broadcast_to(tile > 0, x.shape), over_low[...], 0.0)
    cells_high = jnp.where(jnp.broadcast_to(tile < TILES - 1, x.shape), over_high[...], 0.0)
    factorize([beside(halos, 6, r) for r in range(DEPTH)], near_factors)
    main_rhs, over_rhs, near_rhs = [], [], []
    for r in range(DEPTH):
        main_adds, over_adds, near_sums = [], [], []
        for c in range(2):
            near = jnp.where(keep, beside(halos, c, r), 0.0)
            cells = over_beside(cells_low, cells_high, c, r)
            main_adds.append(jnp.where(outermost, near, 0.0))
            over_adds.append(jnp.where(over_outermost, cells, 0.0))
            main = main_in[pl.ds((2 * r + c) * SLABS, SLABS), :]
            near_sums.append(beside(halos, 2 + c, r) + main + sum_y(near, cells))
        main_rhs.append(relax(get(main_part, r), main_adds))
        over_rhs.append(relax(get(over_part, r), over_adds))
        near_rhs.append(relax((beside(halos, 4, r), beside(halos, 5, r)), near_sums))
    put_all(main_mid, line_solve(main_rhs, factors))
    put_all(over_mid, masked(line_solve(over_rhs, over_factors, True), inside()))
    put_all(near_mid, masked(line_solve(near_rhs, near_factors), keep))
    rhs = []
    for r in range(DEPTH):
        parts = zip(get(main_mid, r), get(over_mid, r), get(near_mid, r))
        rhs.append(relax(source_layer(arrived, r), [sum_main(*part) for part in parts]))
    field = line_solve(rhs, factors)
    for r in range(DEPTH):
        for c in range(2):
            out[pl.ds(c * 8 + r, SLABS, stride=16), :] = field[r][c]


def call(kernel, name, outs, *args, scratch=(), spec=VMEM):
    return pl.pallas_call(
        kernel,
        out_shape=[jax.ShapeDtypeStruct(s, F32) for s in outs],
        in_specs=[spec] * len(args),
        out_specs=[VMEM] * len(outs),
        scratch_shapes=list(scratch),
        compiler_params=pltpu.CompilerParams(vmem_limit_bytes=32 << 20),
        cost_estimate=pl.CostEstimate(flops=2_000_000, bytes_accessed=1_000_000, transcendentals=0),
        name=name,
    )(*args)


FIELD = (DEPTH * 2 * SLABS, LANES)
FACTORS = (N_FACTORS * 2 * SLABS, LANES)
EDGE = (7 * SLABS, LANES)
OVER_EDGE = (SLABS, LANES)

RING_UP = [(i, (i + 1) % TILES) for i in range(TILES)]
RING_DOWN = [(b, a) for a, b in RING_UP]


def exchange(low, high):
    return lax.ppermute(high, "tile", RING_UP), lax.ppermute(low, "tile", RING_DOWN)


def local(source, labels, permittivity):
    rows = source.reshape(2 * 16 * 8, 256)
    marks = labels.reshape(16 * 8, 256)
    inputs = [pltpu.with_memory_space_constraint(v, pltpu.HBM) for v in (permittivity, rows, marks)]
    (packed,) = call(
        pack_kernel, "pack", [(SLABS * ROWS, LANES)], *inputs, spec=HBM,
        scratch=[
            pltpu.VMEM((2, 3 * LANES, LANES), F32),
            pltpu.VMEM((2, LANES, LANES), jnp.int32),
            pltpu.SMEM((8,), F32),
            pltpu.SemaphoreType.DMA((5,)),
        ],
    )
    arrived = lax.all_to_all(packed.reshape(SLABS, ROWS // 4, 4, LANES), "slab", 0, 0).reshape(SLABS * ROWS, LANES)
    factors, main, *edges = call(first_kernel, "first", [FACTORS, FIELD, EDGE, EDGE], arrived)
    halos = exchange(*edges)
    over_factors, main_part, over_part, *edges = call(
        over_kernel, "over", [FACTORS, FIELD, FIELD, OVER_EDGE, OVER_EDGE], arrived, main
    )
    over_halos = exchange(*edges)
    (packed,) = call(
        last_kernel, "last", [(SLABS * 16, LANES)],
        arrived, factors, over_factors, main, main_part, over_part, *halos, *over_halos,
        scratch=[pltpu.VMEM(FACTORS, F32)] + [pltpu.VMEM(FIELD, F32)] * 3,
    )
    arrived = lax.all_to_all(packed.reshape(SLABS, 16, LANES), "slab", 0, 0).reshape(SLABS * 16, LANES)
    (out,) = call(
        unpack_kernel, "unpack", [(2 * 16 * 8, 256)], arrived, scratch=[pltpu.VMEM((2, 2 * LANES, LANES), F32)]
    )
    return out.reshape(2, 16, 8, 256)


def solution(mesh):
    placed = (P("tilt", "slab", "tile", None), P("slab", "tile", "tilt"), P("tilt"))
    return jax.shard_map(
        local,
        mesh=mesh,
        in_specs=placed,
        out_specs=P("tilt", "slab", "tile", None),
        check_vma=False,
    )
```

```python
import jax
import jax.numpy as jnp
from jax import lax
from jax.experimental import pallas as pl
from jax.experimental.pallas import tpu as pltpu
from jax.sharding import PartitionSpec as P

PML = 8
COUPLE = 0.02
WAVE_SHIFT = 0.15
DAMPING = 0.15
ABSORB = 0.5
NZ = 512
SLABS = 32
TILES = 8
LANES = 128
DEPTH = 8
STEPS = 6
F32 = jnp.float32
VMEM = pl.BlockSpec(memory_space=pltpu.VMEM)
HBM = pl.BlockSpec(memory_space=pltpu.HBM)


ROWS = 36


def roll(x, shift, axis):
    shift %= x.shape[axis]
    return x if shift == 0 else pltpu.roll(x, shift, axis)


def cmul(a, b):
    return a[0] * b[0] - a[1] * b[1], a[0] * b[1] + a[1] * b[0]


def cadd(a, b):
    return a[0] + b[0], a[1] + b[1]


def csub(a, b):
    return a[0] - b[0], a[1] - b[1]


def crecip(a):
    scale = 1.0 / (a[0] * a[0] + a[1] * a[1])
    return a[0] * scale, -a[1] * scale


def lanes8():
    return lax.broadcasted_iota(jnp.int32, (8, LANES), 1)


def lanes8():
    return lax.broadcasted_iota(jnp.int32, (8, LANES), 1)


def block_transpose(turned):
    block = lanes8() // 8
    for bit in (1, 2, 4, 8):
        odd = (block & bit) != 0
        turned = [jnp.where(odd, turned[(j + bit) % 16], turned[j]) for j in range(16)]
    return [roll(turned[-c % 16], -8 * c, 1) for c in range(16)]


def turn(arrays, shift=0):
    return [roll(array, shift + 8 * i, 1) for i, array in enumerate(arrays)]


def pack_kernel(table_hbm, source, labels, out, sides, marks, table, sems):
    copies = [pltpu.make_async_copy(table_hbm, table, sems.at[0])]
    for side in range(2):
        lanes = pl.ds(side * LANES, LANES)
        copies.append(pltpu.make_async_copy(labels.at[:, lanes], marks.at[side], sems.at[1 + side]))
        into = sides.at[side, pl.ds(0, 2 * LANES)]
        copies.append(pltpu.make_async_copy(source.at[:, lanes], into, sems.at[3 + side]))
    for copy in copies:
        copy.start()
    for copy in copies:
        copy.wait()
    for side in range(2):
        lab = marks[side]
        rel = jnp.full(lab.shape, table[0], F32)
        for m in range(1, 8):
            rel = jnp.where(lab == m, table[m], rel)
        sides[side, pl.ds(2 * LANES, LANES), :] = rel

    def load(side, quantity):
        places = [quantity * LANES + half * 64 + x for half in range(2) for x in range(8)]
        return [sides[side, pl.ds(place, 8, stride=8), :] for place in places]

    slot = lanes8() % 8
    first = slot < 4
    pairs, singles = [], []
    for side in range(2):
        arrays = [load(side, quantity) for quantity in range(3)]
        for quantity in range(3):
            for block, part in enumerate(block_transpose(turn(arrays[quantity]))):
                out[pl.ds((16 * side + block) * ROWS + quantity * 8, 8), :] = part
        pair = [jnp.where(first, v, w) for v, w in zip(turn(arrays[0], 2), turn(arrays[1], 6))]
        pairs += block_transpose(pair)
        late = [roll(v, 4, 0) for v in turn(arrays[2], 6)]
        singles += block_transpose([jnp.where(first, v, w) for v, w in zip(turn(arrays[2], 2), late)])
    from_above = (slot & 2) != 0
    for chunk in range(SLABS):
        lower = (chunk + 16) % SLABS if chunk % 16 == 0 else chunk
        upper = (chunk + 1) % SLABS
        out[pl.ds(chunk * ROWS + 24, 8), :] = jnp.where(from_above, pairs[upper], pairs[lower])
        out[pl.ds(chunk * ROWS + 32, 4), :] = jnp.where(from_above, singles[upper], singles[lower])[:4]


def unpack_kernel(arrived, out, sides):
    for side in range(2):
        for c in range(2):
            parts = [arrived[pl.ds((16 * side + b) * 16 + c * 8, 8), :] for b in range(16)]
            for i, part in enumerate(block_transpose(turn(parts))):
                half, x = divmod(i, 8)
                sides[side, pl.ds(c * LANES + half * 64 + x, 8, stride=8), :] = part
        out[:, pl.ds(side * LANES, LANES)] = sides[side]


def lane_ids():
    lane = lax.broadcasted_iota(jnp.int32, (SLABS, LANES), 1)
    return lane >= 64, (lane // 8) % 8, lane % 8


def upper_half(overlap):
    lane = lax.broadcasted_iota(jnp.int32, (SLABS, LANES), 1)
    if overlap:
        lane = (lane + jnp.where(lane % 8 >= 4, 8, LANES - 8)) % LANES
    return lane >= 64


def up(a, h, upper):
    if h >= 2:
        return roll(a, h // 2, 0)
    turned = roll(a, 64, 1)
    return jnp.where(upper, turned, roll(turned, 1, 0))


def down(a, h, upper):
    if h >= 2:
        return roll(a, -(h // 2), 0)
    turned = roll(a, 64, 1)
    return jnp.where(upper, roll(turned, -1, 0), turned)


def both(f, a, h, upper):
    return f(a[0], h, upper), f(a[1], h, upper)


def layer(ref, quantity, r):
    return ref[pl.ds(quantity * 8 + r, SLABS, stride=ROWS), :]


def source_layer(ref, r):
    return layer(ref, 0, r), layer(ref, 1, r)


def overlap_layer(ref, r):
    _, _, y = lane_ids()
    pair = ref[pl.ds(24 + r, SLABS, stride=ROWS), :]
    single = ref[pl.ds(32 + r % 4, SLABS, stride=ROWS), :]
    quantities = []
    for packed, base in ((pair, 0), (pair, 4), (single, 4 * (r // 4))):
        quantities.append(jnp.where(y >= 4, roll(packed, -2 - base, 1), roll(packed, 6 - base, 1)))
    used = (y <= 1) | (y >= 6)
    return quantities[0], quantities[1], jnp.where(used, quantities[2], 1.0)


def inside():
    chunk = lax.axis_index("slab")
    _, _, y = lane_ids()
    below = (y >= 6) & jnp.broadcast_to(chunk > 0, y.shape)
    above = (y <= 1) & jnp.broadcast_to(chunk < SLABS - 1, y.shape)
    return below | above


def put(ref, i, a):
    ref[pl.ds(2 * i * SLABS, SLABS), :] = a[0]
    ref[pl.ds((2 * i + 1) * SLABS, SLABS), :] = a[1]


def get(ref, i):
    return ref[pl.ds(2 * i * SLABS, SLABS), :], ref[pl.ds((2 * i + 1) * SLABS, SLABS), :]


N_FACTORS = 7 + 2 * STEPS + 1


def factorize(relatives, factors, overlap=False):
    upper = upper_half(overlap)
    row = lax.broadcasted_iota(jnp.int32, (SLABS, LANES), 0)
    first = row * 16 + jnp.where(upper, 8, 0)
    pivots = []
    diagonal = None
    for r in range(DEPTH):
        z = first + r
        relative = relatives[r]
        inward = jnp.maximum(jnp.maximum(PML - z, z - (NZ - 1 - PML)), 0)
        fraction = inward.astype(F32) / PML
        diagonal = (
            (2.0 + 4.0 * COUPLE) - WAVE_SHIFT * relative,
            (DAMPING * WAVE_SHIFT) * relative + ABSORB * fraction * fraction,
        )
        if r < DEPTH - 1:
            pivots.append(crecip(diagonal if r == 0 else csub(diagonal, pivots[-1])))
            put(factors, r, pivots[-1])
    to_first = pivots[0]
    first_first = pivots[0]
    for r in range(1, DEPTH - 1):
        reached = cmul(to_first, to_first)
        to_first = cmul(to_first, pivots[r])
        first_first = cadd(first_first, cmul(reached, pivots[r]))
    corner = to_first
    last_last = pivots[-1]
    low = (row == 0) & jnp.logical_not(upper)
    left = tuple(jnp.where(low, 0.0, v) for v in corner)
    high = (row == SLABS - 1) & upper
    next_first = tuple(jnp.where(high, 0.0, v) for v in both(down, first_first, 1, upper))
    d = csub(csub(diagonal, last_last), next_first)
    for step in range(STEPS):
        h = 1 << step
        right = both(down, left, h, upper)
        inverse = crecip(d)
        alpha = cmul(left, both(up, inverse, h, upper))
        gamma = cmul(right, both(down, inverse, h, upper))
        put(factors, 7 + 2 * step, alpha)
        put(factors, 8 + 2 * step, gamma)
        d = csub(csub(d, cmul(alpha, left)), cmul(gamma, right))
        left = cmul(alpha, both(up, left, h, upper))
    put(factors, 7 + 2 * STEPS, crecip(d))


def line_solve(rhs, factors, overlap=False):
    pivots = [get(factors, r) for r in range(DEPTH - 1)]
    gone = [rhs[0]]
    for r in range(1, DEPTH - 1):
        gone.append(cadd(rhs[r], cmul(pivots[r - 1], gone[-1])))
    last = cmul(pivots[-1], gone[-1])
    reach = pivots[0]
    reaches = []
    first = cmul(pivots[0], gone[0])
    for r in range(1, DEPTH - 1):
        reaches.append(reach)
        reach = cmul(reach, pivots[r])
        first = cadd(first, cmul(reach, gone[r]))
    upper = upper_half(overlap)
    row = lax.broadcasted_iota(jnp.int32, (SLABS, LANES), 0)
    high = (row == SLABS - 1) & upper
    low = (row == 0) & jnp.logical_not(upper)
    after = tuple(jnp.where(high, 0.0, v) for v in both(down, first, 1, upper))
    g = cadd(cadd(rhs[DEPTH - 1], last), after)
    for step in range(STEPS):
        h = 1 << step
        from_low = cmul(get(factors, 7 + 2 * step), both(up, g, h, upper))
        from_high = cmul(get(factors, 8 + 2 * step), both(down, g, h, upper))
        g = cadd(g, cadd(from_low, from_high))
    separator = cmul(get(factors, 7 + 2 * STEPS), g)
    before = tuple(jnp.where(low, 0.0, v) for v in both(up, separator, 1, upper))
    field = [None] * DEPTH
    field[DEPTH - 1] = separator
    for r in range(DEPTH - 2, -1, -1):
        lit = cadd(gone[r], before if r == 0 else cmul(reaches[r - 1], before))
        field[r] = cmul(pivots[r], cadd(lit, field[r + 1]))
    return field


def put_edges(main, source, relatives, edges):
    _, x, _ = lane_ids()
    for edge, is_high in zip(edges, (False, True)):
        place_to = 0 if is_high else 7
        near, far = (7, 6) if is_high else (0, 1)
        lines = [([f[c] for f in main], line) for line in (near, far) for c in range(2)]
        lines += [([f[c] for f in source], near) for c in range(2)] + [(relatives, near)]
        for place, (layers, line) in enumerate(lines):
            total = None
            for r in range(DEPTH):
                moved = roll(layers[r], 8 * (place_to - line + r), 1)
                total = moved if r == 0 else jnp.where(x == (place_to + r) % 8, moved, total)
            edge[pl.ds(place * SLABS, SLABS), :] = total


def over_place(c, r):
    n = 8 * c + r
    return n if n < 9 else n + 9


def over_lanes(base, c, r):
    lane = lax.broadcasted_iota(jnp.int32, (SLABS, LANES), 1) % 64
    first = base + over_place(c, r)
    return (lane == (first - 1) % 64) | (lane == (first + 8) % 64)


def put_over_edges(over, edges):
    for edge, is_high in zip(edges, (False, True)):
        turned, base = (-56, 0) if is_high else (56, 56)
        total = jnp.zeros((SLABS, LANES), F32)
        for c in range(2):
            for r in range(DEPTH):
                moved = roll(over[r][c], turned + over_place(c, r), 1)
                total = jnp.where(over_lanes(base, c, r), moved, total)
        edge[pl.ds(7 * SLABS, SLABS), :] = total


def within():
    tile = lax.axis_index("tile")
    _, x, _ = lane_ids()
    low = (x < 4) & jnp.broadcast_to(tile > 0, x.shape)
    high = (x >= 4) & jnp.broadcast_to(tile < TILES - 1, x.shape)
    return low | high


def beside(halos, place, r):
    _, x, _ = lane_ids()
    low, high = (ref[pl.ds(place * SLABS, SLABS), :] for ref in halos)
    return roll(jnp.where(x == r, low, high), -8 * r, 1)


def over_beside(low, high, c, r):
    return roll(jnp.where(over_lanes(0, c, r), low, high), -over_place(c, r), 1)


def sum_y(field, over):
    _, _, y = lane_ids()
    return roll(jnp.where(y == 7, over, field), 1, 1) + roll(jnp.where(y == 0, over, field), -1, 1)


def sum_main(main, over, near):
    _, x, _ = lane_ids()
    along_x = jnp.where(x == 0, near, roll(main, 8, 1)) + jnp.where(x == 7, near, roll(main, -8, 1))
    return along_x + sum_y(main, over)


def over_edge():
    _, x, y = lane_ids()
    below = y >= 4
    return x == jnp.where(below, 7, 1), x == jnp.where(below, 6, 0)


def sum_over(main, over):
    at_low, at_high = over_edge()
    along_x = jnp.where(at_low, 0.0, roll(over, 8, 1)) + jnp.where(at_high, 0.0, roll(over, -8, 1))
    return along_x + sum_y(over, main)


def relax(source, spread):
    return tuple(s + COUPLE * t for s, t in zip(source, spread))


def masked(field, keep):
    return [tuple(jnp.where(keep, v, 0.0) for v in f) for f in field]


def put_all(ref, field):
    for r in range(DEPTH):
        put(ref, r, field[r])


def get_all(ref):
    return [get(ref, r) for r in range(DEPTH)]


def first_kernel(arrived, factors, over_factors, over_source, main_out, over_out, *edges):
    relatives = [layer(arrived, 2, r) for r in range(DEPTH)]
    source = [source_layer(arrived, r) for r in range(DEPTH)]
    factorize(relatives, factors)
    main = line_solve(source, factors)
    put_all(main_out, main)
    put_edges(main, source, relatives, edges)
    overlap = [overlap_layer(arrived, r) for r in range(DEPTH)]
    put_all(over_source, [o[:2] for o in overlap])
    factorize([o[2] for o in overlap], over_factors, True)
    over = masked(line_solve([o[:2] for o in overlap], over_factors, True), inside())
    put_all(over_out, over)
    put_over_edges(over, edges)


def own_kernel(arrived, over_source, main_in, over_in, main_part, over_part):
    for r in range(DEPTH):
        main, over = get(main_in, r), get(over_in, r)
        put(main_part, r, relax(source_layer(arrived, r), [sum_main(m, e, 0.0) for m, e in zip(main, over)]))
        put(over_part, r, relax(get(over_source, r), [sum_over(m, e) for m, e in zip(main, over)]))


def last_kernel(
    arrived, factors, over_factors, main_in, main_part, over_part, low, high,
    out, near_factors, main_mid, over_mid, near_mid,
):
    halos = (low, high)
    keep = within()
    _, x, _ = lane_ids()
    outermost = (x == 0) | (x == 7)
    at_low, at_high = over_edge()
    over_outermost = at_low | at_high
    tile = lax.axis_index("tile")
    cells_low = jnp.where(jnp.broadcast_to(tile > 0, x.shape), low[pl.ds(7 * SLABS, SLABS), :], 0.0)
    cells_high = jnp.where(jnp.broadcast_to(tile < TILES - 1, x.shape), high[pl.ds(7 * SLABS, SLABS), :], 0.0)
    factorize([beside(halos, 6, r) for r in range(DEPTH)], near_factors)
    main_rhs, over_rhs, near_rhs = [], [], []
    for r in range(DEPTH):
        main_adds, over_adds, near_sums = [], [], []
        for c in range(2):
            near = jnp.where(keep, beside(halos, c, r), 0.0)
            cells = over_beside(cells_low, cells_high, c, r)
            main_adds.append(jnp.where(outermost, near, 0.0))
            over_adds.append(jnp.where(over_outermost, cells, 0.0))
            main = main_in[pl.ds((2 * r + c) * SLABS, SLABS), :]
            near_sums.append(beside(halos, 2 + c, r) + main + sum_y(near, cells))
        main_rhs.append(relax(get(main_part, r), main_adds))
        over_rhs.append(relax(get(over_part, r), over_adds))
        near_rhs.append(relax((beside(halos, 4, r), beside(halos, 5, r)), near_sums))
    put_all(main_mid, line_solve(main_rhs, factors))
    put_all(over_mid, masked(line_solve(over_rhs, over_factors, True), inside()))
    put_all(near_mid, masked(line_solve(near_rhs, near_factors), keep))
    rhs = []
    for r in range(DEPTH):
        parts = zip(get(main_mid, r), get(over_mid, r), get(near_mid, r))
        rhs.append(relax(source_layer(arrived, r), [sum_main(*part) for part in parts]))
    field = line_solve(rhs, factors)
    for r in range(DEPTH):
        for c in range(2):
            out[pl.ds(c * 8 + r, SLABS, stride=16), :] = field[r][c]


def call(kernel, name, outs, *args, scratch=(), spec=VMEM):
    return pl.pallas_call(
        kernel,
        out_shape=[jax.ShapeDtypeStruct(s, F32) for s in outs],
        in_specs=[spec] * len(args),
        out_specs=[VMEM] * len(outs),
        scratch_shapes=list(scratch),
        compiler_params=pltpu.CompilerParams(vmem_limit_bytes=32 << 20),
        cost_estimate=pl.CostEstimate(flops=2_000_000, bytes_accessed=1_000_000, transcendentals=0),
        name=name,
    )(*args)


FIELD = (DEPTH * 2 * SLABS, LANES)
FACTORS = (N_FACTORS * 2 * SLABS, LANES)
EDGE = (8 * SLABS, LANES)

RING_UP = [(i, (i + 1) % TILES) for i in range(TILES)]
RING_DOWN = [(b, a) for a, b in RING_UP]


def exchange(low, high):
    return lax.ppermute(high, "tile", RING_UP), lax.ppermute(low, "tile", RING_DOWN)


def local(source, labels, permittivity):
    rows = source.reshape(2 * 16 * 8, 256)
    marks = labels.reshape(16 * 8, 256)
    inputs = [pltpu.with_memory_space_constraint(v, pltpu.HBM) for v in (permittivity, rows, marks)]
    (packed,) = call(
        pack_kernel, "pack", [(SLABS * ROWS, LANES)], *inputs, spec=HBM,
        scratch=[
            pltpu.VMEM((2, 3 * LANES, LANES), F32),
            pltpu.VMEM((2, LANES, LANES), jnp.int32),
            pltpu.SMEM((8,), F32),
            pltpu.SemaphoreType.DMA((5,)),
        ],
    )
    arrived = lax.all_to_all(packed.reshape(SLABS, ROWS // 4, 4, LANES), "slab", 0, 0).reshape(SLABS * ROWS, LANES)
    factors, over_factors, over_source, main, over, *edges = call(
        first_kernel, "first", [FACTORS, FACTORS, FIELD, FIELD, FIELD, EDGE, EDGE], arrived
    )
    halos = exchange(*edges)
    main_part, over_part = call(own_kernel, "own", [FIELD, FIELD], arrived, over_source, main, over)
    (packed,) = call(
        last_kernel, "last", [(SLABS * 16, LANES)],
        arrived, factors, over_factors, main, main_part, over_part, *halos,
        scratch=[pltpu.VMEM(FACTORS, F32)] + [pltpu.VMEM(FIELD, F32)] * 3,
    )
    arrived = lax.all_to_all(packed.reshape(SLABS, 16, LANES), "slab", 0, 0).reshape(SLABS * 16, LANES)
    (out,) = call(
        unpack_kernel, "unpack", [(2 * 16 * 8, 256)], arrived, scratch=[pltpu.VMEM((2, 2 * LANES, LANES), F32)]
    )
    return out.reshape(2, 16, 8, 256)


def solution(mesh):
    placed = (P("tilt", "slab", "tile", None), P("slab", "tile", "tilt"), P("tilt"))
    return jax.shard_map(
        local,
        mesh=mesh,
        in_specs=placed,
        out_specs=P("tilt", "slab", "tile", None),
        check_vma=False,
    )
```

```python
import jax
import jax.numpy as jnp
from jax import lax
from jax.experimental import pallas as pl
from jax.experimental.pallas import tpu as pltpu
from jax.sharding import PartitionSpec as P

PML = 8
COUPLE = 0.02
WAVE_SHIFT = 0.15
DAMPING = 0.15
ABSORB = 0.5
NZ = 512
SLABS = 32
TILES = 8
LANES = 128
DEPTH = 8
STEPS = 6
F32 = jnp.float32
VMEM = pl.BlockSpec(memory_space=pltpu.VMEM)
HBM = pl.BlockSpec(memory_space=pltpu.HBM)


ROWS = 36


def roll(x, shift, axis):
    shift %= x.shape[axis]
    return x if shift == 0 else pltpu.roll(x, shift, axis)


def cmul(a, b):
    return a[0] * b[0] - a[1] * b[1], a[0] * b[1] + a[1] * b[0]


def cadd(a, b):
    return a[0] + b[0], a[1] + b[1]


def csub(a, b):
    return a[0] - b[0], a[1] - b[1]


def crecip(a):
    scale = 1.0 / (a[0] * a[0] + a[1] * a[1])
    return a[0] * scale, -a[1] * scale


def lanes8():
    return lax.broadcasted_iota(jnp.int32, (8, LANES), 1)


def lanes8():
    return lax.broadcasted_iota(jnp.int32, (8, LANES), 1)


def block_transpose(turned):
    block = lanes8() // 8
    for bit in (1, 2, 4, 8):
        odd = (block & bit) != 0
        turned = [jnp.where(odd, turned[(j + bit) % 16], turned[j]) for j in range(16)]
    return [roll(turned[-c % 16], -8 * c, 1) for c in range(16)]


def turn(arrays, shift=0):
    return [roll(array, shift + 8 * i, 1) for i, array in enumerate(arrays)]


def pack_kernel(table_hbm, source, labels, out, sides, marks, table, sems):
    copies = [pltpu.make_async_copy(table_hbm, table, sems.at[0])]
    for side in range(2):
        lanes = pl.ds(side * LANES, LANES)
        copies.append(pltpu.make_async_copy(labels.at[:, lanes], marks.at[side], sems.at[1 + side]))
        into = sides.at[side, pl.ds(0, 2 * LANES)]
        copies.append(pltpu.make_async_copy(source.at[:, lanes], into, sems.at[3 + side]))
    for copy in copies:
        copy.start()
    for copy in copies:
        copy.wait()
    for side in range(2):
        lab = marks[side]
        rel = jnp.full(lab.shape, table[0], F32)
        for m in range(1, 8):
            rel = jnp.where(lab == m, table[m], rel)
        sides[side, pl.ds(2 * LANES, LANES), :] = rel

    def load(side, quantity):
        places = [quantity * LANES + half * 64 + x for half in range(2) for x in range(8)]
        return [sides[side, pl.ds(place, 8, stride=8), :] for place in places]

    slot = lanes8() % 8
    first = slot < 4
    pairs, singles = [], []
    for side in range(2):
        arrays = [load(side, quantity) for quantity in range(3)]
        for quantity in range(3):
            for block, part in enumerate(block_transpose(turn(arrays[quantity]))):
                out[pl.ds((16 * side + block) * ROWS + quantity * 8, 8), :] = part
        pair = [jnp.where(first, v, w) for v, w in zip(turn(arrays[0], 2), turn(arrays[1], 6))]
        pairs += block_transpose(pair)
        late = [roll(v, 4, 0) for v in turn(arrays[2], 6)]
        singles += block_transpose([jnp.where(first, v, w) for v, w in zip(turn(arrays[2], 2), late)])
    from_above = (slot & 2) != 0
    for chunk in range(SLABS):
        lower = (chunk + 16) % SLABS if chunk % 16 == 0 else chunk
        upper = (chunk + 1) % SLABS
        out[pl.ds(chunk * ROWS + 24, 8), :] = jnp.where(from_above, pairs[upper], pairs[lower])
        out[pl.ds(chunk * ROWS + 32, 4), :] = jnp.where(from_above, singles[upper], singles[lower])[:4]


def unpack_kernel(arrived, out, sides):
    for side in range(2):
        for c in range(2):
            parts = [arrived[pl.ds((16 * side + b) * 16 + c * 8, 8), :] for b in range(16)]
            for i, part in enumerate(block_transpose(turn(parts))):
                half, x = divmod(i, 8)
                sides[side, pl.ds(c * LANES + half * 64 + x, 8, stride=8), :] = part
        out[:, pl.ds(side * LANES, LANES)] = sides[side]


def lane_ids():
    lane = lax.broadcasted_iota(jnp.int32, (SLABS, LANES), 1)
    return lane >= 64, (lane // 8) % 8, lane % 8


def upper_half(overlap):
    lane = lax.broadcasted_iota(jnp.int32, (SLABS, LANES), 1)
    if overlap:
        lane = (lane + jnp.where(lane % 8 >= 4, 8, LANES - 8)) % LANES
    return lane >= 64


def up(a, h, upper):
    if h >= 2:
        return roll(a, h // 2, 0)
    turned = roll(a, 64, 1)
    return jnp.where(upper, turned, roll(turned, 1, 0))


def down(a, h, upper):
    if h >= 2:
        return roll(a, -(h // 2), 0)
    turned = roll(a, 64, 1)
    return jnp.where(upper, roll(turned, -1, 0), turned)


def both(f, a, h, upper):
    return f(a[0], h, upper), f(a[1], h, upper)


def layer(ref, quantity, r):
    return ref[pl.ds(quantity * 8 + r, SLABS, stride=ROWS), :]


def source_layer(ref, r):
    return layer(ref, 0, r), layer(ref, 1, r)


def overlap_layer(ref, r):
    _, _, y = lane_ids()
    pair = ref[pl.ds(24 + r, SLABS, stride=ROWS), :]
    single = ref[pl.ds(32 + r % 4, SLABS, stride=ROWS), :]
    quantities = []
    for packed, base in ((pair, 0), (pair, 4), (single, 4 * (r // 4))):
        quantities.append(jnp.where(y >= 4, roll(packed, -2 - base, 1), roll(packed, 6 - base, 1)))
    used = (y <= 1) | (y >= 6)
    return quantities[0], quantities[1], jnp.where(used, quantities[2], 1.0)


def inside():
    chunk = lax.axis_index("slab")
    _, _, y = lane_ids()
    below = (y >= 6) & jnp.broadcast_to(chunk > 0, y.shape)
    above = (y <= 1) & jnp.broadcast_to(chunk < SLABS - 1, y.shape)
    return below | above


def put(ref, i, a):
    ref[pl.ds(2 * i * SLABS, SLABS), :] = a[0]
    ref[pl.ds((2 * i + 1) * SLABS, SLABS), :] = a[1]


def get(ref, i):
    return ref[pl.ds(2 * i * SLABS, SLABS), :], ref[pl.ds((2 * i + 1) * SLABS, SLABS), :]


N_FACTORS = 7 + 2 * STEPS + 1


def factorize(relatives, factors, overlap=False):
    upper = upper_half(overlap)
    row = lax.broadcasted_iota(jnp.int32, (SLABS, LANES), 0)
    first = row * 16 + jnp.where(upper, 8, 0)
    pivots = []
    diagonal = None
    for r in range(DEPTH):
        z = first + r
        relative = relatives[r]
        inward = jnp.maximum(jnp.maximum(PML - z, z - (NZ - 1 - PML)), 0)
        fraction = inward.astype(F32) / PML
        diagonal = (
            (2.0 + 4.0 * COUPLE) - WAVE_SHIFT * relative,
            (DAMPING * WAVE_SHIFT) * relative + ABSORB * fraction * fraction,
        )
        if r < DEPTH - 1:
            pivots.append(crecip(diagonal if r == 0 else csub(diagonal, pivots[-1])))
            put(factors, r, pivots[-1])
    to_first = pivots[0]
    first_first = pivots[0]
    for r in range(1, DEPTH - 1):
        reached = cmul(to_first, to_first)
        to_first = cmul(to_first, pivots[r])
        first_first = cadd(first_first, cmul(reached, pivots[r]))
    corner = to_first
    last_last = pivots[-1]
    low = (row == 0) & jnp.logical_not(upper)
    left = tuple(jnp.where(low, 0.0, v) for v in corner)
    high = (row == SLABS - 1) & upper
    next_first = tuple(jnp.where(high, 0.0, v) for v in both(down, first_first, 1, upper))
    d = csub(csub(diagonal, last_last), next_first)
    for step in range(STEPS):
        h = 1 << step
        right = both(down, left, h, upper)
        inverse = crecip(d)
        alpha = cmul(left, both(up, inverse, h, upper))
        gamma = cmul(right, both(down, inverse, h, upper))
        put(factors, 7 + 2 * step, alpha)
        put(factors, 8 + 2 * step, gamma)
        d = csub(csub(d, cmul(alpha, left)), cmul(gamma, right))
        left = cmul(alpha, both(up, left, h, upper))
    put(factors, 7 + 2 * STEPS, crecip(d))


def line_solve(rhs, factors, overlap=False):
    pivots = [get(factors, r) for r in range(DEPTH - 1)]
    gone = [rhs[0]]
    for r in range(1, DEPTH - 1):
        gone.append(cadd(rhs[r], cmul(pivots[r - 1], gone[-1])))
    last = cmul(pivots[-1], gone[-1])
    reach = pivots[0]
    reaches = []
    first = cmul(pivots[0], gone[0])
    for r in range(1, DEPTH - 1):
        reaches.append(reach)
        reach = cmul(reach, pivots[r])
        first = cadd(first, cmul(reach, gone[r]))
    upper = upper_half(overlap)
    row = lax.broadcasted_iota(jnp.int32, (SLABS, LANES), 0)
    high = (row == SLABS - 1) & upper
    low = (row == 0) & jnp.logical_not(upper)
    after = tuple(jnp.where(high, 0.0, v) for v in both(down, first, 1, upper))
    g = cadd(cadd(rhs[DEPTH - 1], last), after)
    for step in range(STEPS):
        h = 1 << step
        from_low = cmul(get(factors, 7 + 2 * step), both(up, g, h, upper))
        from_high = cmul(get(factors, 8 + 2 * step), both(down, g, h, upper))
        g = cadd(g, cadd(from_low, from_high))
    separator = cmul(get(factors, 7 + 2 * STEPS), g)
    before = tuple(jnp.where(low, 0.0, v) for v in both(up, separator, 1, upper))
    field = [None] * DEPTH
    field[DEPTH - 1] = separator
    for r in range(DEPTH - 2, -1, -1):
        lit = cadd(gone[r], before if r == 0 else cmul(reaches[r - 1], before))
        field[r] = cmul(pivots[r], cadd(lit, field[r + 1]))
    return field


def put_edges(main, part, relatives, edges):
    _, x, _ = lane_ids()
    for edge, is_high in zip(edges, (False, True)):
        place_to, turned = (0, -56) if is_high else (7, 56)
        arrays = [[f[c] for f in main] for c in range(2)] + [[f[c] for f in part] for c in range(2)] + [relatives]
        for place, layers in enumerate(arrays):
            total = None
            for r in range(DEPTH):
                moved = roll(layers[r], turned + 8 * r, 1)
                total = moved if r == 0 else jnp.where(x == (place_to + r) % 8, moved, total)
            edge[pl.ds(place * SLABS, SLABS), :] = total


def over_place(c, r):
    n = 8 * c + r
    return n if n < 9 else n + 9


def over_lanes(base, c, r):
    lane = lax.broadcasted_iota(jnp.int32, (SLABS, LANES), 1) % 64
    first = base + over_place(c, r)
    return (lane == (first - 1) % 64) | (lane == (first + 8) % 64)


def put_over_edges(over, edges):
    for edge, is_high in zip(edges, (False, True)):
        turned, base = (-56, 0) if is_high else (56, 56)
        total = jnp.zeros((SLABS, LANES), F32)
        for c in range(2):
            for r in range(DEPTH):
                moved = roll(over[r][c], turned + over_place(c, r), 1)
                total = jnp.where(over_lanes(base, c, r), moved, total)
        edge[pl.ds(5 * SLABS, SLABS), :] = total


def within():
    tile = lax.axis_index("tile")
    _, x, _ = lane_ids()
    low = (x < 4) & jnp.broadcast_to(tile > 0, x.shape)
    high = (x >= 4) & jnp.broadcast_to(tile < TILES - 1, x.shape)
    return low | high


def beside(halos, place, r):
    _, x, _ = lane_ids()
    low, high = (ref[pl.ds(place * SLABS, SLABS), :] for ref in halos)
    return roll(jnp.where(x == r, low, high), -8 * r, 1)


def over_beside(low, high, c, r):
    return roll(jnp.where(over_lanes(0, c, r), low, high), -over_place(c, r), 1)


def sum_y(field, over):
    _, _, y = lane_ids()
    return roll(jnp.where(y == 7, over, field), 1, 1) + roll(jnp.where(y == 0, over, field), -1, 1)


def sum_main(main, over, near):
    _, x, _ = lane_ids()
    along_x = jnp.where(x == 0, near, roll(main, 8, 1)) + jnp.where(x == 7, near, roll(main, -8, 1))
    return along_x + sum_y(main, over)


def over_edge():
    _, x, y = lane_ids()
    below = y >= 4
    return x == jnp.where(below, 7, 1), x == jnp.where(below, 6, 0)


def sum_over(main, over):
    at_low, at_high = over_edge()
    along_x = jnp.where(at_low, 0.0, roll(over, 8, 1)) + jnp.where(at_high, 0.0, roll(over, -8, 1))
    return along_x + sum_y(over, main)


def relax(source, spread):
    return tuple(s + COUPLE * t for s, t in zip(source, spread))


def masked(field, keep):
    return [tuple(jnp.where(keep, v, 0.0) for v in f) for f in field]


def put_all(ref, field):
    for r in range(DEPTH):
        put(ref, r, field[r])


def get_all(ref):
    return [get(ref, r) for r in range(DEPTH)]


def first_kernel(arrived, factors, over_factors, over_source, main_out, over_out, main_part, *edges):
    overlap = [overlap_layer(arrived, r) for r in range(DEPTH)]
    put_all(over_source, [o[:2] for o in overlap])
    factorize([o[2] for o in overlap], over_factors, True)
    over = masked(line_solve([o[:2] for o in overlap], over_factors, True), inside())
    put_all(over_out, over)
    put_over_edges(over, edges)
    relatives = [layer(arrived, 2, r) for r in range(DEPTH)]
    source = [source_layer(arrived, r) for r in range(DEPTH)]
    factorize(relatives, factors)
    main = line_solve(source, factors)
    put_all(main_out, main)
    part = [relax(source[r], [sum_main(m, e, 0.0) for m, e in zip(main[r], get(over_out, r))]) for r in range(DEPTH)]
    put_all(main_part, part)
    put_edges(main, part, relatives, edges)


def own_kernel(over_source, main_in, over_in, over_part):
    for r in range(DEPTH):
        put(over_part, r, relax(get(over_source, r), [sum_over(m, e) for m, e in zip(get(main_in, r), get(over_in, r))]))


def last_kernel(
    arrived, factors, over_factors, main_in, main_part, over_part, low, high,
    out, near_factors, main_mid, over_mid, near_mid,
):
    halos = (low, high)
    keep = within()
    _, x, _ = lane_ids()
    outermost = (x == 0) | (x == 7)
    at_low, at_high = over_edge()
    over_outermost = at_low | at_high
    tile = lax.axis_index("tile")
    cells_low = jnp.where(jnp.broadcast_to(tile > 0, x.shape), low[pl.ds(5 * SLABS, SLABS), :], 0.0)
    cells_high = jnp.where(jnp.broadcast_to(tile < TILES - 1, x.shape), high[pl.ds(5 * SLABS, SLABS), :], 0.0)
    factorize([beside(halos, 4, r) for r in range(DEPTH)], near_factors)
    main_rhs, over_rhs, near_rhs = [], [], []
    for r in range(DEPTH):
        main_adds, over_adds = [], []
        for c in range(2):
            near = jnp.where(keep, beside(halos, c, r), 0.0)
            main_adds.append(jnp.where(outermost, near, 0.0))
            over_adds.append(jnp.where(over_outermost, over_beside(cells_low, cells_high, c, r), 0.0))
        main_rhs.append(relax(get(main_part, r), main_adds))
        over_rhs.append(relax(get(over_part, r), over_adds))
        near_rhs.append(relax((beside(halos, 2, r), beside(halos, 3, r)), get(main_in, r)))
    put_all(main_mid, line_solve(main_rhs, factors))
    put_all(over_mid, masked(line_solve(over_rhs, over_factors, True), inside()))
    put_all(near_mid, masked(line_solve(near_rhs, near_factors), keep))
    rhs = []
    for r in range(DEPTH):
        parts = zip(get(main_mid, r), get(over_mid, r), get(near_mid, r))
        rhs.append(relax(source_layer(arrived, r), [sum_main(*part) for part in parts]))
    field = line_solve(rhs, factors)
    for r in range(DEPTH):
        for c in range(2):
            out[pl.ds(c * 8 + r, SLABS, stride=16), :] = field[r][c]


def call(kernel, name, outs, *args, scratch=(), spec=VMEM):
    return pl.pallas_call(
        kernel,
        out_shape=[jax.ShapeDtypeStruct(s, F32) for s in outs],
        in_specs=[spec] * len(args),
        out_specs=[VMEM] * len(outs),
        scratch_shapes=list(scratch),
        compiler_params=pltpu.CompilerParams(vmem_limit_bytes=32 << 20),
        cost_estimate=pl.CostEstimate(flops=2_000_000, bytes_accessed=1_000_000, transcendentals=0),
        name=name,
    )(*args)


FIELD = (DEPTH * 2 * SLABS, LANES)
FACTORS = (N_FACTORS * 2 * SLABS, LANES)
EDGE = (6 * SLABS, LANES)

RING_UP = [(i, (i + 1) % TILES) for i in range(TILES)]
RING_DOWN = [(b, a) for a, b in RING_UP]


def exchange(low, high):
    return lax.ppermute(high, "tile", RING_UP), lax.ppermute(low, "tile", RING_DOWN)


def local(source, labels, permittivity):
    rows = source.reshape(2 * 16 * 8, 256)
    marks = labels.reshape(16 * 8, 256)
    inputs = [pltpu.with_memory_space_constraint(v, pltpu.HBM) for v in (permittivity, rows, marks)]
    (packed,) = call(
        pack_kernel, "pack", [(SLABS * ROWS, LANES)], *inputs, spec=HBM,
        scratch=[
            pltpu.VMEM((2, 3 * LANES, LANES), F32),
            pltpu.VMEM((2, LANES, LANES), jnp.int32),
            pltpu.SMEM((8,), F32),
            pltpu.SemaphoreType.DMA((5,)),
        ],
    )
    arrived = lax.all_to_all(packed.reshape(SLABS, ROWS // 4, 4, LANES), "slab", 0, 0).reshape(SLABS * ROWS, LANES)
    factors, over_factors, over_source, main, over, main_part, *edges = call(
        first_kernel, "first", [FACTORS, FACTORS, FIELD, FIELD, FIELD, FIELD, EDGE, EDGE], arrived
    )
    halos = exchange(*edges)
    (over_part,) = call(own_kernel, "own", [FIELD], over_source, main, over)
    (packed,) = call(
        last_kernel, "last", [(SLABS * 16, LANES)],
        arrived, factors, over_factors, main, main_part, over_part, *halos,
        scratch=[pltpu.VMEM(FACTORS, F32)] + [pltpu.VMEM(FIELD, F32)] * 3,
    )
    arrived = lax.all_to_all(packed.reshape(SLABS, 16, LANES), "slab", 0, 0).reshape(SLABS * 16, LANES)
    (out,) = call(
        unpack_kernel, "unpack", [(2 * 16 * 8, 256)], arrived, scratch=[pltpu.VMEM((2, 2 * LANES, LANES), F32)]
    )
    return out.reshape(2, 16, 8, 256)


def solution(mesh):
    placed = (P("tilt", "slab", "tile", None), P("slab", "tile", "tilt"), P("tilt"))
    return jax.shard_map(
        local,
        mesh=mesh,
        in_specs=placed,
        out_specs=P("tilt", "slab", "tile", None),
        check_vma=False,
    )
```

```python
import jax
import jax.numpy as jnp
from jax import lax
from jax.experimental import pallas as pl
from jax.experimental.pallas import tpu as pltpu
from jax.sharding import PartitionSpec as P

PML = 8
COUPLE = 0.02
WAVE_SHIFT = 0.15
DAMPING = 0.15
ABSORB = 0.5
NZ = 512
SLABS = 32
TILES = 8
LANES = 128
DEPTH = 8
STEPS = 6
F32 = jnp.float32
VMEM = pl.BlockSpec(memory_space=pltpu.VMEM)
HBM = pl.BlockSpec(memory_space=pltpu.HBM)


ROWS = 36


def roll(x, shift, axis):
    shift %= x.shape[axis]
    return x if shift == 0 else pltpu.roll(x, shift, axis)


def cmul(a, b):
    return a[0] * b[0] - a[1] * b[1], a[0] * b[1] + a[1] * b[0]


def cadd(a, b):
    return a[0] + b[0], a[1] + b[1]


def csub(a, b):
    return a[0] - b[0], a[1] - b[1]


def crecip(a):
    scale = 1.0 / (a[0] * a[0] + a[1] * a[1])
    return a[0] * scale, -a[1] * scale


def lanes8():
    return lax.broadcasted_iota(jnp.int32, (8, LANES), 1)


def lanes8():
    return lax.broadcasted_iota(jnp.int32, (8, LANES), 1)


def block_transpose(turned):
    block = lanes8() // 8
    for bit in (1, 2, 4, 8):
        odd = (block & bit) != 0
        turned = [jnp.where(odd, turned[(j + bit) % 16], turned[j]) for j in range(16)]
    return [roll(turned[-c % 16], -8 * c, 1) for c in range(16)]


def turn(arrays, shift=0):
    return [roll(array, shift + 8 * i, 1) for i, array in enumerate(arrays)]


def pack_kernel(table_hbm, source, labels, out, sides, marks, table, sems):
    copies = [pltpu.make_async_copy(table_hbm, table, sems.at[0])]
    for side in range(2):
        lanes = pl.ds(side * LANES, LANES)
        copies.append(pltpu.make_async_copy(labels.at[:, lanes], marks.at[side], sems.at[1 + side]))
    for side in range(2):
        lanes = pl.ds(side * LANES, LANES)
        into = sides.at[side, pl.ds(0, 2 * LANES)]
        copies.append(pltpu.make_async_copy(source.at[:, lanes], into, sems.at[3 + side]))
    for copy in copies:
        copy.start()
    for copy in copies[:3]:
        copy.wait()
    for side in range(2):
        lab = marks[side]
        rel = jnp.full(lab.shape, table[0], F32)
        for m in range(1, 8):
            rel = jnp.where(lab == m, table[m], rel)
        sides[side, pl.ds(2 * LANES, LANES), :] = rel
    for copy in copies[3:]:
        copy.wait()

    def load(side, quantity):
        places = [quantity * LANES + half * 64 + x for half in range(2) for x in range(8)]
        return [sides[side, pl.ds(place, 8, stride=8), :] for place in places]

    slot = lanes8() % 8
    first = slot < 4
    pairs, singles = [], []
    for side in range(2):
        arrays = [load(side, quantity) for quantity in range(3)]
        for quantity in range(3):
            for block, part in enumerate(block_transpose(turn(arrays[quantity]))):
                out[pl.ds((16 * side + block) * ROWS + quantity * 8, 8), :] = part
        pair = [jnp.where(first, v, w) for v, w in zip(turn(arrays[0], 2), turn(arrays[1], 6))]
        pairs += block_transpose(pair)
        late = [roll(v, 4, 0) for v in turn(arrays[2], 6)]
        singles += block_transpose([jnp.where(first, v, w) for v, w in zip(turn(arrays[2], 2), late)])
    from_above = (slot & 2) != 0
    for chunk in range(SLABS):
        lower = (chunk + 16) % SLABS if chunk % 16 == 0 else chunk
        upper = (chunk + 1) % SLABS
        out[pl.ds(chunk * ROWS + 24, 8), :] = jnp.where(from_above, pairs[upper], pairs[lower])
        out[pl.ds(chunk * ROWS + 32, 4), :] = jnp.where(from_above, singles[upper], singles[lower])[:4]


def unpack_kernel(arrived, out, sides, sems):
    copies = []
    for side in range(2):
        for c in range(2):
            parts = [arrived[pl.ds((16 * side + b) * 16 + c * 8, 8), :] for b in range(16)]
            for i, part in enumerate(block_transpose(turn(parts))):
                half, x = divmod(i, 8)
                sides[side, pl.ds(c * LANES + half * 64 + x, 8, stride=8), :] = part
        lanes = pl.ds(side * LANES, LANES)
        copies.append(pltpu.make_async_copy(sides.at[side], out.at[:, lanes], sems.at[side]))
        copies[-1].start()
    for copy in copies:
        copy.wait()


def lane_ids():
    lane = lax.broadcasted_iota(jnp.int32, (SLABS, LANES), 1)
    return lane >= 64, (lane // 8) % 8, lane % 8


def upper_half(overlap):
    lane = lax.broadcasted_iota(jnp.int32, (SLABS, LANES), 1)
    if overlap:
        lane = (lane + jnp.where(lane % 8 >= 4, 8, LANES - 8)) % LANES
    return lane >= 64


def up(a, h, upper):
    if h >= 2:
        return roll(a, h // 2, 0)
    turned = roll(a, 64, 1)
    return jnp.where(upper, turned, roll(turned, 1, 0))


def down(a, h, upper):
    if h >= 2:
        return roll(a, -(h // 2), 0)
    turned = roll(a, 64, 1)
    return jnp.where(upper, roll(turned, -1, 0), turned)


def both(f, a, h, upper):
    return f(a[0], h, upper), f(a[1], h, upper)


def layer(ref, quantity, r):
    return ref[pl.ds(quantity * 8 + r, SLABS, stride=ROWS), :]


def source_layer(ref, r):
    return layer(ref, 0, r), layer(ref, 1, r)


def overlap_layer(ref, r):
    _, _, y = lane_ids()
    pair = ref[pl.ds(24 + r, SLABS, stride=ROWS), :]
    single = ref[pl.ds(32 + r % 4, SLABS, stride=ROWS), :]
    quantities = []
    for packed, base in ((pair, 0), (pair, 4), (single, 4 * (r // 4))):
        quantities.append(jnp.where(y >= 4, roll(packed, -2 - base, 1), roll(packed, 6 - base, 1)))
    used = (y <= 1) | (y >= 6)
    return quantities[0], quantities[1], jnp.where(used, quantities[2], 1.0)


def inside():
    chunk = lax.axis_index("slab")
    _, _, y = lane_ids()
    below = (y >= 6) & jnp.broadcast_to(chunk > 0, y.shape)
    above = (y <= 1) & jnp.broadcast_to(chunk < SLABS - 1, y.shape)
    return below | above


def put(ref, i, a):
    ref[pl.ds(2 * i * SLABS, SLABS), :] = a[0]
    ref[pl.ds((2 * i + 1) * SLABS, SLABS), :] = a[1]


def get(ref, i):
    return ref[pl.ds(2 * i * SLABS, SLABS), :], ref[pl.ds((2 * i + 1) * SLABS, SLABS), :]


N_FACTORS = 7 + 2 * STEPS + 1


def factorize(relatives, factors, overlap=False):
    upper = upper_half(overlap)
    row = lax.broadcasted_iota(jnp.int32, (SLABS, LANES), 0)
    first = row * 16 + jnp.where(upper, 8, 0)
    pivots = []
    diagonal = None
    for r in range(DEPTH):
        z = first + r
        relative = relatives[r]
        inward = jnp.maximum(jnp.maximum(PML - z, z - (NZ - 1 - PML)), 0)
        fraction = inward.astype(F32) / PML
        diagonal = (
            (2.0 + 4.0 * COUPLE) - WAVE_SHIFT * relative,
            (DAMPING * WAVE_SHIFT) * relative + ABSORB * fraction * fraction,
        )
        if r < DEPTH - 1:
            pivots.append(crecip(diagonal if r == 0 else csub(diagonal, pivots[-1])))
            put(factors, r, pivots[-1])
    to_first = pivots[0]
    first_first = pivots[0]
    for r in range(1, DEPTH - 1):
        reached = cmul(to_first, to_first)
        to_first = cmul(to_first, pivots[r])
        first_first = cadd(first_first, cmul(reached, pivots[r]))
    corner = to_first
    last_last = pivots[-1]
    low = (row == 0) & jnp.logical_not(upper)
    left = tuple(jnp.where(low, 0.0, v) for v in corner)
    high = (row == SLABS - 1) & upper
    next_first = tuple(jnp.where(high, 0.0, v) for v in both(down, first_first, 1, upper))
    d = csub(csub(diagonal, last_last), next_first)
    for step in range(STEPS):
        h = 1 << step
        right = both(down, left, h, upper)
        inverse = crecip(d)
        alpha = cmul(left, both(up, inverse, h, upper))
        gamma = cmul(right, both(down, inverse, h, upper))
        put(factors, 7 + 2 * step, alpha)
        put(factors, 8 + 2 * step, gamma)
        d = csub(csub(d, cmul(alpha, left)), cmul(gamma, right))
        left = cmul(alpha, both(up, left, h, upper))
    put(factors, 7 + 2 * STEPS, crecip(d))


def line_solve(rhs, factors, overlap=False):
    pivots = [get(factors, r) for r in range(DEPTH - 1)]
    gone = [rhs[0]]
    for r in range(1, DEPTH - 1):
        gone.append(cadd(rhs[r], cmul(pivots[r - 1], gone[-1])))
    last = cmul(pivots[-1], gone[-1])
    reach = pivots[0]
    reaches = []
    first = cmul(pivots[0], gone[0])
    for r in range(1, DEPTH - 1):
        reaches.append(reach)
        reach = cmul(reach, pivots[r])
        first = cadd(first, cmul(reach, gone[r]))
    upper = upper_half(overlap)
    row = lax.broadcasted_iota(jnp.int32, (SLABS, LANES), 0)
    high = (row == SLABS - 1) & upper
    low = (row == 0) & jnp.logical_not(upper)
    after = tuple(jnp.where(high, 0.0, v) for v in both(down, first, 1, upper))
    g = cadd(cadd(rhs[DEPTH - 1], last), after)
    for step in range(STEPS):
        h = 1 << step
        from_low = cmul(get(factors, 7 + 2 * step), both(up, g, h, upper))
        from_high = cmul(get(factors, 8 + 2 * step), both(down, g, h, upper))
        g = cadd(g, cadd(from_low, from_high))
    separator = cmul(get(factors, 7 + 2 * STEPS), g)
    before = tuple(jnp.where(low, 0.0, v) for v in both(up, separator, 1, upper))
    field = [None] * DEPTH
    field[DEPTH - 1] = separator
    for r in range(DEPTH - 2, -1, -1):
        lit = cadd(gone[r], before if r == 0 else cmul(reaches[r - 1], before))
        field[r] = cmul(pivots[r], cadd(lit, field[r + 1]))
    return field


def cell_lanes(r, low_line):
    _, x, y = lane_ids()
    at = r if low_line else 7 + r
    return ((x == (at - 1) % 8) & (y == 7)) | ((x == (at + 1) % 8) & (y == 0))


def put_edges(main, over, source, relatives, edges):
    _, x, _ = lane_ids()

    def pack(layers, low_line, high_line):
        low = high = layers[0]
        for r in range(1, DEPTH):
            moved = roll(layers[r], 8 * r, 1)
            low = jnp.where(x == (low_line + r) % 8, moved, low)
            high = jnp.where(x == (high_line + r) % 8, moved, high)
        return low, high

    def pack_cells(layers):
        low = high = jnp.zeros((SLABS, LANES), F32)
        for r in range(DEPTH):
            moved = roll(layers[r], 8 * r, 1)
            low = jnp.where(cell_lanes(r, True), moved, low)
            high = jnp.where(cell_lanes(r, False), moved, high)
        return low, high

    packed = [None] * 7
    for c in range(2):
        near = pack([f[c] for f in main], 0, 7)
        far = pack([f[c] for f in main], 1, 6)
        far = roll(far[0], -8, 1), roll(far[1], 8, 1)
        own = pack([f[c] for f in source], 0, 7)
        cells = pack_cells([f[c] for f in over])
        packed[c] = near
        packed[2 + c] = [own[i] + COUPLE * (far[i] + sum_y(near[i], cells[i])) for i in range(2)]
        packed[5 + c] = cells
    packed[4] = pack(relatives, 0, 7)
    for place, pair in enumerate(packed):
        for edge, array, turned in zip(edges, pair, (56, -56)):
            edge[pl.ds(place * SLABS, SLABS), :] = roll(array, turned, 1)


def within():
    tile = lax.axis_index("tile")
    _, x, _ = lane_ids()
    low = (x < 4) & jnp.broadcast_to(tile > 0, x.shape)
    high = (x >= 4) & jnp.broadcast_to(tile < TILES - 1, x.shape)
    return low | high


def beside(halos, place, r):
    _, x, _ = lane_ids()
    low, high = (ref[pl.ds(place * SLABS, SLABS), :] for ref in halos)
    return roll(jnp.where(x == r, low, high), -8 * r, 1)


def over_beside(low, high, r):
    return roll(jnp.where(cell_lanes(r, True), low, high), -8 * r, 1)


def sum_y(field, over):
    _, _, y = lane_ids()
    return roll(jnp.where(y == 7, over, field), 1, 1) + roll(jnp.where(y == 0, over, field), -1, 1)


def sum_main(main, over, near):
    _, x, _ = lane_ids()
    along_x = jnp.where(x == 0, near, roll(main, 8, 1)) + jnp.where(x == 7, near, roll(main, -8, 1))
    return along_x + sum_y(main, over)


def over_edge():
    _, x, y = lane_ids()
    below = y >= 4
    return x == jnp.where(below, 7, 1), x == jnp.where(below, 6, 0)


def sum_over(main, over):
    at_low, at_high = over_edge()
    along_x = jnp.where(at_low, 0.0, roll(over, 8, 1)) + jnp.where(at_high, 0.0, roll(over, -8, 1))
    return along_x + sum_y(over, main)


def relax(source, spread):
    return tuple(s + COUPLE * t for s, t in zip(source, spread))


def masked(field, keep):
    return [tuple(jnp.where(keep, v, 0.0) for v in f) for f in field]


def put_all(ref, field):
    for r in range(DEPTH):
        put(ref, r, field[r])


def get_all(ref):
    return [get(ref, r) for r in range(DEPTH)]


def first_kernel(arrived, factors, over_factors, over_source, main_out, over_out, *edges):
    overlap = [overlap_layer(arrived, r) for r in range(DEPTH)]
    put_all(over_source, [o[:2] for o in overlap])
    factorize([o[2] for o in overlap], over_factors, True)
    over = masked(line_solve([o[:2] for o in overlap], over_factors, True), inside())
    put_all(over_out, over)
    relatives = [layer(arrived, 2, r) for r in range(DEPTH)]
    source = [source_layer(arrived, r) for r in range(DEPTH)]
    factorize(relatives, factors)
    main = line_solve(source, factors)
    put_all(main_out, main)
    put_edges(main, over, source, relatives, edges)


def own_kernel(arrived, over_source, main_in, over_in, main_part, over_part):
    for r in range(DEPTH):
        main, over = get(main_in, r), get(over_in, r)
        put(main_part, r, relax(source_layer(arrived, r), [sum_main(m, e, 0.0) for m, e in zip(main, over)]))
        put(over_part, r, relax(get(over_source, r), [sum_over(m, e) for m, e in zip(main, over)]))


def last_kernel(
    arrived, factors, over_factors, main_in, main_part, over_part, low, high,
    out, near_factors, main_mid, over_mid, near_mid,
):
    halos = (low, high)
    keep = within()
    _, x, _ = lane_ids()
    outermost = (x == 0) | (x == 7)
    at_low, at_high = over_edge()
    over_outermost = at_low | at_high
    tile = lax.axis_index("tile")
    exists = [jnp.broadcast_to(k, x.shape) for k in (tile > 0, tile < TILES - 1)]
    cells = [[jnp.where(k, h[pl.ds((5 + c) * SLABS, SLABS), :], 0.0) for h, k in zip(halos, exists)] for c in range(2)]
    factorize([beside(halos, 4, r) for r in range(DEPTH)], near_factors)
    main_rhs, over_rhs, near_rhs = [], [], []
    for r in range(DEPTH):
        main_adds, over_adds = [], []
        for c in range(2):
            near = jnp.where(keep, beside(halos, c, r), 0.0)
            main_adds.append(jnp.where(outermost, near, 0.0))
            over_adds.append(jnp.where(over_outermost, over_beside(*cells[c], r), 0.0))
        main_rhs.append(relax(get(main_part, r), main_adds))
        over_rhs.append(relax(get(over_part, r), over_adds))
        near_rhs.append(relax((beside(halos, 2, r), beside(halos, 3, r)), get(main_in, r)))
    put_all(main_mid, line_solve(main_rhs, factors))
    put_all(over_mid, masked(line_solve(over_rhs, over_factors, True), inside()))
    put_all(near_mid, masked(line_solve(near_rhs, near_factors), keep))
    rhs = []
    for r in range(DEPTH):
        parts = zip(get(main_mid, r), get(over_mid, r), get(near_mid, r))
        rhs.append(relax(source_layer(arrived, r), [sum_main(*part) for part in parts]))
    field = line_solve(rhs, factors)
    for r in range(DEPTH):
        for c in range(2):
            out[pl.ds(c * 8 + r, SLABS, stride=16), :] = field[r][c]


def call(kernel, name, outs, *args, scratch=(), spec=VMEM, out_spec=VMEM):
    return pl.pallas_call(
        kernel,
        out_shape=[jax.ShapeDtypeStruct(s, F32) for s in outs],
        in_specs=[spec] * len(args),
        out_specs=[out_spec] * len(outs),
        scratch_shapes=list(scratch),
        compiler_params=pltpu.CompilerParams(vmem_limit_bytes=32 << 20),
        cost_estimate=pl.CostEstimate(flops=2_000_000, bytes_accessed=1_000_000, transcendentals=0),
        name=name,
    )(*args)


FIELD = (DEPTH * 2 * SLABS, LANES)
FACTORS = (N_FACTORS * 2 * SLABS, LANES)
EDGE = (7 * SLABS, LANES)

RING_UP = [(i, (i + 1) % TILES) for i in range(TILES)]
RING_DOWN = [(b, a) for a, b in RING_UP]


def exchange(low, high):
    return lax.ppermute(high, "tile", RING_UP), lax.ppermute(low, "tile", RING_DOWN)


def local(source, labels, permittivity):
    rows = source.reshape(2 * 16 * 8, 256)
    marks = labels.reshape(16 * 8, 256)
    inputs = [pltpu.with_memory_space_constraint(v, pltpu.HBM) for v in (permittivity, rows, marks)]
    (packed,) = call(
        pack_kernel, "pack", [(SLABS * ROWS, LANES)], *inputs, spec=HBM,
        scratch=[
            pltpu.VMEM((2, 3 * LANES, LANES), F32),
            pltpu.VMEM((2, LANES, LANES), jnp.int32),
            pltpu.SMEM((8,), F32),
            pltpu.SemaphoreType.DMA((5,)),
        ],
    )
    arrived = lax.all_to_all(packed.reshape(SLABS, ROWS // 4, 4, LANES), "slab", 0, 0).reshape(SLABS * ROWS, LANES)
    factors, over_factors, over_source, main, over, *edges = call(
        first_kernel, "first", [FACTORS, FACTORS, FIELD, FIELD, FIELD, EDGE, EDGE], arrived
    )
    halos = exchange(*edges)
    main_part, over_part = call(own_kernel, "own", [FIELD, FIELD], arrived, over_source, main, over)
    (packed,) = call(
        last_kernel, "last", [(SLABS * 16, LANES)],
        arrived, factors, over_factors, main, main_part, over_part, *halos,
        scratch=[pltpu.VMEM(FACTORS, F32)] + [pltpu.VMEM(FIELD, F32)] * 3,
    )
    arrived = lax.all_to_all(packed.reshape(SLABS, 16, LANES), "slab", 0, 0).reshape(SLABS * 16, LANES)
    (out,) = call(
        unpack_kernel, "unpack", [(2 * 16 * 8, 256)], arrived, out_spec=HBM,
        scratch=[pltpu.VMEM((2, 2 * LANES, LANES), F32), pltpu.SemaphoreType.DMA((2,))],
    )
    return out.reshape(2, 16, 8, 256)


def solution(mesh):
    placed = (P("tilt", "slab", "tile", None), P("slab", "tile", "tilt"), P("tilt"))
    return jax.shard_map(
        local,
        mesh=mesh,
        in_specs=placed,
        out_specs=P("tilt", "slab", "tile", None),
        check_vma=False,
    )
```

```python
import jax
import jax.numpy as jnp
from jax import lax
from jax.experimental import pallas as pl
from jax.experimental.pallas import tpu as pltpu
from jax.sharding import PartitionSpec as P

PML = 8
COUPLE = 0.02
WAVE_SHIFT = 0.15
DAMPING = 0.15
ABSORB = 0.5
NZ = 512
SLABS = 32
TILES = 8
LANES = 128
DEPTH = 8
STEPS = 6
F32 = jnp.float32
VMEM = pl.BlockSpec(memory_space=pltpu.VMEM)
HBM = pl.BlockSpec(memory_space=pltpu.HBM)


ROWS = 36


def roll(x, shift, axis):
    shift %= x.shape[axis]
    return x if shift == 0 else pltpu.roll(x, shift, axis)


def cmul(a, b):
    return a[0] * b[0] - a[1] * b[1], a[0] * b[1] + a[1] * b[0]


def cadd(a, b):
    return a[0] + b[0], a[1] + b[1]


def csub(a, b):
    return a[0] - b[0], a[1] - b[1]


def crecip(a):
    square = a[0] * a[0] + a[1] * a[1]
    scale = pl.reciprocal(square, approx=True)
    scale = scale * (2.0 - square * scale)
    return a[0] * scale, -a[1] * scale


def lanes8():
    return lax.broadcasted_iota(jnp.int32, (8, LANES), 1)


def lanes8():
    return lax.broadcasted_iota(jnp.int32, (8, LANES), 1)


def block_transpose(turned):
    block = lanes8() // 8
    for bit in (1, 2, 4, 8):
        odd = (block & bit) != 0
        turned = [jnp.where(odd, turned[(j + bit) % 16], turned[j]) for j in range(16)]
    return [roll(turned[-c % 16], -8 * c, 1) for c in range(16)]


def turn(arrays, shift=0):
    return [roll(array, shift + 8 * i, 1) for i, array in enumerate(arrays)]


def pack_kernel(table_hbm, source, labels, out, sides, marks, table, sems):
    copies = [pltpu.make_async_copy(table_hbm, table, sems.at[0])]
    for side in range(2):
        lanes = pl.ds(side * LANES, LANES)
        copies.append(pltpu.make_async_copy(labels.at[:, lanes], marks.at[side], sems.at[1 + side]))
    for side in range(2):
        lanes = pl.ds(side * LANES, LANES)
        into = sides.at[side, pl.ds(0, 2 * LANES)]
        copies.append(pltpu.make_async_copy(source.at[:, lanes], into, sems.at[3 + side]))
    for copy in copies:
        copy.start()
    for copy in copies[:3]:
        copy.wait()
    for side in range(2):
        lab = marks[side]
        rel = jnp.full(lab.shape, table[0], F32)
        for m in range(1, 8):
            rel = jnp.where(lab == m, table[m], rel)
        sides[side, pl.ds(2 * LANES, LANES), :] = rel
    for copy in copies[3:]:
        copy.wait()

    def load(side, quantity):
        places = [quantity * LANES + half * 64 + x for half in range(2) for x in range(8)]
        return [sides[side, pl.ds(place, 8, stride=8), :] for place in places]

    slot = lanes8() % 8
    first = slot < 4
    pairs, singles = [], []
    for side in range(2):
        arrays = [load(side, quantity) for quantity in range(3)]
        for quantity in range(3):
            for block, part in enumerate(block_transpose(turn(arrays[quantity]))):
                out[pl.ds((16 * side + block) * ROWS + quantity * 8, 8), :] = part
        pair = [jnp.where(first, v, w) for v, w in zip(turn(arrays[0], 2), turn(arrays[1], 6))]
        pairs += block_transpose(pair)
        late = [roll(v, 4, 0) for v in turn(arrays[2], 6)]
        singles += block_transpose([jnp.where(first, v, w) for v, w in zip(turn(arrays[2], 2), late)])
    from_above = (slot & 2) != 0
    for chunk in range(SLABS):
        lower = (chunk + 16) % SLABS if chunk % 16 == 0 else chunk
        upper = (chunk + 1) % SLABS
        out[pl.ds(chunk * ROWS + 24, 8), :] = jnp.where(from_above, pairs[upper], pairs[lower])
        out[pl.ds(chunk * ROWS + 32, 4), :] = jnp.where(from_above, singles[upper], singles[lower])[:4]


def unpack_kernel(arrived, out, sides, sems):
    copies = []
    for side in range(2):
        for c in range(2):
            parts = [arrived[pl.ds((16 * side + b) * 16 + c * 8, 8), :] for b in range(16)]
            for i, part in enumerate(block_transpose(turn(parts))):
                half, x = divmod(i, 8)
                sides[side, pl.ds(c * LANES + half * 64 + x, 8, stride=8), :] = part
        lanes = pl.ds(side * LANES, LANES)
        copies.append(pltpu.make_async_copy(sides.at[side], out.at[:, lanes], sems.at[side]))
        copies[-1].start()
    for copy in copies:
        copy.wait()


def lane_ids():
    lane = lax.broadcasted_iota(jnp.int32, (SLABS, LANES), 1)
    return lane >= 64, (lane // 8) % 8, lane % 8


def upper_half(overlap):
    lane = lax.broadcasted_iota(jnp.int32, (SLABS, LANES), 1)
    if overlap:
        lane = (lane + jnp.where(lane % 8 >= 4, 8, LANES - 8)) % LANES
    return lane >= 64


def up(a, h, upper):
    if h >= 2:
        return roll(a, h // 2, 0)
    turned = roll(a, 64, 1)
    return jnp.where(upper, turned, roll(turned, 1, 0))


def down(a, h, upper):
    if h >= 2:
        return roll(a, -(h // 2), 0)
    turned = roll(a, 64, 1)
    return jnp.where(upper, roll(turned, -1, 0), turned)


def both(f, a, h, upper):
    return f(a[0], h, upper), f(a[1], h, upper)


def layer(ref, quantity, r):
    return ref[pl.ds(quantity * 8 + r, SLABS, stride=ROWS), :]


def source_layer(ref, r):
    return layer(ref, 0, r), layer(ref, 1, r)


def overlap_layer(ref, r):
    _, _, y = lane_ids()
    pair = ref[pl.ds(24 + r, SLABS, stride=ROWS), :]
    single = ref[pl.ds(32 + r % 4, SLABS, stride=ROWS), :]
    quantities = []
    for packed, base in ((pair, 0), (pair, 4), (single, 4 * (r // 4))):
        quantities.append(jnp.where(y >= 4, roll(packed, -2 - base, 1), roll(packed, 6 - base, 1)))
    used = (y <= 1) | (y >= 6)
    return quantities[0], quantities[1], jnp.where(used, quantities[2], 1.0)


def inside():
    chunk = lax.axis_index("slab")
    _, _, y = lane_ids()
    below = (y >= 6) & jnp.broadcast_to(chunk > 0, y.shape)
    above = (y <= 1) & jnp.broadcast_to(chunk < SLABS - 1, y.shape)
    return below | above


def put(ref, i, a):
    ref[pl.ds(2 * i * SLABS, SLABS), :] = a[0]
    ref[pl.ds((2 * i + 1) * SLABS, SLABS), :] = a[1]


def get(ref, i):
    return ref[pl.ds(2 * i * SLABS, SLABS), :], ref[pl.ds((2 * i + 1) * SLABS, SLABS), :]


N_FACTORS = 7 + 2 * STEPS + 1


def factorize(relatives, factors, overlap=False):
    upper = upper_half(overlap)
    row = lax.broadcasted_iota(jnp.int32, (SLABS, LANES), 0)
    first = row * 16 + jnp.where(upper, 8, 0)
    pivots = []
    diagonal = None
    for r in range(DEPTH):
        z = first + r
        relative = relatives[r]
        inward = jnp.maximum(jnp.maximum(PML - z, z - (NZ - 1 - PML)), 0)
        fraction = inward.astype(F32) / PML
        diagonal = (
            (2.0 + 4.0 * COUPLE) - WAVE_SHIFT * relative,
            (DAMPING * WAVE_SHIFT) * relative + ABSORB * fraction * fraction,
        )
        if r < DEPTH - 1:
            pivots.append(crecip(diagonal if r == 0 else csub(diagonal, pivots[-1])))
            put(factors, r, pivots[-1])
    to_first = pivots[0]
    first_first = pivots[0]
    for r in range(1, DEPTH - 1):
        reached = cmul(to_first, to_first)
        to_first = cmul(to_first, pivots[r])
        first_first = cadd(first_first, cmul(reached, pivots[r]))
    corner = to_first
    last_last = pivots[-1]
    low = (row == 0) & jnp.logical_not(upper)
    left = tuple(jnp.where(low, 0.0, v) for v in corner)
    high = (row == SLABS - 1) & upper
    next_first = tuple(jnp.where(high, 0.0, v) for v in both(down, first_first, 1, upper))
    d = csub(csub(diagonal, last_last), next_first)
    for step in range(STEPS):
        h = 1 << step
        right = both(down, left, h, upper)
        inverse = crecip(d)
        alpha = cmul(left, both(up, inverse, h, upper))
        gamma = cmul(right, both(down, inverse, h, upper))
        put(factors, 7 + 2 * step, alpha)
        put(factors, 8 + 2 * step, gamma)
        d = csub(csub(d, cmul(alpha, left)), cmul(gamma, right))
        left = cmul(alpha, both(up, left, h, upper))
    put(factors, 7 + 2 * STEPS, crecip(d))


def line_solve(rhs, factors, overlap=False):
    pivots = [get(factors, r) for r in range(DEPTH - 1)]
    gone = [rhs[0]]
    for r in range(1, DEPTH - 1):
        gone.append(cadd(rhs[r], cmul(pivots[r - 1], gone[-1])))
    last = cmul(pivots[-1], gone[-1])
    reach = pivots[0]
    reaches = []
    first = cmul(pivots[0], gone[0])
    for r in range(1, DEPTH - 1):
        reaches.append(reach)
        reach = cmul(reach, pivots[r])
        first = cadd(first, cmul(reach, gone[r]))
    upper = upper_half(overlap)
    row = lax.broadcasted_iota(jnp.int32, (SLABS, LANES), 0)
    high = (row == SLABS - 1) & upper
    low = (row == 0) & jnp.logical_not(upper)
    after = tuple(jnp.where(high, 0.0, v) for v in both(down, first, 1, upper))
    g = cadd(cadd(rhs[DEPTH - 1], last), after)
    for step in range(STEPS):
        h = 1 << step
        from_low = cmul(get(factors, 7 + 2 * step), both(up, g, h, upper))
        from_high = cmul(get(factors, 8 + 2 * step), both(down, g, h, upper))
        g = cadd(g, cadd(from_low, from_high))
    separator = cmul(get(factors, 7 + 2 * STEPS), g)
    before = tuple(jnp.where(low, 0.0, v) for v in both(up, separator, 1, upper))
    field = [None] * DEPTH
    field[DEPTH - 1] = separator
    for r in range(DEPTH - 2, -1, -1):
        lit = cadd(gone[r], before if r == 0 else cmul(reaches[r - 1], before))
        field[r] = cmul(pivots[r], cadd(lit, field[r + 1]))
    return field


def cell_lanes(r, low_line):
    _, x, y = lane_ids()
    at = r if low_line else 7 + r
    return ((x == (at - 1) % 8) & (y == 7)) | ((x == (at + 1) % 8) & (y == 0))


def put_edges(main, over, source, relatives, edges):
    _, x, _ = lane_ids()

    def pack(layers, low_line, high_line):
        low = high = layers[0]
        for r in range(1, DEPTH):
            moved = roll(layers[r], 8 * r, 1)
            low = jnp.where(x == (low_line + r) % 8, moved, low)
            high = jnp.where(x == (high_line + r) % 8, moved, high)
        return low, high

    def pack_cells(layers):
        low = high = jnp.zeros((SLABS, LANES), F32)
        for r in range(DEPTH):
            moved = roll(layers[r], 8 * r, 1)
            low = jnp.where(cell_lanes(r, True), moved, low)
            high = jnp.where(cell_lanes(r, False), moved, high)
        return low, high

    _, _, y = lane_ids()
    beside_lines = (y == 0) | (y == 7)
    packed = [None] * 6
    for c in range(2):
        near = pack([f[c] for f in main], 0, 7)
        far = pack([f[c] for f in main], 1, 6)
        far = roll(far[0], -8, 1), roll(far[1], 8, 1)
        own = pack([f[c] for f in source], 0, 7)
        cells = pack_cells([f[c] for f in over])
        packed[c] = near
        packed[2 + c] = [own[i] + COUPLE * (far[i] + sum_y(near[i], cells[i])) for i in range(2)]
        if c == 0:
            packed[5] = cells
        else:
            packed[5] = [jnp.where(beside_lines, re, roll(im, 2, 1)) for re, im in zip(packed[5], cells)]
    packed[4] = pack(relatives, 0, 7)
    for place, pair in enumerate(packed):
        for edge, array, turned in zip(edges, pair, (56, -56)):
            edge[pl.ds(place * SLABS, SLABS), :] = roll(array, turned, 1)


def within():
    tile = lax.axis_index("tile")
    _, x, _ = lane_ids()
    low = (x < 4) & jnp.broadcast_to(tile > 0, x.shape)
    high = (x >= 4) & jnp.broadcast_to(tile < TILES - 1, x.shape)
    return low | high


def beside(halos, place, r):
    _, x, _ = lane_ids()
    low, high = (ref[pl.ds(place * SLABS, SLABS), :] for ref in halos)
    return roll(jnp.where(x == r, low, high), -8 * r, 1)


def over_beside(low, high, c, r):
    _, x, y = lane_ids()
    if c == 0:
        from_low = cell_lanes(r, True)
    else:
        from_low = ((x == r) & (y == 1)) | ((x == (r + 1) % 8) & (y == 2))
    return roll(jnp.where(from_low, low, high), -8 * r - 2 * c, 1)


def sum_y(field, over):
    _, _, y = lane_ids()
    return roll(jnp.where(y == 7, over, field), 1, 1) + roll(jnp.where(y == 0, over, field), -1, 1)


def sum_main(main, over, near):
    _, x, _ = lane_ids()
    along_x = jnp.where(x == 0, near, roll(main, 8, 1)) + jnp.where(x == 7, near, roll(main, -8, 1))
    return along_x + sum_y(main, over)


def over_edge():
    _, x, y = lane_ids()
    below = y >= 4
    return x == jnp.where(below, 7, 1), x == jnp.where(below, 6, 0)


def sum_over(main, over):
    at_low, at_high = over_edge()
    along_x = jnp.where(at_low, 0.0, roll(over, 8, 1)) + jnp.where(at_high, 0.0, roll(over, -8, 1))
    return along_x + sum_y(over, main)


def relax(source, spread):
    return tuple(s + COUPLE * t for s, t in zip(source, spread))


def masked(field, keep):
    return [tuple(jnp.where(keep, v, 0.0) for v in f) for f in field]


def put_all(ref, field):
    for r in range(DEPTH):
        put(ref, r, field[r])


def get_all(ref):
    return [get(ref, r) for r in range(DEPTH)]


def first_kernel(arrived, factors, over_factors, over_source, main_out, over_out, *edges):
    overlap = [overlap_layer(arrived, r) for r in range(DEPTH)]
    put_all(over_source, [o[:2] for o in overlap])
    factorize([o[2] for o in overlap], over_factors, True)
    over = masked(line_solve([o[:2] for o in overlap], over_factors, True), inside())
    put_all(over_out, over)
    relatives = [layer(arrived, 2, r) for r in range(DEPTH)]
    source = [source_layer(arrived, r) for r in range(DEPTH)]
    factorize(relatives, factors)
    main = line_solve(source, factors)
    put_all(main_out, main)
    put_edges(main, over, source, relatives, edges)


def own_kernel(arrived, over_source, main_in, over_in, main_part, over_part):
    for r in range(DEPTH):
        main, over = get(main_in, r), get(over_in, r)
        put(main_part, r, relax(source_layer(arrived, r), [sum_main(m, e, 0.0) for m, e in zip(main, over)]))
        put(over_part, r, relax(get(over_source, r), [sum_over(m, e) for m, e in zip(main, over)]))


def last_kernel(
    arrived, factors, over_factors, main_in, main_part, over_part, low, high,
    out, near_factors, main_mid, over_mid, near_mid,
):
    halos = (low, high)
    keep = within()
    _, x, _ = lane_ids()
    outermost = (x == 0) | (x == 7)
    at_low, at_high = over_edge()
    over_outermost = at_low | at_high
    tile = lax.axis_index("tile")
    exists = [jnp.broadcast_to(k, x.shape) for k in (tile > 0, tile < TILES - 1)]
    cells = [jnp.where(k, h[pl.ds(5 * SLABS, SLABS), :], 0.0) for h, k in zip(halos, exists)]
    factorize([beside(halos, 4, r) for r in range(DEPTH)], near_factors)
    main_rhs, over_rhs, near_rhs = [], [], []
    for r in range(DEPTH):
        main_adds, over_adds = [], []
        for c in range(2):
            near = jnp.where(keep, beside(halos, c, r), 0.0)
            main_adds.append(jnp.where(outermost, near, 0.0))
            over_adds.append(jnp.where(over_outermost, over_beside(*cells, c, r), 0.0))
        main_rhs.append(relax(get(main_part, r), main_adds))
        over_rhs.append(relax(get(over_part, r), over_adds))
        near_rhs.append(relax((beside(halos, 2, r), beside(halos, 3, r)), get(main_in, r)))
    put_all(main_mid, line_solve(main_rhs, factors))
    put_all(over_mid, masked(line_solve(over_rhs, over_factors, True), inside()))
    put_all(near_mid, masked(line_solve(near_rhs, near_factors), keep))
    rhs = []
    for r in range(DEPTH):
        parts = zip(get(main_mid, r), get(over_mid, r), get(near_mid, r))
        rhs.append(relax(source_layer(arrived, r), [sum_main(*part) for part in parts]))
    field = line_solve(rhs, factors)
    for r in range(DEPTH):
        for c in range(2):
            out[pl.ds(c * 8 + r, SLABS, stride=16), :] = field[r][c]


def call(kernel, name, outs, *args, scratch=(), spec=VMEM, out_spec=VMEM):
    return pl.pallas_call(
        kernel,
        out_shape=[jax.ShapeDtypeStruct(s, F32) for s in outs],
        in_specs=[spec] * len(args),
        out_specs=[out_spec] * len(outs),
        scratch_shapes=list(scratch),
        compiler_params=pltpu.CompilerParams(vmem_limit_bytes=32 << 20),
        cost_estimate=pl.CostEstimate(flops=2_000_000, bytes_accessed=1_000_000, transcendentals=0),
        name=name,
    )(*args)


FIELD = (DEPTH * 2 * SLABS, LANES)
FACTORS = (N_FACTORS * 2 * SLABS, LANES)
EDGE = (6 * SLABS, LANES)

RING_UP = [(i, (i + 1) % TILES) for i in range(TILES)]
RING_DOWN = [(b, a) for a, b in RING_UP]


def exchange(low, high):
    return lax.ppermute(high, "tile", RING_UP), lax.ppermute(low, "tile", RING_DOWN)


def local(source, labels, permittivity):
    rows = source.reshape(2 * 16 * 8, 256)
    marks = labels.reshape(16 * 8, 256)
    inputs = [pltpu.with_memory_space_constraint(v, pltpu.HBM) for v in (permittivity, rows, marks)]
    (packed,) = call(
        pack_kernel, "pack", [(SLABS * ROWS, LANES)], *inputs, spec=HBM,
        scratch=[
            pltpu.VMEM((2, 3 * LANES, LANES), F32),
            pltpu.VMEM((2, LANES, LANES), jnp.int32),
            pltpu.SMEM((8,), F32),
            pltpu.SemaphoreType.DMA((5,)),
        ],
    )
    arrived = lax.all_to_all(packed.reshape(SLABS, ROWS // 4, 4, LANES), "slab", 0, 0).reshape(SLABS * ROWS, LANES)
    factors, over_factors, over_source, main, over, *edges = call(
        first_kernel, "first", [FACTORS, FACTORS, FIELD, FIELD, FIELD, EDGE, EDGE], arrived
    )
    halos = exchange(*edges)
    main_part, over_part = call(own_kernel, "own", [FIELD, FIELD], arrived, over_source, main, over)
    (packed,) = call(
        last_kernel, "last", [(SLABS * 16, LANES)],
        arrived, factors, over_factors, main, main_part, over_part, *halos,
        scratch=[pltpu.VMEM(FACTORS, F32)] + [pltpu.VMEM(FIELD, F32)] * 3,
    )
    arrived = lax.all_to_all(packed.reshape(SLABS, 16, LANES), "slab", 0, 0).reshape(SLABS * 16, LANES)
    (out,) = call(
        unpack_kernel, "unpack", [(2 * 16 * 8, 256)], arrived, out_spec=HBM,
        scratch=[pltpu.VMEM((2, 2 * LANES, LANES), F32), pltpu.SemaphoreType.DMA((2,))],
    )
    return out.reshape(2, 16, 8, 256)


def solution(mesh):
    placed = (P("tilt", "slab", "tile", None), P("slab", "tile", "tilt"), P("tilt"))
    return jax.shard_map(
        local,
        mesh=mesh,
        in_specs=placed,
        out_specs=P("tilt", "slab", "tile", None),
        check_vma=False,
    )
```

```python
import jax
import jax.numpy as jnp
from jax import lax
from jax.experimental import pallas as pl
from jax.experimental.pallas import tpu as pltpu
from jax.sharding import PartitionSpec as P

PML = 8
COUPLE = 0.02
WAVE_SHIFT = 0.15
DAMPING = 0.15
ABSORB = 0.5
NZ = 512
SLABS = 32
TILES = 8
LANES = 128
DEPTH = 8
STEPS = 6
F32 = jnp.float32
VMEM = pl.BlockSpec(memory_space=pltpu.VMEM)
HBM = pl.BlockSpec(memory_space=pltpu.HBM)


ROWS = 36


def roll(x, shift, axis):
    shift %= x.shape[axis]
    return x if shift == 0 else pltpu.roll(x, shift, axis)


def cmul(a, b):
    return a[0] * b[0] - a[1] * b[1], a[0] * b[1] + a[1] * b[0]


def cadd(a, b):
    return a[0] + b[0], a[1] + b[1]


def csub(a, b):
    return a[0] - b[0], a[1] - b[1]


def crecip(a):
    square = a[0] * a[0] + a[1] * a[1]
    scale = pl.reciprocal(square, approx=True)
    scale = scale * (2.0 - square * scale)
    return a[0] * scale, -a[1] * scale


def lanes8():
    return lax.broadcasted_iota(jnp.int32, (8, LANES), 1)


def lanes8():
    return lax.broadcasted_iota(jnp.int32, (8, LANES), 1)


def block_transpose(turned):
    block = lanes8() // 8
    for bit in (1, 2, 4, 8):
        odd = (block & bit) != 0
        turned = [jnp.where(odd, turned[(j + bit) % 16], turned[j]) for j in range(16)]
    return [roll(turned[-c % 16], -8 * c, 1) for c in range(16)]


def turn(arrays, shift=0):
    return [roll(array, shift + 8 * i, 1) for i, array in enumerate(arrays)]


def pack_kernel(table_hbm, source, labels, out, sides, marks, table, sems):
    copies = [pltpu.make_async_copy(table_hbm, table, sems.at[0])]
    for side in range(2):
        lanes = pl.ds(side * LANES, LANES)
        copies.append(pltpu.make_async_copy(labels.at[:, lanes], marks.at[side], sems.at[1 + side]))
    for side in range(2):
        lanes = pl.ds(side * LANES, LANES)
        into = sides.at[side, pl.ds(0, 2 * LANES)]
        copies.append(pltpu.make_async_copy(source.at[:, lanes], into, sems.at[3 + side]))
    for copy in copies:
        copy.start()
    for copy in copies[:3]:
        copy.wait()
    for side in range(2):
        lab = marks[side]
        rel = jnp.full(lab.shape, table[0], F32)
        for m in range(1, 8):
            rel = jnp.where(lab == m, table[m], rel)
        sides[side, pl.ds(2 * LANES, LANES), :] = rel
    for copy in copies[3:]:
        copy.wait()

    def load(side, quantity):
        places = [quantity * LANES + half * 64 + x for half in range(2) for x in range(8)]
        return [sides[side, pl.ds(place, 8, stride=8), :] for place in places]

    slot = lanes8() % 8
    first = slot < 4
    chunks = []
    for quantity in range(3):
        blocks = block_transpose(turn(load(0, quantity))) + block_transpose(turn(load(1, quantity)))
        chunks.append(blocks)
        for chunk, block in enumerate(blocks):
            out[pl.ds(chunk * ROWS + quantity * 8, 8), :] = block
    for chunk in range(SLABS):
        picked = [jnp.where(first, blocks[(chunk + 1) % SLABS], blocks[chunk - 1]) for blocks in chunks]
        pair = jnp.where(first, roll(picked[0], 2, 1), roll(picked[1], 6, 1))
        single = jnp.where(first, roll(picked[2], 2, 1), roll(roll(picked[2], 6, 1), 4, 0))
        out[pl.ds(chunk * ROWS + 24, 8), :] = pair
        out[pl.ds(chunk * ROWS + 32, 4), :] = single[:4]


def unpack_kernel(arrived, out, sides, sems):
    copies = []
    for side in range(2):
        for c in range(2):
            parts = [arrived[pl.ds((16 * side + b) * 16 + c * 8, 8), :] for b in range(16)]
            for i, part in enumerate(block_transpose(turn(parts))):
                half, x = divmod(i, 8)
                sides[side, pl.ds(c * LANES + half * 64 + x, 8, stride=8), :] = part
        lanes = pl.ds(side * LANES, LANES)
        copies.append(pltpu.make_async_copy(sides.at[side], out.at[:, lanes], sems.at[side]))
        copies[-1].start()
    for copy in copies:
        copy.wait()


def lane_ids():
    lane = lax.broadcasted_iota(jnp.int32, (SLABS, LANES), 1)
    return lane >= 64, (lane // 8) % 8, lane % 8


def upper_half(overlap):
    lane = lax.broadcasted_iota(jnp.int32, (SLABS, LANES), 1)
    if overlap:
        lane = (lane + jnp.where(lane % 8 >= 4, 8, LANES - 8)) % LANES
    return lane >= 64


def up(a, h, upper):
    if h >= 2:
        return roll(a, h // 2, 0)
    turned = roll(a, 64, 1)
    return jnp.where(upper, turned, roll(turned, 1, 0))


def down(a, h, upper):
    if h >= 2:
        return roll(a, -(h // 2), 0)
    turned = roll(a, 64, 1)
    return jnp.where(upper, roll(turned, -1, 0), turned)


def both(f, a, h, upper):
    return f(a[0], h, upper), f(a[1], h, upper)


def layer(ref, quantity, r):
    return ref[pl.ds(quantity * 8 + r, SLABS, stride=ROWS), :]


def source_layer(ref, r):
    return layer(ref, 0, r), layer(ref, 1, r)


def overlap_layer(ref, r):
    _, _, y = lane_ids()
    pair = ref[pl.ds(24 + r, SLABS, stride=ROWS), :]
    single = ref[pl.ds(32 + r % 4, SLABS, stride=ROWS), :]
    quantities = []
    for packed, base in ((pair, 0), (pair, 4), (single, 4 * (r // 4))):
        quantities.append(jnp.where(y >= 4, roll(packed, -10 - base, 1), roll(packed, 6 - base, 1)))
    used = (y <= 1) | (y >= 6)
    return quantities[0], quantities[1], jnp.where(used, quantities[2], 1.0)


def inside():
    chunk = lax.axis_index("slab")
    _, _, y = lane_ids()
    below = (y >= 6) & jnp.broadcast_to(chunk > 0, y.shape)
    above = (y <= 1) & jnp.broadcast_to(chunk < SLABS - 1, y.shape)
    return below | above


def put(ref, i, a):
    ref[pl.ds(2 * i * SLABS, SLABS), :] = a[0]
    ref[pl.ds((2 * i + 1) * SLABS, SLABS), :] = a[1]


def get(ref, i):
    return ref[pl.ds(2 * i * SLABS, SLABS), :], ref[pl.ds((2 * i + 1) * SLABS, SLABS), :]


N_FACTORS = 7 + 2 * STEPS + 1


def factorize(relatives, factors, overlap=False):
    upper = upper_half(overlap)
    row = lax.broadcasted_iota(jnp.int32, (SLABS, LANES), 0)
    first = row * 16 + jnp.where(upper, 8, 0)
    pivots = []
    diagonal = None
    for r in range(DEPTH):
        z = first + r
        relative = relatives[r]
        inward = jnp.maximum(jnp.maximum(PML - z, z - (NZ - 1 - PML)), 0)
        fraction = inward.astype(F32) / PML
        diagonal = (
            (2.0 + 4.0 * COUPLE) - WAVE_SHIFT * relative,
            (DAMPING * WAVE_SHIFT) * relative + ABSORB * fraction * fraction,
        )
        if r < DEPTH - 1:
            pivots.append(crecip(diagonal if r == 0 else csub(diagonal, pivots[-1])))
            put(factors, r, pivots[-1])
    to_first = pivots[0]
    first_first = pivots[0]
    for r in range(1, DEPTH - 1):
        reached = cmul(to_first, to_first)
        to_first = cmul(to_first, pivots[r])
        first_first = cadd(first_first, cmul(reached, pivots[r]))
    corner = to_first
    last_last = pivots[-1]
    low = (row == 0) & jnp.logical_not(upper)
    left = tuple(jnp.where(low, 0.0, v) for v in corner)
    high = (row == SLABS - 1) & upper
    next_first = tuple(jnp.where(high, 0.0, v) for v in both(down, first_first, 1, upper))
    d = csub(csub(diagonal, last_last), next_first)
    for step in range(STEPS):
        h = 1 << step
        right = both(down, left, h, upper)
        inverse = crecip(d)
        alpha = cmul(left, both(up, inverse, h, upper))
        gamma = cmul(right, both(down, inverse, h, upper))
        put(factors, 7 + 2 * step, alpha)
        put(factors, 8 + 2 * step, gamma)
        d = csub(csub(d, cmul(alpha, left)), cmul(gamma, right))
        left = cmul(alpha, both(up, left, h, upper))
    put(factors, 7 + 2 * STEPS, crecip(d))


def line_solve(rhs, factors, overlap=False):
    pivots = [get(factors, r) for r in range(DEPTH - 1)]
    gone = [rhs[0]]
    for r in range(1, DEPTH - 1):
        gone.append(cadd(rhs[r], cmul(pivots[r - 1], gone[-1])))
    last = cmul(pivots[-1], gone[-1])
    reach = pivots[0]
    reaches = []
    first = cmul(pivots[0], gone[0])
    for r in range(1, DEPTH - 1):
        reaches.append(reach)
        reach = cmul(reach, pivots[r])
        first = cadd(first, cmul(reach, gone[r]))
    upper = upper_half(overlap)
    row = lax.broadcasted_iota(jnp.int32, (SLABS, LANES), 0)
    high = (row == SLABS - 1) & upper
    low = (row == 0) & jnp.logical_not(upper)
    after = tuple(jnp.where(high, 0.0, v) for v in both(down, first, 1, upper))
    g = cadd(cadd(rhs[DEPTH - 1], last), after)
    for step in range(STEPS):
        h = 1 << step
        from_low = cmul(get(factors, 7 + 2 * step), both(up, g, h, upper))
        from_high = cmul(get(factors, 8 + 2 * step), both(down, g, h, upper))
        g = cadd(g, cadd(from_low, from_high))
    separator = cmul(get(factors, 7 + 2 * STEPS), g)
    before = tuple(jnp.where(low, 0.0, v) for v in both(up, separator, 1, upper))
    field = [None] * DEPTH
    field[DEPTH - 1] = separator
    for r in range(DEPTH - 2, -1, -1):
        lit = cadd(gone[r], before if r == 0 else cmul(reaches[r - 1], before))
        field[r] = cmul(pivots[r], cadd(lit, field[r + 1]))
    return field


def cell_lanes(r, low_line):
    _, x, y = lane_ids()
    at = r if low_line else 7 + r
    return ((x == (at - 1) % 8) & (y == 7)) | ((x == (at + 1) % 8) & (y == 0))


def put_edges(main, over, source, relatives, edges):
    _, x, _ = lane_ids()

    def pack(layers, low_line, high_line):
        low = high = layers[0]
        for r in range(1, DEPTH):
            moved = roll(layers[r], 8 * r, 1)
            low = jnp.where(x == (low_line + r) % 8, moved, low)
            high = jnp.where(x == (high_line + r) % 8, moved, high)
        return low, high

    def pack_cells(layers):
        low = high = jnp.zeros((SLABS, LANES), F32)
        for r in range(DEPTH):
            moved = roll(layers[r], 8 * r, 1)
            low = jnp.where(cell_lanes(r, True), moved, low)
            high = jnp.where(cell_lanes(r, False), moved, high)
        return low, high

    _, _, y = lane_ids()
    beside_lines = (y == 0) | (y == 7)
    packed = [None] * 6
    for c in range(2):
        near = pack([f[c] for f in main], 0, 7)
        far = pack([f[c] for f in main], 1, 6)
        far = roll(far[0], -8, 1), roll(far[1], 8, 1)
        own = pack([f[c] for f in source], 0, 7)
        cells = pack_cells([f[c] for f in over])
        packed[c] = near
        packed[2 + c] = [own[i] + COUPLE * (far[i] + sum_y(near[i], cells[i])) for i in range(2)]
        if c == 0:
            packed[5] = cells
        else:
            packed[5] = [jnp.where(beside_lines, re, roll(im, 2, 1)) for re, im in zip(packed[5], cells)]
    packed[4] = pack(relatives, 0, 7)
    for place, pair in enumerate(packed):
        for edge, array, turned in zip(edges, pair, (56, -56)):
            edge[pl.ds(place * SLABS, SLABS), :] = roll(array, turned, 1)


def within():
    tile = lax.axis_index("tile")
    _, x, _ = lane_ids()
    low = (x < 4) & jnp.broadcast_to(tile > 0, x.shape)
    high = (x >= 4) & jnp.broadcast_to(tile < TILES - 1, x.shape)
    return low | high


def beside(halos, place, r):
    _, x, _ = lane_ids()
    low, high = (ref[pl.ds(place * SLABS, SLABS), :] for ref in halos)
    return roll(jnp.where(x == r, low, high), -8 * r, 1)


def over_beside(low, high, c, r):
    _, x, y = lane_ids()
    if c == 0:
        from_low = cell_lanes(r, True)
    else:
        from_low = ((x == r) & (y == 1)) | ((x == (r + 1) % 8) & (y == 2))
    return roll(jnp.where(from_low, low, high), -8 * r - 2 * c, 1)


def sum_y(field, over):
    _, _, y = lane_ids()
    return roll(jnp.where(y == 7, over, field), 1, 1) + roll(jnp.where(y == 0, over, field), -1, 1)


def sum_main(main, over, near):
    _, x, _ = lane_ids()
    along_x = jnp.where(x == 0, near, roll(main, 8, 1)) + jnp.where(x == 7, near, roll(main, -8, 1))
    return along_x + sum_y(main, over)


def over_edge():
    _, x, y = lane_ids()
    below = y >= 4
    return x == jnp.where(below, 7, 1), x == jnp.where(below, 6, 0)


def sum_over(main, over):
    at_low, at_high = over_edge()
    along_x = jnp.where(at_low, 0.0, roll(over, 8, 1)) + jnp.where(at_high, 0.0, roll(over, -8, 1))
    return along_x + sum_y(over, main)


def relax(source, spread):
    return tuple(s + COUPLE * t for s, t in zip(source, spread))


def masked(field, keep):
    return [tuple(jnp.where(keep, v, 0.0) for v in f) for f in field]


def put_all(ref, field):
    for r in range(DEPTH):
        put(ref, r, field[r])


def get_all(ref):
    return [get(ref, r) for r in range(DEPTH)]


def first_kernel(arrived, factors, over_factors, over_source, main_out, over_out, *edges):
    overlap = [overlap_layer(arrived, r) for r in range(DEPTH)]
    put_all(over_source, [o[:2] for o in overlap])
    factorize([o[2] for o in overlap], over_factors, True)
    over = masked(line_solve([o[:2] for o in overlap], over_factors, True), inside())
    put_all(over_out, over)
    relatives = [layer(arrived, 2, r) for r in range(DEPTH)]
    source = [source_layer(arrived, r) for r in range(DEPTH)]
    factorize(relatives, factors)
    main = line_solve(source, factors)
    put_all(main_out, main)
    put_edges(main, over, source, relatives, edges)


def own_kernel(arrived, over_source, main_in, over_in, main_part, over_part):
    for r in range(DEPTH):
        main, over = get(main_in, r), get(over_in, r)
        put(main_part, r, relax(source_layer(arrived, r), [sum_main(m, e, 0.0) for m, e in zip(main, over)]))
        put(over_part, r, relax(get(over_source, r), [sum_over(m, e) for m, e in zip(main, over)]))


def last_kernel(
    arrived, factors, over_factors, main_in, main_part, over_part, low, high,
    out, near_factors, main_mid, over_mid, near_mid,
):
    halos = (low, high)
    keep = within()
    _, x, _ = lane_ids()
    outermost = (x == 0) | (x == 7)
    at_low, at_high = over_edge()
    over_outermost = at_low | at_high
    tile = lax.axis_index("tile")
    exists = [jnp.broadcast_to(k, x.shape) for k in (tile > 0, tile < TILES - 1)]
    cells = [jnp.where(k, h[pl.ds(5 * SLABS, SLABS), :], 0.0) for h, k in zip(halos, exists)]
    factorize([beside(halos, 4, r) for r in range(DEPTH)], near_factors)
    main_rhs, over_rhs, near_rhs = [], [], []
    for r in range(DEPTH):
        main_adds, over_adds = [], []
        for c in range(2):
            near = jnp.where(keep, beside(halos, c, r), 0.0)
            main_adds.append(jnp.where(outermost, near, 0.0))
            over_adds.append(jnp.where(over_outermost, over_beside(*cells, c, r), 0.0))
        main_rhs.append(relax(get(main_part, r), main_adds))
        over_rhs.append(relax(get(over_part, r), over_adds))
        near_rhs.append(relax((beside(halos, 2, r), beside(halos, 3, r)), get(main_in, r)))
    put_all(main_mid, line_solve(main_rhs, factors))
    put_all(over_mid, masked(line_solve(over_rhs, over_factors, True), inside()))
    put_all(near_mid, masked(line_solve(near_rhs, near_factors), keep))
    rhs = []
    for r in range(DEPTH):
        parts = zip(get(main_mid, r), get(over_mid, r), get(near_mid, r))
        rhs.append(relax(source_layer(arrived, r), [sum_main(*part) for part in parts]))
    field = line_solve(rhs, factors)
    for r in range(DEPTH):
        for c in range(2):
            out[pl.ds(c * 8 + r, SLABS, stride=16), :] = field[r][c]


def call(kernel, name, outs, *args, scratch=(), spec=VMEM, out_spec=VMEM):
    return pl.pallas_call(
        kernel,
        out_shape=[jax.ShapeDtypeStruct(s, F32) for s in outs],
        in_specs=[spec] * len(args),
        out_specs=[out_spec] * len(outs),
        scratch_shapes=list(scratch),
        compiler_params=pltpu.CompilerParams(vmem_limit_bytes=32 << 20),
        cost_estimate=pl.CostEstimate(flops=2_000_000, bytes_accessed=1_000_000, transcendentals=0),
        name=name,
    )(*args)


FIELD = (DEPTH * 2 * SLABS, LANES)
FACTORS = (N_FACTORS * 2 * SLABS, LANES)
EDGE = (6 * SLABS, LANES)

RING_UP = [(i, (i + 1) % TILES) for i in range(TILES)]
RING_DOWN = [(b, a) for a, b in RING_UP]


def exchange(low, high):
    return lax.ppermute(high, "tile", RING_UP), lax.ppermute(low, "tile", RING_DOWN)


def local(source, labels, permittivity):
    rows = source.reshape(2 * 16 * 8, 256)
    marks = labels.reshape(16 * 8, 256)
    inputs = [pltpu.with_memory_space_constraint(v, pltpu.HBM) for v in (permittivity, rows, marks)]
    (packed,) = call(
        pack_kernel, "pack", [(SLABS * ROWS, LANES)], *inputs, spec=HBM,
        scratch=[
            pltpu.VMEM((2, 3 * LANES, LANES), F32),
            pltpu.VMEM((2, LANES, LANES), jnp.int32),
            pltpu.SMEM((8,), F32),
            pltpu.SemaphoreType.DMA((5,)),
        ],
    )
    arrived = lax.all_to_all(packed.reshape(SLABS, ROWS // 4, 4, LANES), "slab", 0, 0).reshape(SLABS * ROWS, LANES)
    factors, over_factors, over_source, main, over, *edges = call(
        first_kernel, "first", [FACTORS, FACTORS, FIELD, FIELD, FIELD, EDGE, EDGE], arrived
    )
    halos = exchange(*edges)
    main_part, over_part = call(own_kernel, "own", [FIELD, FIELD], arrived, over_source, main, over)
    (packed,) = call(
        last_kernel, "last", [(SLABS * 16, LANES)],
        arrived, factors, over_factors, main, main_part, over_part, *halos,
        scratch=[pltpu.VMEM(FACTORS, F32)] + [pltpu.VMEM(FIELD, F32)] * 3,
    )
    arrived = lax.all_to_all(packed.reshape(SLABS, 16, LANES), "slab", 0, 0).reshape(SLABS * 16, LANES)
    (out,) = call(
        unpack_kernel, "unpack", [(2 * 16 * 8, 256)], arrived, out_spec=HBM,
        scratch=[pltpu.VMEM((2, 2 * LANES, LANES), F32), pltpu.SemaphoreType.DMA((2,))],
    )
    return out.reshape(2, 16, 8, 256)


def solution(mesh):
    placed = (P("tilt", "slab", "tile", None), P("slab", "tile", "tilt"), P("tilt"))
    return jax.shard_map(
        local,
        mesh=mesh,
        in_specs=placed,
        out_specs=P("tilt", "slab", "tile", None),
        check_vma=False,
    )
```

```python
import jax
import jax.numpy as jnp
from jax import lax
from jax.experimental import pallas as pl
from jax.experimental.pallas import tpu as pltpu
from jax.sharding import PartitionSpec as P

PML = 8
COUPLE = 0.02
WAVE_SHIFT = 0.15
DAMPING = 0.15
ABSORB = 0.5
NZ = 512
SLABS = 32
TILES = 8
LANES = 128
DEPTH = 8
STEPS = 6
F32 = jnp.float32
VMEM = pl.BlockSpec(memory_space=pltpu.VMEM)
HBM = pl.BlockSpec(memory_space=pltpu.HBM)


ROWS = 36


def roll(x, shift, axis):
    shift %= x.shape[axis]
    return x if shift == 0 else pltpu.roll(x, shift, axis)


def cmul(a, b):
    return a[0] * b[0] - a[1] * b[1], a[0] * b[1] + a[1] * b[0]


def cadd(a, b):
    return a[0] + b[0], a[1] + b[1]


def csub(a, b):
    return a[0] - b[0], a[1] - b[1]


def crecip(a):
    square = a[0] * a[0] + a[1] * a[1]
    scale = pl.reciprocal(square, approx=True)
    scale = scale * (2.0 - square * scale)
    return a[0] * scale, -a[1] * scale


def lanes8():
    return lax.broadcasted_iota(jnp.int32, (8, LANES), 1)


def lanes8():
    return lax.broadcasted_iota(jnp.int32, (8, LANES), 1)


def block_transpose(turned):
    block = lanes8() // 8
    for bit in (1, 2, 4, 8):
        odd = (block & bit) != 0
        turned = [jnp.where(odd, turned[(j + bit) % 16], turned[j]) for j in range(16)]
    return [roll(turned[-c % 16], -8 * c, 1) for c in range(16)]


def turn(arrays, shift=0):
    return [roll(array, shift + 8 * i, 1) for i, array in enumerate(arrays)]


def pack_kernel(table_hbm, source, labels, out, sides, marks, table, sems):
    copies = [pltpu.make_async_copy(table_hbm, table, sems.at[0])]
    for side in range(2):
        lanes = pl.ds(side * LANES, LANES)
        copies.append(pltpu.make_async_copy(labels.at[:, lanes], marks.at[side], sems.at[1 + side]))
    for side in range(2):
        lanes = pl.ds(side * LANES, LANES)
        into = sides.at[side, pl.ds(0, 2 * LANES)]
        copies.append(pltpu.make_async_copy(source.at[:, lanes], into, sems.at[3 + side]))
    for copy in copies:
        copy.start()
    for copy in copies[:3]:
        copy.wait()
    for side in range(2):
        lab = marks[side]
        rel = jnp.full(lab.shape, table[0], F32)
        for m in range(1, 8):
            rel = jnp.where(lab == m, table[m], rel)
        sides[side, pl.ds(2 * LANES, LANES), :] = rel
    for copy in copies[3:]:
        copy.wait()

    def load(side, quantity):
        places = [quantity * LANES + half * 64 + x for half in range(2) for x in range(8)]
        return [sides[side, pl.ds(place, 8, stride=8), :] for place in places]

    slot = lanes8() % 8
    first = slot < 4
    chunks = []
    for quantity in range(3):
        blocks = block_transpose(turn(load(0, quantity))) + block_transpose(turn(load(1, quantity)))
        chunks.append(blocks)
        for chunk, block in enumerate(blocks):
            out[pl.ds(chunk * ROWS + quantity * 8, 8), :] = block
    for chunk in range(SLABS):
        picked = [jnp.where(first, blocks[(chunk + 1) % SLABS], blocks[chunk - 1]) for blocks in chunks]
        pair = jnp.where(first, roll(picked[0], 2, 1), roll(picked[1], 6, 1))
        single = jnp.where(first, roll(picked[2], 2, 1), roll(roll(picked[2], 6, 1), 4, 0))
        out[pl.ds(chunk * ROWS + 24, 8), :] = pair
        out[pl.ds(chunk * ROWS + 32, 4), :] = single[:4]


def unpack_kernel(arrived, out, sides, sems):
    copies = []
    for side in range(2):
        for c in range(2):
            parts = [arrived[pl.ds((16 * side + b) * 16 + c * 8, 8), :] for b in range(16)]
            for i, part in enumerate(block_transpose(turn(parts))):
                half, x = divmod(i, 8)
                sides[side, pl.ds(c * LANES + half * 64 + x, 8, stride=8), :] = part
        lanes = pl.ds(side * LANES, LANES)
        copies.append(pltpu.make_async_copy(sides.at[side], out.at[:, lanes], sems.at[side]))
        copies[-1].start()
    for copy in copies:
        copy.wait()


def lane_ids():
    lane = lax.broadcasted_iota(jnp.int32, (SLABS, LANES), 1)
    return lane >= 64, (lane // 8) % 8, lane % 8


def upper_half(overlap):
    lane = lax.broadcasted_iota(jnp.int32, (SLABS, LANES), 1)
    if overlap:
        lane = (lane + jnp.where(lane % 8 >= 4, 8, LANES - 8)) % LANES
    return lane >= 64


def up(a, h, upper):
    if h >= 2:
        return roll(a, h // 2, 0)
    turned = roll(a, 64, 1)
    return jnp.where(upper, turned, roll(turned, 1, 0))


def down(a, h, upper):
    if h >= 2:
        return roll(a, -(h // 2), 0)
    turned = roll(a, 64, 1)
    return jnp.where(upper, roll(turned, -1, 0), turned)


def both(f, a, h, upper):
    return f(a[0], h, upper), f(a[1], h, upper)


def layer(ref, quantity, r):
    return ref[pl.ds(quantity * 8 + r, SLABS, stride=ROWS), :]


def source_layer(ref, r):
    return layer(ref, 0, r), layer(ref, 1, r)


def overlap_layer(ref, r):
    _, _, y = lane_ids()
    pair = ref[pl.ds(24 + r, SLABS, stride=ROWS), :]
    single = ref[pl.ds(32 + r % 4, SLABS, stride=ROWS), :]
    quantities = []
    for packed, base in ((pair, 0), (pair, 4), (single, 4 * (r // 4))):
        quantities.append(jnp.where(y >= 4, roll(packed, -10 - base, 1), roll(packed, 6 - base, 1)))
    used = (y <= 1) | (y >= 6)
    return quantities[0], quantities[1], jnp.where(used, quantities[2], 1.0)


def inside():
    chunk = lax.axis_index("slab")
    _, _, y = lane_ids()
    below = (y >= 6) & jnp.broadcast_to(chunk > 0, y.shape)
    above = (y <= 1) & jnp.broadcast_to(chunk < SLABS - 1, y.shape)
    return below | above


def put(ref, i, a):
    ref[pl.ds(2 * i * SLABS, SLABS), :] = a[0]
    ref[pl.ds((2 * i + 1) * SLABS, SLABS), :] = a[1]


def get(ref, i):
    return ref[pl.ds(2 * i * SLABS, SLABS), :], ref[pl.ds((2 * i + 1) * SLABS, SLABS), :]


N_FACTORS = 7 + 2 * STEPS + 1


def factorize(relatives, factors, overlap=False):
    upper = upper_half(overlap)
    row = lax.broadcasted_iota(jnp.int32, (SLABS, LANES), 0)
    first = row * 16 + jnp.where(upper, 8, 0)
    pivots = []
    diagonal = None
    for r in range(DEPTH):
        z = first + r
        relative = relatives[r]
        inward = jnp.maximum(jnp.maximum(PML - z, z - (NZ - 1 - PML)), 0)
        fraction = inward.astype(F32) / PML
        diagonal = (
            (2.0 + 4.0 * COUPLE) - WAVE_SHIFT * relative,
            (DAMPING * WAVE_SHIFT) * relative + ABSORB * fraction * fraction,
        )
        if r < DEPTH - 1:
            pivots.append(crecip(diagonal if r == 0 else csub(diagonal, pivots[-1])))
            put(factors, r, pivots[-1])
    to_first = pivots[0]
    first_first = pivots[0]
    for r in range(1, DEPTH - 1):
        reached = cmul(to_first, to_first)
        to_first = cmul(to_first, pivots[r])
        first_first = cadd(first_first, cmul(reached, pivots[r]))
    corner = to_first
    last_last = pivots[-1]
    low = (row == 0) & jnp.logical_not(upper)
    left = tuple(jnp.where(low, 0.0, v) for v in corner)
    high = (row == SLABS - 1) & upper
    next_first = tuple(jnp.where(high, 0.0, v) for v in both(down, first_first, 1, upper))
    d = csub(csub(diagonal, last_last), next_first)
    for step in range(STEPS):
        h = 1 << step
        right = both(down, left, h, upper)
        inverse = crecip(d)
        alpha = cmul(left, both(up, inverse, h, upper))
        gamma = cmul(right, both(down, inverse, h, upper))
        put(factors, 7 + 2 * step, alpha)
        put(factors, 8 + 2 * step, gamma)
        d = csub(csub(d, cmul(alpha, left)), cmul(gamma, right))
        left = cmul(alpha, both(up, left, h, upper))
    put(factors, 7 + 2 * STEPS, crecip(d))


def line_solve(rhs, factors, overlap=False):
    pivots = [get(factors, r) for r in range(DEPTH - 1)]
    gone = [rhs[0]]
    for r in range(1, DEPTH - 1):
        gone.append(cadd(rhs[r], cmul(pivots[r - 1], gone[-1])))
    last = cmul(pivots[-1], gone[-1])
    reach = pivots[0]
    reaches = []
    first = cmul(pivots[0], gone[0])
    for r in range(1, DEPTH - 1):
        reaches.append(reach)
        reach = cmul(reach, pivots[r])
        first = cadd(first, cmul(reach, gone[r]))
    upper = upper_half(overlap)
    row = lax.broadcasted_iota(jnp.int32, (SLABS, LANES), 0)
    high = (row == SLABS - 1) & upper
    low = (row == 0) & jnp.logical_not(upper)
    after = tuple(jnp.where(high, 0.0, v) for v in both(down, first, 1, upper))
    g = cadd(cadd(rhs[DEPTH - 1], last), after)
    for step in range(STEPS):
        h = 1 << step
        from_low = cmul(get(factors, 7 + 2 * step), both(up, g, h, upper))
        from_high = cmul(get(factors, 8 + 2 * step), both(down, g, h, upper))
        g = cadd(g, cadd(from_low, from_high))
    separator = cmul(get(factors, 7 + 2 * STEPS), g)
    before = tuple(jnp.where(low, 0.0, v) for v in both(up, separator, 1, upper))
    field = [None] * DEPTH
    field[DEPTH - 1] = separator
    for r in range(DEPTH - 2, -1, -1):
        lit = cadd(gone[r], before if r == 0 else cmul(reaches[r - 1], before))
        field[r] = cmul(pivots[r], cadd(lit, field[r + 1]))
    return field


def cell_lanes(r, low_line):
    _, x, y = lane_ids()
    at = r if low_line else 7 + r
    return ((x == (at - 1) % 8) & (y == 7)) | ((x == (at + 1) % 8) & (y == 0))


def put_edges(main, over, source, relatives, edges):
    _, x, _ = lane_ids()

    def pack(layers, low_line, high_line):
        low = high = layers[0]
        for r in range(1, DEPTH):
            moved = roll(layers[r], 8 * r, 1)
            low = jnp.where(x == (low_line + r) % 8, moved, low)
            high = jnp.where(x == (high_line + r) % 8, moved, high)
        return low, high

    def pack_cells(layers):
        low = high = jnp.zeros((SLABS, LANES), F32)
        for r in range(DEPTH):
            moved = roll(layers[r], 8 * r, 1)
            low = jnp.where(cell_lanes(r, True), moved, low)
            high = jnp.where(cell_lanes(r, False), moved, high)
        return low, high

    _, _, y = lane_ids()
    beside_lines = (y == 0) | (y == 7)
    packed = [None] * 6
    for c in range(2):
        near = pack([f[c] for f in main], 0, 7)
        far = pack([f[c] for f in main], 1, 6)
        far = roll(far[0], -8, 1), roll(far[1], 8, 1)
        own = pack([f[c] for f in source], 0, 7)
        cells = pack_cells([f[c] for f in over])
        packed[c] = near
        packed[2 + c] = [own[i] + COUPLE * (far[i] + sum_y(near[i], cells[i])) for i in range(2)]
        if c == 0:
            packed[5] = cells
        else:
            packed[5] = [jnp.where(beside_lines, re, roll(im, 2, 1)) for re, im in zip(packed[5], cells)]
    packed[4] = pack(relatives, 0, 7)
    for place, pair in enumerate(packed):
        for edge, array, turned in zip(edges, pair, (56, -56)):
            edge[pl.ds(place * SLABS, SLABS), :] = roll(array, turned, 1)


def within():
    tile = lax.axis_index("tile")
    _, x, _ = lane_ids()
    low = (x < 4) & jnp.broadcast_to(tile > 0, x.shape)
    high = (x >= 4) & jnp.broadcast_to(tile < TILES - 1, x.shape)
    return low | high


def beside(halos, place, r):
    _, x, _ = lane_ids()
    low, high = (ref[pl.ds(place * SLABS, SLABS), :] for ref in halos)
    return roll(jnp.where(x == r, low, high), -8 * r, 1)


def over_beside(low, high, c, r):
    _, x, y = lane_ids()
    if c == 0:
        from_low = cell_lanes(r, True)
    else:
        from_low = ((x == r) & (y == 1)) | ((x == (r + 1) % 8) & (y == 2))
    return roll(jnp.where(from_low, low, high), -8 * r - 2 * c, 1)


def sum_y(field, over):
    _, _, y = lane_ids()
    return roll(jnp.where(y == 7, over, field), 1, 1) + roll(jnp.where(y == 0, over, field), -1, 1)


def sum_main(main, over, near):
    _, x, _ = lane_ids()
    along_x = jnp.where(x == 0, near, roll(main, 8, 1)) + jnp.where(x == 7, near, roll(main, -8, 1))
    return along_x + sum_y(main, over)


def over_edge():
    _, x, y = lane_ids()
    below = y >= 4
    return x == jnp.where(below, 7, 1), x == jnp.where(below, 6, 0)


def sum_over(main, over):
    at_low, at_high = over_edge()
    along_x = jnp.where(at_low, 0.0, roll(over, 8, 1)) + jnp.where(at_high, 0.0, roll(over, -8, 1))
    return along_x + sum_y(over, main)


def relax(source, spread):
    return tuple(s + COUPLE * t for s, t in zip(source, spread))


def masked(field, keep):
    return [tuple(jnp.where(keep, v, 0.0) for v in f) for f in field]


def put_all(ref, field):
    for r in range(DEPTH):
        put(ref, r, field[r])


def get_all(ref):
    return [get(ref, r) for r in range(DEPTH)]


def first_kernel(arrived, factors, over_factors, main_out, over_out, *edges):
    overlap = [overlap_layer(arrived, r) for r in range(DEPTH)]
    factorize([o[2] for o in overlap], over_factors, True)
    over = masked(line_solve([o[:2] for o in overlap], over_factors, True), inside())
    put_all(over_out, over)
    relatives = [layer(arrived, 2, r) for r in range(DEPTH)]
    source = [source_layer(arrived, r) for r in range(DEPTH)]
    factorize(relatives, factors)
    main = line_solve(source, factors)
    put_all(main_out, main)
    put_edges(main, over, source, relatives, edges)


def own_kernel(arrived, main_in, over_in, main_part, over_part):
    for r in range(DEPTH):
        main, over = get(main_in, r), get(over_in, r)
        put(main_part, r, relax(source_layer(arrived, r), [sum_main(m, e, 0.0) for m, e in zip(main, over)]))
        put(over_part, r, relax(overlap_layer(arrived, r)[:2], [sum_over(m, e) for m, e in zip(main, over)]))


def last_kernel(
    arrived, factors, over_factors, main_in, main_part, over_part, low, high,
    out, near_factors, main_mid, over_mid, near_mid,
):
    halos = (low, high)
    keep = within()
    _, x, _ = lane_ids()
    outermost = (x == 0) | (x == 7)
    at_low, at_high = over_edge()
    over_outermost = at_low | at_high
    tile = lax.axis_index("tile")
    exists = [jnp.broadcast_to(k, x.shape) for k in (tile > 0, tile < TILES - 1)]
    cells = [jnp.where(k, h[pl.ds(5 * SLABS, SLABS), :], 0.0) for h, k in zip(halos, exists)]
    factorize([beside(halos, 4, r) for r in range(DEPTH)], near_factors)
    main_rhs, over_rhs, near_rhs = [], [], []
    for r in range(DEPTH):
        main_adds, over_adds = [], []
        for c in range(2):
            near = jnp.where(keep, beside(halos, c, r), 0.0)
            main_adds.append(jnp.where(outermost, near, 0.0))
            over_adds.append(jnp.where(over_outermost, over_beside(*cells, c, r), 0.0))
        main_rhs.append(relax(get(main_part, r), main_adds))
        over_rhs.append(relax(get(over_part, r), over_adds))
        near_rhs.append(relax((beside(halos, 2, r), beside(halos, 3, r)), get(main_in, r)))
    put_all(main_mid, line_solve(main_rhs, factors))
    put_all(over_mid, masked(line_solve(over_rhs, over_factors, True), inside()))
    put_all(near_mid, masked(line_solve(near_rhs, near_factors), keep))
    rhs = []
    for r in range(DEPTH):
        parts = zip(get(main_mid, r), get(over_mid, r), get(near_mid, r))
        rhs.append(relax(source_layer(arrived, r), [sum_main(*part) for part in parts]))
    field = line_solve(rhs, factors)
    for r in range(DEPTH):
        for c in range(2):
            out[pl.ds(c * 8 + r, SLABS, stride=16), :] = field[r][c]


def call(kernel, name, outs, *args, scratch=(), spec=VMEM, out_spec=VMEM):
    return pl.pallas_call(
        kernel,
        out_shape=[jax.ShapeDtypeStruct(s, F32) for s in outs],
        in_specs=[spec] * len(args),
        out_specs=[out_spec] * len(outs),
        scratch_shapes=list(scratch),
        compiler_params=pltpu.CompilerParams(vmem_limit_bytes=32 << 20),
        cost_estimate=pl.CostEstimate(flops=2_000_000, bytes_accessed=1_000_000, transcendentals=0),
        name=name,
    )(*args)


FIELD = (DEPTH * 2 * SLABS, LANES)
FACTORS = (N_FACTORS * 2 * SLABS, LANES)
EDGE = (6 * SLABS, LANES)

RING_UP = [(i, (i + 1) % TILES) for i in range(TILES)]
RING_DOWN = [(b, a) for a, b in RING_UP]


def exchange(low, high):
    return lax.ppermute(high, "tile", RING_UP), lax.ppermute(low, "tile", RING_DOWN)


def local(source, labels, permittivity):
    rows = source.reshape(2 * 16 * 8, 256)
    marks = labels.reshape(16 * 8, 256)
    inputs = [pltpu.with_memory_space_constraint(v, pltpu.HBM) for v in (permittivity, rows, marks)]
    (packed,) = call(
        pack_kernel, "pack", [(SLABS * ROWS, LANES)], *inputs, spec=HBM,
        scratch=[
            pltpu.VMEM((2, 3 * LANES, LANES), F32),
            pltpu.VMEM((2, LANES, LANES), jnp.int32),
            pltpu.SMEM((8,), F32),
            pltpu.SemaphoreType.DMA((5,)),
        ],
    )
    arrived = lax.all_to_all(packed.reshape(SLABS, ROWS // 4, 4, LANES), "slab", 0, 0).reshape(SLABS * ROWS, LANES)
    factors, over_factors, main, over, *edges = call(
        first_kernel, "first", [FACTORS, FACTORS, FIELD, FIELD, EDGE, EDGE], arrived
    )
    halos = exchange(*edges)
    main_part, over_part = call(own_kernel, "own", [FIELD, FIELD], arrived, main, over)
    (packed,) = call(
        last_kernel, "last", [(SLABS * 16, LANES)],
        arrived, factors, over_factors, main, main_part, over_part, *halos,
        scratch=[pltpu.VMEM(FACTORS, F32)] + [pltpu.VMEM(FIELD, F32)] * 3,
    )
    arrived = lax.all_to_all(packed.reshape(SLABS, 16, LANES), "slab", 0, 0).reshape(SLABS * 16, LANES)
    (out,) = call(
        unpack_kernel, "unpack", [(2 * 16 * 8, 256)], arrived, out_spec=HBM,
        scratch=[pltpu.VMEM((2, 2 * LANES, LANES), F32), pltpu.SemaphoreType.DMA((2,))],
    )
    return out.reshape(2, 16, 8, 256)


def solution(mesh):
    placed = (P("tilt", "slab", "tile", None), P("slab", "tile", "tilt"), P("tilt"))
    return jax.shard_map(
        local,
        mesh=mesh,
        in_specs=placed,
        out_specs=P("tilt", "slab", "tile", None),
        check_vma=False,
    )
```

```python
import jax
import jax.numpy as jnp
from jax import lax
from jax.experimental import pallas as pl
from jax.experimental.pallas import tpu as pltpu
from jax.sharding import PartitionSpec as P

PML = 8
COUPLE = 0.02
WAVE_SHIFT = 0.15
DAMPING = 0.15
ABSORB = 0.5
NZ = 512
SLABS = 32
TILES = 8
LANES = 128
DEPTH = 8
STEPS = 6
F32 = jnp.float32
VMEM = pl.BlockSpec(memory_space=pltpu.VMEM)
HBM = pl.BlockSpec(memory_space=pltpu.HBM)


ROWS = 36


def roll(x, shift, axis):
    shift %= x.shape[axis]
    return x if shift == 0 else pltpu.roll(x, shift, axis)


def cmul(a, b):
    return a[0] * b[0] - a[1] * b[1], a[0] * b[1] + a[1] * b[0]


def cadd(a, b):
    return a[0] + b[0], a[1] + b[1]


def csub(a, b):
    return a[0] - b[0], a[1] - b[1]


def crecip(a):
    square = a[0] * a[0] + a[1] * a[1]
    scale = pl.reciprocal(square, approx=True)
    scale = scale * (2.0 - square * scale)
    return a[0] * scale, -a[1] * scale


def lanes8():
    return lax.broadcasted_iota(jnp.int32, (8, LANES), 1)


def lanes8():
    return lax.broadcasted_iota(jnp.int32, (8, LANES), 1)


def block_transpose(turned):
    block = lanes8() // 8
    for bit in (1, 2, 4, 8):
        odd = (block & bit) != 0
        turned = [jnp.where(odd, turned[(j + bit) % 16], turned[j]) for j in range(16)]
    return [roll(turned[-c % 16], -8 * c, 1) for c in range(16)]


def turn(arrays, shift=0):
    return [roll(array, shift + 8 * i, 1) for i, array in enumerate(arrays)]


def pack_kernel(table_hbm, source, labels, out, sides, marks, table, sems):
    copies = [pltpu.make_async_copy(table_hbm, table, sems.at[0])]
    for side in range(2):
        lanes = pl.ds(side * LANES, LANES)
        copies.append(pltpu.make_async_copy(labels.at[:, lanes], marks.at[side], sems.at[1 + side]))
    for quantity in range(2):
        rows = pl.ds(quantity * LANES, LANES)
        for side in range(2):
            lanes = pl.ds(side * LANES, LANES)
            sem = sems.at[3 + 2 * quantity + side]
            copies.append(pltpu.make_async_copy(source.at[rows, lanes], sides.at[side, rows], sem))
    for copy in copies:
        copy.start()
    for copy in copies[:3]:
        copy.wait()
    for side in range(2):
        lab = marks[side]
        rel = jnp.full(lab.shape, table[0], F32)
        for m in range(1, 8):
            rel = jnp.where(lab == m, table[m], rel)
        sides[side, pl.ds(2 * LANES, LANES), :] = rel

    def load(side, quantity):
        places = [quantity * LANES + half * 64 + x for half in range(2) for x in range(8)]
        return [sides[side, pl.ds(place, 8, stride=8), :] for place in places]

    slot = lanes8() % 8
    first = slot < 4
    chunks = [None] * 3
    for quantity in (2, 0, 1):
        if quantity < 2:
            for copy in copies[3 + 2 * quantity : 5 + 2 * quantity]:
                copy.wait()
        blocks = block_transpose(turn(load(0, quantity))) + block_transpose(turn(load(1, quantity)))
        chunks[quantity] = blocks
        for chunk, block in enumerate(blocks):
            out[pl.ds(chunk * ROWS + quantity * 8, 8), :] = block
    for chunk in range(SLABS):
        picked = [jnp.where(first, blocks[(chunk + 1) % SLABS], blocks[chunk - 1]) for blocks in chunks]
        pair = jnp.where(first, roll(picked[0], 2, 1), roll(picked[1], 6, 1))
        single = jnp.where(first, roll(picked[2], 2, 1), roll(roll(picked[2], 6, 1), 4, 0))
        out[pl.ds(chunk * ROWS + 24, 8), :] = pair
        out[pl.ds(chunk * ROWS + 32, 4), :] = single[:4]


def unpack_kernel(arrived, out, sides, sems):
    copies = []
    for side in range(2):
        for c in range(2):
            parts = [arrived[pl.ds((16 * side + b) * 16 + c * 8, 8), :] for b in range(16)]
            for i, part in enumerate(block_transpose(turn(parts))):
                half, x = divmod(i, 8)
                sides[side, pl.ds(c * LANES + half * 64 + x, 8, stride=8), :] = part
        lanes = pl.ds(side * LANES, LANES)
        copies.append(pltpu.make_async_copy(sides.at[side], out.at[:, lanes], sems.at[side]))
        copies[-1].start()
    for copy in copies:
        copy.wait()


def lane_ids():
    lane = lax.broadcasted_iota(jnp.int32, (SLABS, LANES), 1)
    return lane >= 64, (lane // 8) % 8, lane % 8


def upper_half(overlap):
    lane = lax.broadcasted_iota(jnp.int32, (SLABS, LANES), 1)
    if overlap:
        lane = (lane + jnp.where(lane % 8 >= 4, 8, LANES - 8)) % LANES
    return lane >= 64


def up(a, h, upper):
    if h >= 2:
        return roll(a, h // 2, 0)
    turned = roll(a, 64, 1)
    return jnp.where(upper, turned, roll(turned, 1, 0))


def down(a, h, upper):
    if h >= 2:
        return roll(a, -(h // 2), 0)
    turned = roll(a, 64, 1)
    return jnp.where(upper, roll(turned, -1, 0), turned)


def both(f, a, h, upper):
    return f(a[0], h, upper), f(a[1], h, upper)


def layer(ref, quantity, r):
    return ref[pl.ds(quantity * 8 + r, SLABS, stride=ROWS), :]


def source_layer(ref, r):
    return layer(ref, 0, r), layer(ref, 1, r)


def overlap_layer(ref, r):
    _, _, y = lane_ids()
    pair = ref[pl.ds(24 + r, SLABS, stride=ROWS), :]
    single = ref[pl.ds(32 + r % 4, SLABS, stride=ROWS), :]
    quantities = []
    for packed, base in ((pair, 0), (pair, 4), (single, 4 * (r // 4))):
        quantities.append(jnp.where(y >= 4, roll(packed, -10 - base, 1), roll(packed, 6 - base, 1)))
    used = (y <= 1) | (y >= 6)
    return quantities[0], quantities[1], jnp.where(used, quantities[2], 1.0)


def inside():
    chunk = lax.axis_index("slab")
    _, _, y = lane_ids()
    below = (y >= 6) & jnp.broadcast_to(chunk > 0, y.shape)
    above = (y <= 1) & jnp.broadcast_to(chunk < SLABS - 1, y.shape)
    return below | above


def put(ref, i, a):
    ref[pl.ds(2 * i * SLABS, SLABS), :] = a[0]
    ref[pl.ds((2 * i + 1) * SLABS, SLABS), :] = a[1]


def get(ref, i):
    return ref[pl.ds(2 * i * SLABS, SLABS), :], ref[pl.ds((2 * i + 1) * SLABS, SLABS), :]


N_FACTORS = 7 + 2 * STEPS + 1


def factorize(relatives, factors, overlap=False):
    upper = upper_half(overlap)
    row = lax.broadcasted_iota(jnp.int32, (SLABS, LANES), 0)
    first = row * 16 + jnp.where(upper, 8, 0)
    pivots = []
    diagonal = None
    for r in range(DEPTH):
        z = first + r
        relative = relatives[r]
        inward = jnp.maximum(jnp.maximum(PML - z, z - (NZ - 1 - PML)), 0)
        fraction = inward.astype(F32) / PML
        diagonal = (
            (2.0 + 4.0 * COUPLE) - WAVE_SHIFT * relative,
            (DAMPING * WAVE_SHIFT) * relative + ABSORB * fraction * fraction,
        )
        if r < DEPTH - 1:
            pivots.append(crecip(diagonal if r == 0 else csub(diagonal, pivots[-1])))
            put(factors, r, pivots[-1])
    to_first = pivots[0]
    first_first = pivots[0]
    for r in range(1, DEPTH - 1):
        reached = cmul(to_first, to_first)
        to_first = cmul(to_first, pivots[r])
        first_first = cadd(first_first, cmul(reached, pivots[r]))
    corner = to_first
    last_last = pivots[-1]
    low = (row == 0) & jnp.logical_not(upper)
    left = tuple(jnp.where(low, 0.0, v) for v in corner)
    high = (row == SLABS - 1) & upper
    next_first = tuple(jnp.where(high, 0.0, v) for v in both(down, first_first, 1, upper))
    d = csub(csub(diagonal, last_last), next_first)
    for step in range(STEPS):
        h = 1 << step
        right = both(down, left, h, upper)
        inverse = crecip(d)
        alpha = cmul(left, both(up, inverse, h, upper))
        gamma = cmul(right, both(down, inverse, h, upper))
        put(factors, 7 + 2 * step, alpha)
        put(factors, 8 + 2 * step, gamma)
        d = csub(csub(d, cmul(alpha, left)), cmul(gamma, right))
        left = cmul(alpha, both(up, left, h, upper))
    put(factors, 7 + 2 * STEPS, crecip(d))


def line_solve(rhs, factors, overlap=False):
    pivots = [get(factors, r) for r in range(DEPTH - 1)]
    gone = [rhs[0]]
    for r in range(1, DEPTH - 1):
        gone.append(cadd(rhs[r], cmul(pivots[r - 1], gone[-1])))
    last = cmul(pivots[-1], gone[-1])
    reach = pivots[0]
    reaches = []
    first = cmul(pivots[0], gone[0])
    for r in range(1, DEPTH - 1):
        reaches.append(reach)
        reach = cmul(reach, pivots[r])
        first = cadd(first, cmul(reach, gone[r]))
    upper = upper_half(overlap)
    row = lax.broadcasted_iota(jnp.int32, (SLABS, LANES), 0)
    high = (row == SLABS - 1) & upper
    low = (row == 0) & jnp.logical_not(upper)
    after = tuple(jnp.where(high, 0.0, v) for v in both(down, first, 1, upper))
    g = cadd(cadd(rhs[DEPTH - 1], last), after)
    for step in range(STEPS):
        h = 1 << step
        from_low = cmul(get(factors, 7 + 2 * step), both(up, g, h, upper))
        from_high = cmul(get(factors, 8 + 2 * step), both(down, g, h, upper))
        g = cadd(g, cadd(from_low, from_high))
    separator = cmul(get(factors, 7 + 2 * STEPS), g)
    before = tuple(jnp.where(low, 0.0, v) for v in both(up, separator, 1, upper))
    field = [None] * DEPTH
    field[DEPTH - 1] = separator
    for r in range(DEPTH - 2, -1, -1):
        lit = cadd(gone[r], before if r == 0 else cmul(reaches[r - 1], before))
        field[r] = cmul(pivots[r], cadd(lit, field[r + 1]))
    return field


def cell_lanes(r, low_line):
    _, x, y = lane_ids()
    at = r if low_line else 7 + r
    return ((x == (at - 1) % 8) & (y == 7)) | ((x == (at + 1) % 8) & (y == 0))


def put_edges(main, over, source, relatives, edges):
    _, x, _ = lane_ids()

    def pack(layers, low_line, high_line):
        low = high = layers[0]
        for r in range(1, DEPTH):
            moved = roll(layers[r], 8 * r, 1)
            low = jnp.where(x == (low_line + r) % 8, moved, low)
            high = jnp.where(x == (high_line + r) % 8, moved, high)
        return low, high

    def pack_cells(layers):
        low = high = jnp.zeros((SLABS, LANES), F32)
        for r in range(DEPTH):
            moved = roll(layers[r], 8 * r, 1)
            low = jnp.where(cell_lanes(r, True), moved, low)
            high = jnp.where(cell_lanes(r, False), moved, high)
        return low, high

    _, _, y = lane_ids()
    beside_lines = (y == 0) | (y == 7)
    packed = [None] * 6
    for c in range(2):
        near = pack([f[c] for f in main], 0, 7)
        far = pack([f[c] for f in main], 1, 6)
        far = roll(far[0], -8, 1), roll(far[1], 8, 1)
        own = pack([f[c] for f in source], 0, 7)
        cells = pack_cells([f[c] for f in over])
        packed[c] = near
        packed[2 + c] = [own[i] + COUPLE * (far[i] + sum_y(near[i], cells[i])) for i in range(2)]
        if c == 0:
            packed[5] = cells
        else:
            packed[5] = [jnp.where(beside_lines, re, roll(im, 2, 1)) for re, im in zip(packed[5], cells)]
    packed[4] = pack(relatives, 0, 7)
    for place, pair in enumerate(packed):
        for edge, array, turned in zip(edges, pair, (56, -56)):
            edge[pl.ds(place * SLABS, SLABS), :] = roll(array, turned, 1)


def within():
    tile = lax.axis_index("tile")
    _, x, _ = lane_ids()
    low = (x < 4) & jnp.broadcast_to(tile > 0, x.shape)
    high = (x >= 4) & jnp.broadcast_to(tile < TILES - 1, x.shape)
    return low | high


def beside(halos, place, r):
    _, x, _ = lane_ids()
    low, high = (ref[pl.ds(place * SLABS, SLABS), :] for ref in halos)
    return roll(jnp.where(x == r, low, high), -8 * r, 1)


def over_beside(low, high, c, r):
    _, x, y = lane_ids()
    if c == 0:
        from_low = cell_lanes(r, True)
    else:
        from_low = ((x == r) & (y == 1)) | ((x == (r + 1) % 8) & (y == 2))
    return roll(jnp.where(from_low, low, high), -8 * r - 2 * c, 1)


def sum_y(field, over):
    _, _, y = lane_ids()
    return roll(jnp.where(y == 7, over, field), 1, 1) + roll(jnp.where(y == 0, over, field), -1, 1)


def sum_main(main, over, near):
    _, x, _ = lane_ids()
    along_x = jnp.where(x == 0, near, roll(main, 8, 1)) + jnp.where(x == 7, near, roll(main, -8, 1))
    return along_x + sum_y(main, over)


def over_edge():
    _, x, y = lane_ids()
    below = y >= 4
    return x == jnp.where(below, 7, 1), x == jnp.where(below, 6, 0)


def sum_over(main, over):
    at_low, at_high = over_edge()
    along_x = jnp.where(at_low, 0.0, roll(over, 8, 1)) + jnp.where(at_high, 0.0, roll(over, -8, 1))
    return along_x + sum_y(over, main)


def relax(source, spread):
    return tuple(s + COUPLE * t for s, t in zip(source, spread))


def masked(field, keep):
    return [tuple(jnp.where(keep, v, 0.0) for v in f) for f in field]


def put_all(ref, field):
    for r in range(DEPTH):
        put(ref, r, field[r])


def get_all(ref):
    return [get(ref, r) for r in range(DEPTH)]


def first_kernel(arrived, factors, over_factors, main_out, over_out, *edges):
    overlap = [overlap_layer(arrived, r) for r in range(DEPTH)]
    factorize([o[2] for o in overlap], over_factors, True)
    over = masked(line_solve([o[:2] for o in overlap], over_factors, True), inside())
    put_all(over_out, over)
    relatives = [layer(arrived, 2, r) for r in range(DEPTH)]
    source = [source_layer(arrived, r) for r in range(DEPTH)]
    factorize(relatives, factors)
    main = line_solve(source, factors)
    put_all(main_out, main)
    put_edges(main, over, source, relatives, edges)


def own_kernel(arrived, main_in, over_in, main_part, over_part):
    for r in range(DEPTH):
        main, over = get(main_in, r), get(over_in, r)
        put(main_part, r, relax(source_layer(arrived, r), [sum_main(m, e, 0.0) for m, e in zip(main, over)]))
        put(over_part, r, relax(overlap_layer(arrived, r)[:2], [sum_over(m, e) for m, e in zip(main, over)]))


def last_kernel(
    arrived, factors, over_factors, main_in, main_part, over_part, low, high,
    out, near_factors, main_mid, over_mid, near_mid,
):
    halos = (low, high)
    keep = within()
    _, x, _ = lane_ids()
    outermost = (x == 0) | (x == 7)
    at_low, at_high = over_edge()
    over_outermost = at_low | at_high
    tile = lax.axis_index("tile")
    exists = [jnp.broadcast_to(k, x.shape) for k in (tile > 0, tile < TILES - 1)]
    cells = [jnp.where(k, h[pl.ds(5 * SLABS, SLABS), :], 0.0) for h, k in zip(halos, exists)]
    factorize([beside(halos, 4, r) for r in range(DEPTH)], near_factors)
    main_rhs, over_rhs, near_rhs = [], [], []
    for r in range(DEPTH):
        main_adds, over_adds = [], []
        for c in range(2):
            near = jnp.where(keep, beside(halos, c, r), 0.0)
            main_adds.append(jnp.where(outermost, near, 0.0))
            over_adds.append(jnp.where(over_outermost, over_beside(*cells, c, r), 0.0))
        main_rhs.append(relax(get(main_part, r), main_adds))
        over_rhs.append(relax(get(over_part, r), over_adds))
        near_rhs.append(relax((beside(halos, 2, r), beside(halos, 3, r)), get(main_in, r)))
    put_all(main_mid, line_solve(main_rhs, factors))
    put_all(over_mid, masked(line_solve(over_rhs, over_factors, True), inside()))
    put_all(near_mid, masked(line_solve(near_rhs, near_factors), keep))
    rhs = []
    for r in range(DEPTH):
        parts = zip(get(main_mid, r), get(over_mid, r), get(near_mid, r))
        rhs.append(relax(source_layer(arrived, r), [sum_main(*part) for part in parts]))
    field = line_solve(rhs, factors)
    for r in range(DEPTH):
        for c in range(2):
            out[pl.ds(c * 8 + r, SLABS, stride=16), :] = field[r][c]


def call(kernel, name, outs, *args, scratch=(), spec=VMEM, out_spec=VMEM):
    return pl.pallas_call(
        kernel,
        out_shape=[jax.ShapeDtypeStruct(s, F32) for s in outs],
        in_specs=[spec] * len(args),
        out_specs=[out_spec] * len(outs),
        scratch_shapes=list(scratch),
        compiler_params=pltpu.CompilerParams(vmem_limit_bytes=32 << 20),
        cost_estimate=pl.CostEstimate(flops=2_000_000, bytes_accessed=1_000_000, transcendentals=0),
        name=name,
    )(*args)


FIELD = (DEPTH * 2 * SLABS, LANES)
FACTORS = (N_FACTORS * 2 * SLABS, LANES)
EDGE = (6 * SLABS, LANES)

RING_UP = [(i, (i + 1) % TILES) for i in range(TILES)]
RING_DOWN = [(b, a) for a, b in RING_UP]


def exchange(low, high):
    return lax.ppermute(high, "tile", RING_UP), lax.ppermute(low, "tile", RING_DOWN)


def local(source, labels, permittivity):
    rows = source.reshape(2 * 16 * 8, 256)
    marks = labels.reshape(16 * 8, 256)
    inputs = [pltpu.with_memory_space_constraint(v, pltpu.HBM) for v in (permittivity, rows, marks)]
    (packed,) = call(
        pack_kernel, "pack", [(SLABS * ROWS, LANES)], *inputs, spec=HBM,
        scratch=[
            pltpu.VMEM((2, 3 * LANES, LANES), F32),
            pltpu.VMEM((2, LANES, LANES), jnp.int32),
            pltpu.SMEM((8,), F32),
            pltpu.SemaphoreType.DMA((7,)),
        ],
    )
    arrived = lax.all_to_all(packed.reshape(SLABS, ROWS // 4, 4, LANES), "slab", 0, 0).reshape(SLABS * ROWS, LANES)
    factors, over_factors, main, over, *edges = call(
        first_kernel, "first", [FACTORS, FACTORS, FIELD, FIELD, EDGE, EDGE], arrived
    )
    halos = exchange(*edges)
    main_part, over_part = call(own_kernel, "own", [FIELD, FIELD], arrived, main, over)
    (packed,) = call(
        last_kernel, "last", [(SLABS * 16, LANES)],
        arrived, factors, over_factors, main, main_part, over_part, *halos,
        scratch=[pltpu.VMEM(FACTORS, F32)] + [pltpu.VMEM(FIELD, F32)] * 3,
    )
    arrived = lax.all_to_all(packed.reshape(SLABS, 16, LANES), "slab", 0, 0).reshape(SLABS * 16, LANES)
    (out,) = call(
        unpack_kernel, "unpack", [(2 * 16 * 8, 256)], arrived, out_spec=HBM,
        scratch=[pltpu.VMEM((2, 2 * LANES, LANES), F32), pltpu.SemaphoreType.DMA((2,))],
    )
    return out.reshape(2, 16, 8, 256)


def solution(mesh):
    placed = (P("tilt", "slab", "tile", None), P("slab", "tile", "tilt"), P("tilt"))
    return jax.shard_map(
        local,
        mesh=mesh,
        in_specs=placed,
        out_specs=P("tilt", "slab", "tile", None),
        check_vma=False,
    )
```

```python
import jax
import jax.numpy as jnp
from jax import lax
from jax.experimental import pallas as pl
from jax.experimental.pallas import tpu as pltpu
from jax.sharding import PartitionSpec as P

PML = 8
COUPLE = 0.02
WAVE_SHIFT = 0.15
DAMPING = 0.15
ABSORB = 0.5
NZ = 512
SLABS = 32
TILES = 8
LANES = 128
DEPTH = 8
STEPS = 6
F32 = jnp.float32
VMEM = pl.BlockSpec(memory_space=pltpu.VMEM)
HBM = pl.BlockSpec(memory_space=pltpu.HBM)


ROWS = 36


def roll(x, shift, axis):
    shift %= x.shape[axis]
    return x if shift == 0 else pltpu.roll(x, shift, axis)


def cmul(a, b):
    return a[0] * b[0] - a[1] * b[1], a[0] * b[1] + a[1] * b[0]


def cadd(a, b):
    return a[0] + b[0], a[1] + b[1]


def csub(a, b):
    return a[0] - b[0], a[1] - b[1]


def crecip(a):
    square = a[0] * a[0] + a[1] * a[1]
    scale = pl.reciprocal(square, approx=True)
    scale = scale * (2.0 - square * scale)
    return a[0] * scale, -a[1] * scale


def lanes8():
    return lax.broadcasted_iota(jnp.int32, (8, LANES), 1)


def lanes8():
    return lax.broadcasted_iota(jnp.int32, (8, LANES), 1)


def block_transpose(turned):
    block = lanes8() // 8
    for bit in (1, 2, 4, 8):
        odd = (block & bit) != 0
        turned = [jnp.where(odd, turned[(j + bit) % 16], turned[j]) for j in range(16)]
    return [roll(turned[-c % 16], -8 * c, 1) for c in range(16)]


def turn(arrays, shift=0):
    return [roll(array, shift + 8 * i, 1) for i, array in enumerate(arrays)]


def pack_kernel(table_hbm, source, labels, out, sides, marks, table, sems):
    copies = [pltpu.make_async_copy(table_hbm, table, sems.at[0])]
    for side in range(2):
        lanes = pl.ds(side * LANES, LANES)
        copies.append(pltpu.make_async_copy(labels.at[:, lanes], marks.at[side], sems.at[1 + side]))
    for quantity in range(2):
        rows = pl.ds(quantity * LANES, LANES)
        for side in range(2):
            lanes = pl.ds(side * LANES, LANES)
            sem = sems.at[3 + 2 * quantity + side]
            copies.append(pltpu.make_async_copy(source.at[rows, lanes], sides.at[side, rows], sem))
    for copy in copies:
        copy.start()
    for copy in copies[:3]:
        copy.wait()
    for side in range(2):
        lab = marks[side]
        rel = jnp.full(lab.shape, table[0], F32)
        for m in range(1, 8):
            rel = jnp.where(lab == m, table[m], rel)
        sides[side, pl.ds(2 * LANES, LANES), :] = rel

    def load(side, quantity):
        places = [quantity * LANES + half * 64 + x for half in range(2) for x in range(8)]
        return [sides[side, pl.ds(place, 8, stride=8), :] for place in places]

    slot = lanes8() % 8
    first = slot < 4
    chunks = [None] * 3
    for quantity in (2, 0, 1):
        if quantity < 2:
            for copy in copies[3 + 2 * quantity : 5 + 2 * quantity]:
                copy.wait()
        blocks = block_transpose(turn(load(0, quantity))) + block_transpose(turn(load(1, quantity)))
        chunks[quantity] = blocks
        for chunk, block in enumerate(blocks):
            out[pl.ds(chunk * ROWS + quantity * 8, 8), :] = block
    for chunk in range(SLABS):
        picked = [jnp.where(first, blocks[(chunk + 1) % SLABS], blocks[chunk - 1]) for blocks in chunks]
        pair = jnp.where(first, roll(picked[0], 2, 1), roll(picked[1], 6, 1))
        single = jnp.where(first, roll(picked[2], 2, 1), roll(roll(picked[2], 6, 1), 4, 0))
        out[pl.ds(chunk * ROWS + 24, 8), :] = pair
        out[pl.ds(chunk * ROWS + 32, 4), :] = single[:4]


def unpack_kernel(arrived, out, sides, sems):
    copies = []
    for side in range(2):
        for c in range(2):
            parts = [arrived[pl.ds((16 * side + b) * 16 + c * 8, 8), :] for b in range(16)]
            for i, part in enumerate(block_transpose(turn(parts))):
                half, x = divmod(i, 8)
                sides[side, pl.ds(c * LANES + half * 64 + x, 8, stride=8), :] = part
            rows, lanes = pl.ds(c * LANES, LANES), pl.ds(side * LANES, LANES)
            copies.append(pltpu.make_async_copy(sides.at[side, rows], out.at[rows, lanes], sems.at[2 * side + c]))
            copies[-1].start()
    for copy in copies:
        copy.wait()


def lane_ids():
    lane = lax.broadcasted_iota(jnp.int32, (SLABS, LANES), 1)
    return lane >= 64, (lane // 8) % 8, lane % 8


def upper_half(overlap):
    lane = lax.broadcasted_iota(jnp.int32, (SLABS, LANES), 1)
    if overlap:
        lane = (lane + jnp.where(lane % 8 >= 4, 8, LANES - 8)) % LANES
    return lane >= 64


def up(a, h, upper):
    if h >= 2:
        return roll(a, h // 2, 0)
    turned = roll(a, 64, 1)
    return jnp.where(upper, turned, roll(turned, 1, 0))


def down(a, h, upper):
    if h >= 2:
        return roll(a, -(h // 2), 0)
    turned = roll(a, 64, 1)
    return jnp.where(upper, roll(turned, -1, 0), turned)


def both(f, a, h, upper):
    return f(a[0], h, upper), f(a[1], h, upper)


def layer(ref, quantity, r):
    return ref[pl.ds(quantity * 8 + r, SLABS, stride=ROWS), :]


def source_layer(ref, r):
    return layer(ref, 0, r), layer(ref, 1, r)


def overlap_layer(ref, r):
    _, _, y = lane_ids()
    pair = ref[pl.ds(24 + r, SLABS, stride=ROWS), :]
    single = ref[pl.ds(32 + r % 4, SLABS, stride=ROWS), :]
    quantities = []
    for packed, base in ((pair, 0), (pair, 4), (single, 4 * (r // 4))):
        quantities.append(jnp.where(y >= 4, roll(packed, -10 - base, 1), roll(packed, 6 - base, 1)))
    used = (y <= 1) | (y >= 6)
    return quantities[0], quantities[1], jnp.where(used, quantities[2], 1.0)


def inside():
    chunk = lax.axis_index("slab")
    _, _, y = lane_ids()
    below = (y >= 6) & jnp.broadcast_to(chunk > 0, y.shape)
    above = (y <= 1) & jnp.broadcast_to(chunk < SLABS - 1, y.shape)
    return below | above


def put(ref, i, a):
    ref[pl.ds(2 * i * SLABS, SLABS), :] = a[0]
    ref[pl.ds((2 * i + 1) * SLABS, SLABS), :] = a[1]


def get(ref, i):
    return ref[pl.ds(2 * i * SLABS, SLABS), :], ref[pl.ds((2 * i + 1) * SLABS, SLABS), :]


N_FACTORS = 7 + 2 * STEPS + 1


def factorize(relatives, factors, overlap=False):
    upper = upper_half(overlap)
    row = lax.broadcasted_iota(jnp.int32, (SLABS, LANES), 0)
    first = row * 16 + jnp.where(upper, 8, 0)
    pivots = []
    diagonal = None
    for r in range(DEPTH):
        z = first + r
        relative = relatives[r]
        inward = jnp.maximum(jnp.maximum(PML - z, z - (NZ - 1 - PML)), 0)
        fraction = inward.astype(F32) / PML
        diagonal = (
            (2.0 + 4.0 * COUPLE) - WAVE_SHIFT * relative,
            (DAMPING * WAVE_SHIFT) * relative + ABSORB * fraction * fraction,
        )
        if r < DEPTH - 1:
            pivots.append(crecip(diagonal if r == 0 else csub(diagonal, pivots[-1])))
            put(factors, r, pivots[-1])
    to_first = pivots[0]
    first_first = pivots[0]
    for r in range(1, DEPTH - 1):
        reached = cmul(to_first, to_first)
        to_first = cmul(to_first, pivots[r])
        first_first = cadd(first_first, cmul(reached, pivots[r]))
    corner = to_first
    last_last = pivots[-1]
    low = (row == 0) & jnp.logical_not(upper)
    left = tuple(jnp.where(low, 0.0, v) for v in corner)
    high = (row == SLABS - 1) & upper
    next_first = tuple(jnp.where(high, 0.0, v) for v in both(down, first_first, 1, upper))
    d = csub(csub(diagonal, last_last), next_first)
    for step in range(STEPS):
        h = 1 << step
        right = both(down, left, h, upper)
        inverse = crecip(d)
        alpha = cmul(left, both(up, inverse, h, upper))
        gamma = cmul(right, both(down, inverse, h, upper))
        put(factors, 7 + 2 * step, alpha)
        put(factors, 8 + 2 * step, gamma)
        d = csub(csub(d, cmul(alpha, left)), cmul(gamma, right))
        left = cmul(alpha, both(up, left, h, upper))
    put(factors, 7 + 2 * STEPS, crecip(d))


def line_solve(rhs, factors, overlap=False):
    pivots = [get(factors, r) for r in range(DEPTH - 1)]
    gone = [rhs[0]]
    for r in range(1, DEPTH - 1):
        gone.append(cadd(rhs[r], cmul(pivots[r - 1], gone[-1])))
    last = cmul(pivots[-1], gone[-1])
    reach = pivots[0]
    reaches = []
    first = cmul(pivots[0], gone[0])
    for r in range(1, DEPTH - 1):
        reaches.append(reach)
        reach = cmul(reach, pivots[r])
        first = cadd(first, cmul(reach, gone[r]))
    upper = upper_half(overlap)
    row = lax.broadcasted_iota(jnp.int32, (SLABS, LANES), 0)
    high = (row == SLABS - 1) & upper
    low = (row == 0) & jnp.logical_not(upper)
    after = tuple(jnp.where(high, 0.0, v) for v in both(down, first, 1, upper))
    g = cadd(cadd(rhs[DEPTH - 1], last), after)
    for step in range(STEPS):
        h = 1 << step
        from_low = cmul(get(factors, 7 + 2 * step), both(up, g, h, upper))
        from_high = cmul(get(factors, 8 + 2 * step), both(down, g, h, upper))
        g = cadd(g, cadd(from_low, from_high))
    separator = cmul(get(factors, 7 + 2 * STEPS), g)
    before = tuple(jnp.where(low, 0.0, v) for v in both(up, separator, 1, upper))
    field = [None] * DEPTH
    field[DEPTH - 1] = separator
    for r in range(DEPTH - 2, -1, -1):
        lit = cadd(gone[r], before if r == 0 else cmul(reaches[r - 1], before))
        field[r] = cmul(pivots[r], cadd(lit, field[r + 1]))
    return field


def cell_lanes(r, low_line):
    _, x, y = lane_ids()
    at = r if low_line else 7 + r
    return ((x == (at - 1) % 8) & (y == 7)) | ((x == (at + 1) % 8) & (y == 0))


def put_edges(main, over, source, relatives, edges):
    _, x, _ = lane_ids()

    def pack(layers, low_line, high_line):
        low = high = layers[0]
        for r in range(1, DEPTH):
            moved = roll(layers[r], 8 * r, 1)
            low = jnp.where(x == (low_line + r) % 8, moved, low)
            high = jnp.where(x == (high_line + r) % 8, moved, high)
        return low, high

    def pack_cells(layers):
        low = high = jnp.zeros((SLABS, LANES), F32)
        for r in range(DEPTH):
            moved = roll(layers[r], 8 * r, 1)
            low = jnp.where(cell_lanes(r, True), moved, low)
            high = jnp.where(cell_lanes(r, False), moved, high)
        return low, high

    _, _, y = lane_ids()
    beside_lines = (y == 0) | (y == 7)
    packed = [None] * 6
    for c in range(2):
        near = pack([f[c] for f in main], 0, 7)
        far = pack([f[c] for f in main], 1, 6)
        far = roll(far[0], -8, 1), roll(far[1], 8, 1)
        own = pack([f[c] for f in source], 0, 7)
        cells = pack_cells([f[c] for f in over])
        packed[c] = near
        packed[2 + c] = [own[i] + COUPLE * (far[i] + sum_y(near[i], cells[i])) for i in range(2)]
        if c == 0:
            packed[5] = cells
        else:
            packed[5] = [jnp.where(beside_lines, re, roll(im, 2, 1)) for re, im in zip(packed[5], cells)]
    packed[4] = pack(relatives, 0, 7)
    for place, pair in enumerate(packed):
        for edge, array, turned in zip(edges, pair, (56, -56)):
            edge[pl.ds(place * SLABS, SLABS), :] = roll(array, turned, 1)


def within():
    tile = lax.axis_index("tile")
    _, x, _ = lane_ids()
    low = (x < 4) & jnp.broadcast_to(tile > 0, x.shape)
    high = (x >= 4) & jnp.broadcast_to(tile < TILES - 1, x.shape)
    return low | high


def beside(halos, place, r):
    _, x, _ = lane_ids()
    low, high = (ref[pl.ds(place * SLABS, SLABS), :] for ref in halos)
    return roll(jnp.where(x == r, low, high), -8 * r, 1)


def over_beside(low, high, c, r):
    _, x, y = lane_ids()
    if c == 0:
        from_low = cell_lanes(r, True)
    else:
        from_low = ((x == r) & (y == 1)) | ((x == (r + 1) % 8) & (y == 2))
    return roll(jnp.where(from_low, low, high), -8 * r - 2 * c, 1)


def sum_y(field, over):
    _, _, y = lane_ids()
    return roll(jnp.where(y == 7, over, field), 1, 1) + roll(jnp.where(y == 0, over, field), -1, 1)


def sum_main(main, over, near):
    _, x, _ = lane_ids()
    along_x = jnp.where(x == 0, near, roll(main, 8, 1)) + jnp.where(x == 7, near, roll(main, -8, 1))
    return along_x + sum_y(main, over)


def over_edge():
    _, x, y = lane_ids()
    below = y >= 4
    return x == jnp.where(below, 7, 1), x == jnp.where(below, 6, 0)


def sum_over(main, over):
    at_low, at_high = over_edge()
    along_x = jnp.where(at_low, 0.0, roll(over, 8, 1)) + jnp.where(at_high, 0.0, roll(over, -8, 1))
    return along_x + sum_y(over, main)


def relax(source, spread):
    return tuple(s + COUPLE * t for s, t in zip(source, spread))


def masked(field, keep):
    return [tuple(jnp.where(keep, v, 0.0) for v in f) for f in field]


def put_all(ref, field):
    for r in range(DEPTH):
        put(ref, r, field[r])


def get_all(ref):
    return [get(ref, r) for r in range(DEPTH)]


def first_kernel(arrived, factors, over_factors, main_out, over_out, *edges):
    overlap = [overlap_layer(arrived, r) for r in range(DEPTH)]
    factorize([o[2] for o in overlap], over_factors, True)
    over = masked(line_solve([o[:2] for o in overlap], over_factors, True), inside())
    put_all(over_out, over)
    relatives = [layer(arrived, 2, r) for r in range(DEPTH)]
    source = [source_layer(arrived, r) for r in range(DEPTH)]
    factorize(relatives, factors)
    main = line_solve(source, factors)
    put_all(main_out, main)
    put_edges(main, over, source, relatives, edges)


def own_kernel(arrived, main_in, over_in, main_part, over_part):
    for r in range(DEPTH):
        main, over = get(main_in, r), get(over_in, r)
        put(main_part, r, relax(source_layer(arrived, r), [sum_main(m, e, 0.0) for m, e in zip(main, over)]))
        put(over_part, r, relax(overlap_layer(arrived, r)[:2], [sum_over(m, e) for m, e in zip(main, over)]))


def last_kernel(
    arrived, factors, over_factors, main_in, main_part, over_part, low, high,
    out, near_factors, main_mid, over_mid, near_mid,
):
    halos = (low, high)
    keep = within()
    _, x, _ = lane_ids()
    outermost = (x == 0) | (x == 7)
    at_low, at_high = over_edge()
    over_outermost = at_low | at_high
    tile = lax.axis_index("tile")
    exists = [jnp.broadcast_to(k, x.shape) for k in (tile > 0, tile < TILES - 1)]
    cells = [jnp.where(k, h[pl.ds(5 * SLABS, SLABS), :], 0.0) for h, k in zip(halos, exists)]
    factorize([beside(halos, 4, r) for r in range(DEPTH)], near_factors)
    main_rhs, over_rhs, near_rhs = [], [], []
    for r in range(DEPTH):
        main_adds, over_adds = [], []
        for c in range(2):
            near = jnp.where(keep, beside(halos, c, r), 0.0)
            main_adds.append(jnp.where(outermost, near, 0.0))
            over_adds.append(jnp.where(over_outermost, over_beside(*cells, c, r), 0.0))
        main_rhs.append(relax(get(main_part, r), main_adds))
        over_rhs.append(relax(get(over_part, r), over_adds))
        near_rhs.append(relax((beside(halos, 2, r), beside(halos, 3, r)), get(main_in, r)))
    put_all(main_mid, line_solve(main_rhs, factors))
    put_all(over_mid, masked(line_solve(over_rhs, over_factors, True), inside()))
    put_all(near_mid, masked(line_solve(near_rhs, near_factors), keep))
    rhs = []
    for r in range(DEPTH):
        parts = zip(get(main_mid, r), get(over_mid, r), get(near_mid, r))
        rhs.append(relax(source_layer(arrived, r), [sum_main(*part) for part in parts]))
    field = line_solve(rhs, factors)
    for r in range(DEPTH):
        for c in range(2):
            out[pl.ds(c * 8 + r, SLABS, stride=16), :] = field[r][c]


def call(kernel, name, outs, *args, scratch=(), spec=VMEM, out_spec=VMEM):
    return pl.pallas_call(
        kernel,
        out_shape=[jax.ShapeDtypeStruct(s, F32) for s in outs],
        in_specs=[spec] * len(args),
        out_specs=[out_spec] * len(outs),
        scratch_shapes=list(scratch),
        compiler_params=pltpu.CompilerParams(vmem_limit_bytes=32 << 20),
        cost_estimate=pl.CostEstimate(flops=2_000_000, bytes_accessed=1_000_000, transcendentals=0),
        name=name,
    )(*args)


FIELD = (DEPTH * 2 * SLABS, LANES)
FACTORS = (N_FACTORS * 2 * SLABS, LANES)
EDGE = (6 * SLABS, LANES)

RING_UP = [(i, (i + 1) % TILES) for i in range(TILES)]
RING_DOWN = [(b, a) for a, b in RING_UP]


def exchange(low, high):
    return lax.ppermute(high, "tile", RING_UP), lax.ppermute(low, "tile", RING_DOWN)


def local(source, labels, permittivity):
    rows = source.reshape(2 * 16 * 8, 256)
    marks = labels.reshape(16 * 8, 256)
    inputs = [pltpu.with_memory_space_constraint(v, pltpu.HBM) for v in (permittivity, rows, marks)]
    (packed,) = call(
        pack_kernel, "pack", [(SLABS * ROWS, LANES)], *inputs, spec=HBM,
        scratch=[
            pltpu.VMEM((2, 3 * LANES, LANES), F32),
            pltpu.VMEM((2, LANES, LANES), jnp.int32),
            pltpu.SMEM((8,), F32),
            pltpu.SemaphoreType.DMA((7,)),
        ],
    )
    arrived = lax.all_to_all(packed.reshape(SLABS, ROWS // 4, 4, LANES), "slab", 0, 0).reshape(SLABS * ROWS, LANES)
    factors, over_factors, main, over, *edges = call(
        first_kernel, "first", [FACTORS, FACTORS, FIELD, FIELD, EDGE, EDGE], arrived
    )
    halos = exchange(*edges)
    main_part, over_part = call(own_kernel, "own", [FIELD, FIELD], arrived, main, over)
    (packed,) = call(
        last_kernel, "last", [(SLABS * 16, LANES)],
        arrived, factors, over_factors, main, main_part, over_part, *halos,
        scratch=[pltpu.VMEM(FACTORS, F32)] + [pltpu.VMEM(FIELD, F32)] * 3,
    )
    arrived = lax.all_to_all(packed.reshape(SLABS, 16, LANES), "slab", 0, 0).reshape(SLABS * 16, LANES)
    (out,) = call(
        unpack_kernel, "unpack", [(2 * 16 * 8, 256)], arrived, out_spec=HBM,
        scratch=[pltpu.VMEM((2, 2 * LANES, LANES), F32), pltpu.SemaphoreType.DMA((4,))],
    )
    return out.reshape(2, 16, 8, 256)


def solution(mesh):
    placed = (P("tilt", "slab", "tile", None), P("slab", "tile", "tilt"), P("tilt"))
    return jax.shard_map(
        local,
        mesh=mesh,
        in_specs=placed,
        out_specs=P("tilt", "slab", "tile", None),
        check_vma=False,
    )
```
